128 devices in a mesh: dom: 32 (over y, z, core), sub: 4 (over x).
Axes of the slice: x: 4, y: 4, z: 4, core: 2. Of those that a mesh axis runs over, the one named last changes fastest.
Arguments:
- displace: float32 [3, 262144, 128], P(None, ('dom', 'sub')), may hold values from -3 to 3
- velocity: float32 [3, 262144, 128], P(None, ('dom', 'sub')), may hold values from -3 to 3
- nodal_mass: float32 [262144, 128], P(('dom', 'sub')), may hold values from 1 to 4
- stiffness: float32 [262144, 128], P(('dom', 'sub')), may hold values from 0.5 to 2
- die_planes: float32 [3, 8192, 4, 128], P(None, ('dom', 'sub')), may hold values from -3 to 3
- owners: int32 [3, 16384, 1], P(None, ('dom', 'sub')), may hold values from 0 to 127; in each aligned block of 128 rows (0 to 127, 128 to 255, ..., all dimensions but the last counted through in order) at most 2 rows name the same one
- pairs: int32 [3, 16384], P(None, ('dom', 'sub')), may hold values from 0 to 63
Outputs:
- final_displace: float32 [3, 262144, 128], P(None, ('dom', 'sub'))
- final_velocity: float32 [3, 262144, 128], P(None, ('dom', 'sub'))
The draws below stay inside these ranges and needn't reach their ends.
Inputs may be any that keep to these rules, and one draw needn't show every extreme that they name: `owners`: in each step, no bin owner gets more than 2 of the segment blocks of one device, and some device sends exactly 2 to one owner.
All inputs are finite; a program needn't handle non-finite values.
Results may differ from the reference program's by a relative error of at most 0.0001.
Values sent between devices are 32-bit elements; how exact they have to be, the bound alone decides.
A program may use at most 128 MiB of HBM per device.

```python
import math
import jax
import jax.numpy as jnp
import numpy as np

NCOL = 128
RX = 2048
SEG_DEV = 128
DIE_DEV = 64
STEPS = 3
CAP = 2
NR = 262144
SEGS = 16384
DIES = 8192
N_DOM = 32
N_SUB = 4


def touch_ends(result, rng, least, largest):
    extent = result.shape
    spot = [jax.random.randint(jax.random.fold_in(rng, axis), (), 0, extent[axis]) for axis in range(len(extent))]
    result = result.at[tuple(spot)].set(least)
    longest = extent.index(max(extent))
    spot[longest] = (spot[longest] + 1) % extent[longest]
    return result.at[tuple(spot)].set(largest)


def level_of(key, dims, cuts, smallest, top_value):
    def one(axis_at, shards_of):
        heights = jax.random.uniform(jax.random.fold_in(jax.random.fold_in(key, 6), axis_at), (shards_of,), jnp.float32, smallest / len(cuts), top_value / len(cuts))
        return jnp.repeat(jnp.exp(heights), dims[axis_at] // shards_of).reshape((-1,) + (1,) * (len(dims) - axis_at - 1))

    level = one(*cuts[0])
    for cut in cuts[1:]:
        level = level * one(*cut)
    return level


def deal_out(own_key, own, number, rows, count, top, limit, slope):
    ranking = jax.random.permutation(own_key, count)
    packed, usual = portions_of(count, rows * top, limit, slope, True), portions_of(count, rows * top, limit, slope, False)
    places = jnp.arange(count)

    def named(tallies, offset_by):
        used = int((tallies > 0).sum())
        fixed = max(1, used // 4)
        moved = fixed + (places - fixed + offset_by * (used - fixed)) % max(1, count - fixed)
        return jnp.zeros((count,), jnp.int32).at[ranking[jnp.where(places < fixed, places, moved)]].set(jnp.asarray(tallies, jnp.int32))

    tallies = jnp.where(number % 4 == 0, named(packed, number // 4), named(usual, number - number // 4 - 1))
    mixed = jax.random.permutation(jax.random.fold_in(own, 3), count)
    source_of, taker = mixed[0:count // 2 * 2:2], mixed[1:count // 2 * 2:2]
    room = jnp.minimum(tallies[source_of] - 1, limit - tallies[taker]) // 2
    room = jnp.where((source_of == ranking[0]) | (taker == ranking[0]) | (tallies[taker] == 0), 0, jnp.maximum(room, 0))
    moved = jax.random.randint(jax.random.fold_in(own, 4), (count // 2,), 0, 1 << 20) % (room + 1)
    tallies = tallies.at[source_of].add(-moved).at[taker].add(moved)
    items = jnp.searchsorted(jnp.cumsum(tallies), jnp.arange(rows * top), side="right").astype(jnp.int32)
    table = items.reshape(top, rows).T
    table = table[jax.random.permutation(jax.random.fold_in(own, 1), rows)]
    offset_by = jax.random.randint(jax.random.fold_in(own, 2), (rows, 1), 0, top)
    return jnp.take_along_axis(table, (jnp.arange(top)[None, :] + offset_by) % top, axis=1)


def portions_of(number_of, total, limit, lean, full):
    portions = [(1 << 20) // math.isqrt(grade ** lean) + 1 for grade in range(1, number_of + 1)]
    largest = limit if full else min(limit, max(-(-total // number_of), total * portions[0] // sum(portions)))
    least = 1 if total - largest >= number_of - 1 else 0
    counts, spare = [largest] + [least] * (number_of - 1), total - largest - least * (number_of - 1)
    while spare > 0:
        free = [i for i in range(1, number_of) if counts[i] < largest] or [i for i in range(1, number_of) if counts[i] < limit]
        pool, budget = sum([portions[i] for i in free]), spare
        for i in free:
            more = min(limit - counts[i], max(1, budget * portions[i] // pool), spare)
            counts[i] = counts[i] + more
            spare = spare - more
    return np.array(counts)


def gaussian(own_key, dims, scale, most, pieces=(), kind=jnp.bfloat16):
    array = scale * jax.random.normal(own_key, dims, jnp.float32)
    if pieces:
        array = array * level_of(own_key, dims, pieces, -0.22, 0.18)
    return jnp.clip(array, -most, most).astype(kind)


def setup_inputs(seed: int = 0) -> dict:
    keys = jax.random.split(jax.random.key(seed), 8)
    displace = gaussian(keys[0], (3, NR, NCOL), 0.5, 3.0, ((1, 128),), jnp.float32)
    velocity = gaussian(keys[1], (3, NR, NCOL), 0.5, 3.0, ((1, 128),), jnp.float32)
    nodal_mass = jnp.clip(jnp.exp(math.log(4.0) - 1.3862944 * jax.random.uniform(keys[2], (NR, NCOL), jnp.float32) ** level_of(keys[2], (NR, NCOL), ((0, 128),), -0.2, 0.2)), 1.0, 4.0)
    stiffness = jnp.clip(jnp.exp(math.log(2.0) - 1.3862944 * jax.random.uniform(keys[3], (NR, NCOL), jnp.float32) ** level_of(keys[3], (NR, NCOL), ((0, 128),), -0.2, 0.2)), 0.5, 2.0)
    die_planes = gaussian(keys[4], (STEPS, DIES, 4, NCOL), 1.0, 3.0, ((1, 128),), jnp.float32)
    owners_keys = jax.random.split(jax.random.fold_in(keys[5], 1), STEPS * SEGS // SEG_DEV)
    owners_turns = jax.random.permutation(jax.random.fold_in(keys[5], 3), STEPS * SEGS // SEG_DEV)
    owners = jax.vmap(lambda own, number: deal_out(jax.random.fold_in(keys[5], 2), own, number, SEG_DEV, N_DOM * N_SUB, 1, CAP, 1))(owners_keys, owners_turns).reshape((STEPS, SEGS, 1))
    pairs = touch_ends(jax.random.randint(keys[6], (STEPS, SEGS), 0, DIE_DEV), jax.random.fold_in(keys[6], 1), 0, DIE_DEV - 1).astype(jnp.int32)
    return dict(displace=displace, velocity=velocity, nodal_mass=nodal_mass, stiffness=stiffness, die_planes=die_planes, owners=owners, pairs=pairs)


time_step = 0.2
penalty = 1.0


def shift_cols(values):
    return jnp.pad(values, ((0, 0), (0, 0), (1, 0)))[:, :, :-1]


def shift_rows(values):
    return jnp.pad(values, ((0, 0), (1, 0), (0, 0)))[:, :-1, :]


def internal_force(displace, stiffness):
    nrows = displace.shape[1]
    row_ids = jnp.arange(nrows, dtype=jnp.int32)[:, None]
    col_ids = jnp.arange(NCOL, dtype=jnp.int32)[None, :]
    valid = ((row_ids < nrows - 1) & (col_ids < NCOL - 1)).astype(jnp.float32)
    weight = (stiffness * valid)[None]
    padded = jnp.pad(displace, ((0, 0), (0, 1), (0, 1)))
    corner_aa = padded[:, :-1, :-1]
    corner_ab = padded[:, :-1, 1:]
    corner_ba = padded[:, 1:, :-1]
    corner_bb = padded[:, 1:, 1:]
    centre = (corner_aa + corner_ab + corner_ba + corner_bb) * 0.25
    force_aa = -weight * (corner_aa - centre)
    force_ab = -weight * (corner_ab - centre)
    force_ba = -weight * (corner_ba - centre)
    force_bb = -weight * (corner_bb - centre)
    return force_aa + shift_cols(force_ab) + shift_rows(force_ba + shift_cols(force_bb))


def reference(displace, velocity, nodal_mass, stiffness, die_planes, owners, pairs):
    stride = RX // SEG_DEV
    nrows = displace.shape[1]
    for step_index in range(STEPS):
        force = internal_force(displace, stiffness)
        blocks = displace.reshape(3, SEGS, stride, NCOL)[:, :, 0, :]
        patch_ids = owners[step_index, :, 0] * DIE_DEV + pairs[step_index]
        planes = jnp.take(die_planes[step_index], patch_ids, axis=0)
        normals = jnp.transpose(planes[:, 0:3, :], (1, 0, 2))
        depth = planes[:, 3, :] - jnp.sum(normals * blocks, axis=0)
        push = penalty * jnp.maximum(depth, 0.0)[None] * normals
        grouped = force.reshape(3, SEGS, stride, NCOL)
        grouped = jnp.concatenate([grouped[:, :, :1, :] + push[:, :, None, :], grouped[:, :, 1:, :]], axis=2)
        force = grouped.reshape(3, nrows, NCOL)
        velocity = velocity + time_step * force / nodal_mass[None]
        displace = displace + time_step * velocity
    return displace, velocity
```

```python
import functools

import jax
import jax.numpy as jnp
from jax import lax
from jax.experimental import pallas as pl
from jax.experimental.pallas import tpu as pltpu
from jax.sharding import PartitionSpec as P

STEPS = 3
time_step = 0.2
penalty = 1.0

MESH = pl.DeviceIdType.MESH
PAD = 16
HALO = 8


def next_col(x):
    return pltpu.roll(x, x.shape[-1] - 1, x.ndim - 1)


def prev_col(x):
    return pltpu.roll(x, 1, x.ndim - 1)


def contact(planes, position):
    normal, height = planes[:3], planes[3]
    depth = height - (normal[0] * position[0] + normal[1] * position[1] + normal[2] * position[2])
    push = penalty * jnp.maximum(depth, 0.0)
    return [push * normal[c] for c in range(3)]


def contact_response(planes, rows):
    cm = {o: rows("cm", o) for o in range(-2, 3)}
    kq = {o: rows("kq", o) for o in range(-2, 2)}
    w4 = {o: rows("w4", o) for o in range(-1, 2)}
    u = {}
    z = {}
    for step in range(STEPS):
        free = rows("d%d" % step, 0)
        position = [free[c] + u[0][c] if step else free[c] for c in range(3)]
        push = contact(planes[step], position)
        new_u, new_z = {}, {}
        for o in range(-step, step + 1):
            new_u[o], new_z[o] = [], []
        for c in range(3):
            spread = {}
            for o in range(-step, step):
                parts = [u[r][c] for r in (o, o + 1) if r in u]
                box = parts[0] if len(parts) == 1 else parts[0] + parts[1]
                t = kq[o] * (box + next_col(box))
                spread[o] = t + prev_col(t)
            for o in range(-step, step + 1):
                terms = [spread[r] for r in (o - 1, o) if r in spread]
                if o in u:
                    terms.append(-(w4[o] * u[o][c]))
                if o == 0:
                    terms.append(push[c])
                force = terms[0]
                for term in terms[1:]:
                    force = force + term
                dz = cm[o] * force
                zc = z[o][c] + dz if o in z else dz
                uc = time_step * zc
                if o in u:
                    uc = u[o][c] + uc
                new_z[o].append(zc)
                new_u[o].append(uc)
        u, z = new_u, new_z
    return u, z


def kernel(
    n_dom, n_sub, cap, near, block, last_block, width,
    own_hbm, pair_hbm, d_hbm, v_hbm, m_hbm, k_hbm, die_hbm,
    od_ref, ov_ref,
    own_ref, pair_ref, d0, d1, d2, vel, cm, kq, w4, die, req, passed, asked, asked_rows, asked_s, idx, idx_s, answer, got, planes, first_patch, ghost, above_u, above_z,
    load_sem, halo_send, halo_recv, req_send, req_recv, ans_send, ans_recv, small_sem, ghost_sem,
):
    n = n_dom * n_sub
    steps, seg = pair_hbm.shape
    here = d_hbm.shape[1]
    stride = here // seg
    ncol = d_hbm.shape[2]
    slots = steps * cap
    lists_rows = asked_s.shape[0]
    patches = die_hbm.shape[1]
    dom, sub = lax.axis_index("dom"), lax.axis_index("sub")
    me = dom * n_sub + sub

    def device(i):
        return (lax.div(i, n_sub), lax.rem(i, n_sub))

    far = n // near
    my_w = lax.rem(dom, near)
    my_g = lax.div(dom, near) * n_sub + sub

    def device_at(g, w):
        return (lax.div(g, n_sub) * near + w, lax.rem(g, n_sub))

    def other_group(t):
        return lax.rem(my_g + t, far)

    def other_member(t):
        return lax.rem(my_w + t, near)

    def partner(t):
        return lax.rem(me + t * 37, n)

    following, previous = lax.rem(me + 1, n), lax.rem(me + n - 1, n)

    inner = pl.ds(PAD, here)
    lists = [
        pltpu.make_async_copy(own_hbm, own_ref, load_sem.at[5]),
        pltpu.make_async_copy(pair_hbm, pair_ref, load_sem.at[6]),
    ]
    loads = [
        pltpu.make_async_copy(d_hbm, d0.at[:, inner], load_sem.at[0]),
        pltpu.make_async_copy(v_hbm, vel.at[:, inner], load_sem.at[1]),
        pltpu.make_async_copy(m_hbm, cm.at[inner], load_sem.at[2]),
        pltpu.make_async_copy(k_hbm, kq.at[inner], load_sem.at[3]),
        pltpu.make_async_copy(die_hbm, die, load_sem.at[4]),
    ]
    for copy in lists + loads:
        copy.start()

    barrier = pltpu.get_barrier_semaphore()

    def greet(to):
        pl.semaphore_signal(barrier, inc=1, device_id=to, device_id_type=MESH)

    def greet_groups(t, carry):
        greet(device_at(other_group(t), my_w))
        return carry

    def greet_members(t, carry):
        greet(device_at(my_g, other_member(t)))
        return carry

    lax.fori_loop(1, far, greet_groups, 0)
    lax.fori_loop(1, near, greet_members, 0)
    greet(device(following))
    greet(device(previous))

    lane_of = lax.broadcasted_iota(jnp.int32, (n, 128), 1)
    row = lax.broadcasted_iota(jnp.int32, (n, seg), 0)
    row_g, row_w = lax.div(row, near), lax.rem(row, near)
    owner_of = (lax.div(row_g, n_sub) * near + row_w) * n_sub + lax.rem(row_g, n_sub)
    before = lax.broadcasted_iota(jnp.int32, (seg, seg), 0) < lax.broadcasted_iota(jnp.int32, (seg, seg), 1)
    table = jnp.zeros((n, 128), jnp.int32)
    places = []
    for copy in lists:
        copy.wait()
    for s in range(steps):
        own = own_ref[s]
        wide = jnp.broadcast_to(own, (seg, seg))
        same = (wide == wide.T) & before
        slot = jnp.minimum(jnp.sum(same.astype(jnp.int32), axis=0, keepdims=True), cap - 1)
        places.append(own * slots + (s * cap + slot))
        pair = pair_ref[s : s + 1, :]
        mine = owner_of == own
        for k in range(cap):
            chosen = jnp.where(mine & (slot == k), pair, 0)
            table = jnp.where(lane_of == s * cap + k, jnp.sum(chosen, axis=1, keepdims=True), table)
    req[...] = table.reshape(far, near, 128)
    pl.semaphore_wait(barrier, far + near)

    def ask(t, carry):
        g = other_group(t)
        pltpu.make_async_remote_copy(
            req.at[g], passed.at[my_g], req_send.at[0], req_recv.at[0],
            device_id=device_at(g, my_w), device_id_type=MESH,
        ).start()
        return carry

    lax.fori_loop(1, far, ask, 0)
    pltpu.make_async_copy(req.at[my_g], passed.at[my_g], req_recv.at[0]).start()

    for s in range(steps):
        idx[s : s + 1, :] = places[s]
    idx_copy = pltpu.make_async_copy(idx, idx_s, small_sem.at[0])
    idx_copy.start()

    first, last = pl.ds(0, HALO), pl.ds(here - HALO, HALO)
    front, back = pl.ds(PAD - HALO, HALO), pl.ds(PAD + here, HALO)
    halos = []
    for a, (src, dst) in enumerate(((d_hbm, d0), (v_hbm, vel), (m_hbm, cm), (k_hbm, kq))):
        three = len(src.shape) == 3
        for side, (rows, place, to) in enumerate(((last, front, following), (first, back, previous))):
            copy = pltpu.make_async_remote_copy(
                src.at[:, rows] if three else src.at[rows],
                dst.at[:, place] if three else dst.at[place],
                halo_send.at[2 * a + side], halo_recv.at[2 * a + side],
                device_id=device(to), device_id_type=MESH,
            )
            copy.start()
            halos.append(copy)

    for copy in loads:
        copy.wait()

    def prepare(base, size):
        at = pl.ds(base, size)
        col = lax.broadcasted_iota(jnp.int32, (size, ncol), 1)
        kq[at, :] = jnp.where(col < ncol - 1, kq[at, :] * 0.25, 0.0)
        cm[at, :] = time_step / cm[at, :]

    def prepare_block(b, carry):
        prepare(pl.multiple_of(PAD + b * last_block, 8), last_block)
        return carry

    lax.fori_loop(0, here // last_block, prepare_block, 0)

    pltpu.make_async_copy(req, passed, req_recv.at[0]).wait()

    def hand_on(t, carry):
        w = other_member(t)
        pltpu.make_async_remote_copy(
            passed.at[:, w], asked.at[my_w], req_send.at[1], req_recv.at[1],
            device_id=device_at(my_g, w), device_id_type=MESH,
        ).start()
        return carry

    lax.fori_loop(1, near, hand_on, 0)
    pltpu.make_async_copy(passed.at[:, my_w], asked.at[my_w], req_recv.at[1]).start()

    for copy in halos:
        copy.wait()
    prepare(PAD - HALO, HALO)
    prepare(PAD + here, HALO)

    @pl.when(me == 0)
    def _():
        kq[front, :] = jnp.zeros((HALO, ncol), jnp.float32)

    @pl.when(me == n - 1)
    def _():
        tail = pl.ds(PAD + here - HALO, HALO)
        row = lax.broadcasted_iota(jnp.int32, (HALO, ncol), 0)
        kq[tail, :] = jnp.where(row == HALO - 1, 0.0, kq[tail, :])

    blocks = (here + 2 * HALO) // block
    assert blocks * block == here + 2 * HALO

    def weights(b, carry):
        base = pl.multiple_of(PAD - HALO + b * block, 8)
        both = kq[pl.ds(base, block), :] + kq[pl.ds(base - 1, block), :]
        w4[pl.ds(base, block), :] = 4.0 * (both + prev_col(both))
        return carry

    lax.fori_loop(0, blocks, weights, 0)

    pltpu.make_async_copy(asked, asked, req_recv.at[1]).wait()
    asked_rows[...] = asked[...].reshape(n, 128).T[:lists_rows]
    to_scalar = pltpu.make_async_copy(asked_rows, asked_s, small_sem.at[1])
    to_scalar.start()
    to_scalar.wait()
    idx_copy.wait()

    def gather(p, dst, at):
        p_dom, p_sub = device(p)
        w, g = lax.rem(p_dom, near), lax.div(p_dom, near) * n_sub + p_sub
        for s in range(steps):
            for k in range(cap):
                dst[at + (s * cap + k)] = die[s, jnp.clip(asked_s[s * cap + k, w * far + g], 0, patches - 1)]

    def reply(t, carry):
        p = partner(t)
        gather(p, answer, p * slots)
        pltpu.make_async_remote_copy(
            answer.at[pl.ds(p * slots, slots)], got.at[pl.ds(me * slots, slots)], ans_send, ans_recv,
            device_id=device(p), device_id_type=MESH,
        ).start()
        return carry

    lax.fori_loop(1, n, reply, 0)
    gather(me, got, me * slots)

    def free_step(src, d_to, v_to, first_row, count, size):
        def part(b, carry):
            base = pl.multiple_of(first_row + b * size, 8)
            top_row = lax.broadcasted_iota(jnp.int32, (8, ncol), 0) == 0
            shifted = [None] * 3
            for i in range(size // 8 + 1):
                at = pl.ds(base + 8 * (i - 1), 8)
                below = pl.ds(base + 8 * (i - 1) + 1, 8)
                for c in range(3):
                    d = src[c, at, :]
                    box = d + src[c, below, :]
                    t = kq[at, :] * (box + next_col(box))
                    down = pltpu.roll(t, 1, 0)
                    if i:
                        t = t + jnp.where(top_row, shifted[c], down)
                        force = t + prev_col(t) - w4[at, :] * d
                        v = vel[c, at, :] + cm[at, :] * force
                        v_to(base, size)[c, 8 * (i - 1) : 8 * i, :] = v
                        d_to(base, size)[c, 8 * (i - 1) : 8 * i, :] = d + time_step * v
                    shifted[c] = down
            return carry

        lax.fori_loop(0, count, part, 0)

    def same_rows(ref):
        return lambda base, size: ref.at[:, pl.ds(base, size)]

    def own_rows(ref):
        return lambda base, size: ref.at[:, pl.ds(pl.multiple_of(base - PAD, 8), size)]

    free_step(d0, same_rows(d1), same_rows(vel), PAD - HALO, blocks, block)
    free_step(d1, same_rows(d2), same_rows(vel), PAD - HALO, blocks, block)
    free_step(d2, own_rows(od_ref), own_rows(ov_ref), PAD, here // last_block, last_block)

    wire = pl.ds(0, (n - 1) * slots)
    pltpu.make_async_copy(answer.at[wire], got.at[wire], ans_recv).wait()

    for s in range(steps):
        first_patch[s] = got[idx_s[s, 0]]
    ghost_copy = pltpu.make_async_remote_copy(
        first_patch, ghost, ghost_sem.at[0], ghost_sem.at[1],
        device_id=device(previous), device_id_type=MESH,
    )
    ghost_copy.start()

    def place(j, carry):
        for s in range(steps):
            planes[s, pl.ds(j * 4, 4), :] = got[idx_s[s, j]]
        return carry

    lax.fori_loop(0, seg, place, 0, unroll=8)

    flat = {"cm": cm, "kq": kq, "w4": w4}
    deep = {"d0": d0, "d1": d1, "d2": d2}
    chunk = width * stride

    def correct(q, carry):
        base = PAD + q * chunk

        def rows(name, o):
            at = pl.ds(base + o, width, stride=stride)
            if name in flat:
                return flat[name][at, :]
            return [deep[name][c, at, :] for c in range(3)]

        nearby = [[planes[s, pl.ds(q * width * 4 + c, width, stride=4), :] for c in range(4)] for s in range(steps)]
        u, z = contact_response(nearby, rows)
        for c in range(3):
            for o in range(0, 3):
                at = pl.ds(q * chunk + o, width, stride=stride)
                od_ref[c, at, :] += u[o][c]
                ov_ref[c, at, :] += z[o][c]
            for o in (-2, -1):
                at = pl.ds(pl.multiple_of(q * width, 8), width)
                above_u[o + 2, c, at, :] = u[o][c]
                above_z[o + 2, c, at, :] = z[o][c]
        return carry

    lax.fori_loop(0, seg // width, correct, 0)

    ghost_copy.wait()

    def ghost_rows(name, o):
        at = pl.ds(PAD + here + o, 1)
        if name in flat:
            return flat[name][at, :]
        return [deep[name][c, at, :] for c in range(3)]

    nearby = [[ghost[s, pl.ds(c, 1), :] for c in range(4)] for s in range(steps)]
    u, z = contact_response(nearby, ghost_rows)
    for o in (-2, -1):
        for c in range(3):
            above_u[o + 2, c, pl.ds(seg, 1), :] = u[o][c]
            above_z[o + 2, c, pl.ds(seg, 1), :] = z[o][c]

    def correct_above(q, carry):
        for o in (-2, -1):
            at = pl.ds(q * chunk + stride + o, width, stride=stride)
            block_after = pl.ds(q * width + 1, width)
            for c in range(3):
                od_ref[c, at, :] += above_u[o + 2, c, block_after, :]
                ov_ref[c, at, :] += above_z[o + 2, c, block_after, :]
        return carry

    lax.fori_loop(0, seg // width, correct_above, 0)

    pltpu.make_async_copy(answer.at[wire], got.at[wire], ans_send).wait()
    pltpu.make_async_copy(req.at[pl.ds(0, far - 1)], passed.at[pl.ds(0, far - 1)], req_send.at[0]).wait()
    pltpu.make_async_copy(asked.at[pl.ds(0, near - 1)], asked.at[pl.ds(0, near - 1)], req_send.at[1]).wait()


def body(n_dom, n_sub, displace, velocity, nodal_mass, stiffness, die_planes, owners, pairs):
    n = n_dom * n_sub
    here, ncol = displace.shape[1:]
    steps, seg = pairs.shape
    cap = max(2, 2 * seg // n)
    slots = steps * cap
    ext = here + 2 * PAD
    tiles = (here + 2 * HALO) // 8
    block = 8 * max(b for b in range(1, 44) if tiles % b == 0)
    last_block = 8 * max(b for b in range(1, 33) if here // 8 % b == 0)
    width = min(32, seg)
    near = min(8, n_dom // 2)
    far = n // near
    f32, i32 = jnp.float32, jnp.int32
    any_spec = pl.BlockSpec(memory_space=pl.ANY)
    vmem_spec = pl.BlockSpec(memory_space=pltpu.VMEM)
    dma = pltpu.SemaphoreType.DMA
    return pl.pallas_call(
        functools.partial(kernel, n_dom, n_sub, cap, near, block, last_block, width),
        out_shape=[pltpu.VMEM(displace.shape, f32)] * 2,
        in_specs=[any_spec] * 7,
        out_specs=[vmem_spec] * 2,
        scratch_shapes=[
            pltpu.VMEM((steps, 1, seg), i32),
            pltpu.VMEM((steps, seg), i32),
            pltpu.VMEM((3, ext, ncol), f32),
            pltpu.VMEM((3, ext, ncol), f32),
            pltpu.VMEM((3, ext, ncol), f32),
            pltpu.VMEM((3, ext, ncol), f32),
            pltpu.VMEM((ext, ncol), f32),
            pltpu.VMEM((ext, ncol), f32),
            pltpu.VMEM((ext, ncol), f32),
            pltpu.VMEM(die_planes.shape, f32),
            pltpu.VMEM((far, near, 128), i32),
            pltpu.VMEM((far, near, 128), i32),
            pltpu.VMEM((near, far, 128), i32),
            pltpu.VMEM((-(-slots // 8) * 8, n), i32),
            pltpu.SMEM((-(-slots // 8) * 8, n), i32),
            pltpu.VMEM((8, seg), i32),
            pltpu.SMEM((8, seg), i32),
            pltpu.VMEM((n * slots, 4, ncol), f32),
            pltpu.VMEM((n * slots, 4, ncol), f32),
            pltpu.VMEM((steps, seg * 4 + 32, ncol), f32),
            pltpu.VMEM((steps, 4, ncol), f32),
            pltpu.VMEM((steps, 4, ncol), f32),
            pltpu.VMEM((2, 3, seg + 8, ncol), f32),
            pltpu.VMEM((2, 3, seg + 8, ncol), f32),
            dma((7,)), dma((8,)), dma((8,)), dma((2,)), dma((2,)), dma, dma, dma((2,)), dma((2,)),
        ],
        compiler_params=pltpu.CompilerParams(
            collective_id=0, has_side_effects=True, vmem_limit_bytes=40 * 1024 * 1024
        ),
        name="stamp",
    )(*[
        pltpu.with_memory_space_constraint(x, pltpu.HBM)
        for x in (jnp.swapaxes(owners, 1, 2), pairs, displace, velocity, nodal_mass, stiffness, die_planes)
    ])


def solution(mesh):
    in_specs = (
        P(None, ("dom", "sub"), None),
        P(None, ("dom", "sub"), None),
        P(("dom", "sub"), None),
        P(("dom", "sub"), None),
        P(None, ("dom", "sub"), None, None),
        P(None, ("dom", "sub"), None),
        P(None, ("dom", "sub")),
    )
    out_specs = (P(None, ("dom", "sub"), None), P(None, ("dom", "sub"), None))
    run = functools.partial(body, mesh.shape["dom"], mesh.shape["sub"])
    return jax.shard_map(run, mesh=mesh, in_specs=in_specs, out_specs=out_specs, check_vma=False)
```

```python
import functools

import jax
import jax.numpy as jnp
from jax import lax
from jax.experimental import pallas as pl
from jax.experimental.pallas import tpu as pltpu
from jax.sharding import PartitionSpec as P

STEPS = 3
time_step = 0.2
penalty = 1.0

MESH = pl.DeviceIdType.MESH
PAD = 16
HALO = 8
LEAD = 2


def next_col(x):
    return pltpu.roll(x, x.shape[-1] - 1, x.ndim - 1)


def prev_col(x):
    return pltpu.roll(x, 1, x.ndim - 1)


def contact(planes, position):
    normal, height = planes[:3], planes[3]
    depth = height - (normal[0] * position[0] + normal[1] * position[1] + normal[2] * position[2])
    push = penalty * jnp.maximum(depth, 0.0)
    return [push * normal[c] for c in range(3)]


def contact_response(planes, rows):
    cm = {o: rows("cm", o) for o in range(-2, 3)}
    kq = {o: rows("kq", o) for o in range(-2, 2)}
    w4 = {o: rows("w4", o) for o in range(-1, 2)}
    u = {}
    z = {}
    for step in range(STEPS):
        free = rows("d%d" % step, 0)
        position = [free[c] + u[0][c] if step else free[c] for c in range(3)]
        push = contact(planes[step], position)
        new_u, new_z = {}, {}
        for o in range(-step, step + 1):
            new_u[o], new_z[o] = [], []
        for c in range(3):
            spread = {}
            for o in range(-step, step):
                parts = [u[r][c] for r in (o, o + 1) if r in u]
                box = parts[0] if len(parts) == 1 else parts[0] + parts[1]
                t = kq[o] * (box + next_col(box))
                spread[o] = t + prev_col(t)
            for o in range(-step, step + 1):
                terms = [spread[r] for r in (o - 1, o) if r in spread]
                if o in u:
                    terms.append(-(w4[o] * u[o][c]))
                if o == 0:
                    terms.append(push[c])
                force = terms[0]
                for term in terms[1:]:
                    force = force + term
                dz = cm[o] * force
                zc = z[o][c] + dz if o in z else dz
                uc = time_step * zc
                if o in u:
                    uc = u[o][c] + uc
                new_z[o].append(zc)
                new_u[o].append(uc)
        u, z = new_u, new_z
    return u, z


def kernel(
    n_dom, n_sub, cap, near, lead, block, last_block, width,
    own_hbm, pair_hbm, d_hbm, v_hbm, m_hbm, k_hbm, die_hbm,
    od_ref, ov_ref,
    own_ref, pair_ref, d0, d1, d2, vel, cm, kq, w4, die, req, passed, asked, asked_rows, asked_s, idx, idx_s, answer, got, planes, first_patch, ghost, above_u, above_z,
    load_sem, halo_send, halo_recv, req_send, req_recv, ans_send, ans_recv, small_sem, ghost_sem,
):
    n = n_dom * n_sub
    steps, seg = pair_hbm.shape
    here = d_hbm.shape[1]
    stride = here // seg
    ncol = d_hbm.shape[2]
    slots = steps * cap
    lists_rows = asked_s.shape[0]
    patches = die_hbm.shape[1]
    dom, sub = lax.axis_index("dom"), lax.axis_index("sub")
    me = dom * n_sub + sub

    def device(i):
        return (lax.div(i, n_sub), lax.rem(i, n_sub))

    far = n // near
    my_w = lax.rem(dom, near)
    my_g = lax.div(dom, near) * n_sub + sub

    def device_at(g, w):
        return (lax.div(g, n_sub) * near + w, lax.rem(g, n_sub))

    def other_group(t):
        return lax.rem(my_g + t, far)

    def other_member(t):
        return lax.rem(my_w + t, near)

    following, previous = lax.rem(me + 1, n), lax.rem(me + n - 1, n)

    inner = pl.ds(PAD, here)
    lists = [
        pltpu.make_async_copy(own_hbm, own_ref, load_sem.at[5]),
        pltpu.make_async_copy(pair_hbm, pair_ref, load_sem.at[6]),
    ]
    loads = [
        pltpu.make_async_copy(d_hbm, d0.at[:, inner], load_sem.at[0]),
        pltpu.make_async_copy(v_hbm, vel.at[:, inner], load_sem.at[1]),
        pltpu.make_async_copy(m_hbm, cm.at[inner], load_sem.at[2]),
        pltpu.make_async_copy(k_hbm, kq.at[inner], load_sem.at[3]),
        pltpu.make_async_copy(die_hbm, die, load_sem.at[4]),
    ]
    for copy in lists + loads:
        copy.start()

    barrier = pltpu.get_barrier_semaphore()

    def greet(to):
        pl.semaphore_signal(barrier, inc=1, device_id=to, device_id_type=MESH)

    def greet_groups(t, carry):
        greet(device_at(other_group(t), my_w))
        return carry

    def greet_members(t, carry):
        greet(device_at(my_g, other_member(t)))
        return carry

    lax.fori_loop(1, far, greet_groups, 0)
    lax.fori_loop(1, near, greet_members, 0)
    greet(device(following))
    greet(device(previous))

    lane_of = lax.broadcasted_iota(jnp.int32, (n, 128), 1)
    row = lax.broadcasted_iota(jnp.int32, (n, seg), 0)
    row_g, row_w = lax.div(row, near), lax.rem(row, near)
    owner_of = (lax.div(row_g, n_sub) * near + row_w) * n_sub + lax.rem(row_g, n_sub)
    before = lax.broadcasted_iota(jnp.int32, (seg, seg), 0) < lax.broadcasted_iota(jnp.int32, (seg, seg), 1)
    table = jnp.zeros((n, 128), jnp.int32)
    places = []
    for copy in lists:
        copy.wait()
    for s in range(steps):
        own = own_ref[s]
        wide = jnp.broadcast_to(own, (seg, seg))
        same = (wide == wide.T) & before
        slot = jnp.minimum(jnp.sum(same.astype(jnp.int32), axis=0, keepdims=True), cap - 1)
        places.append(own * slots + (s * cap + slot))
        pair = pair_ref[s : s + 1, :]
        mine = owner_of == own
        for k in range(cap):
            chosen = jnp.where(mine & (slot == k), pair, 0)
            table = jnp.where(lane_of == s * cap + k, jnp.sum(chosen, axis=1, keepdims=True), table)
    req[...] = table.reshape(far, near, 128)
    pl.semaphore_wait(barrier, far + near)

    def ask(t, carry):
        g = other_group(t)
        pltpu.make_async_remote_copy(
            req.at[g], passed.at[my_g], req_send.at[0], req_recv.at[0],
            device_id=device_at(g, my_w), device_id_type=MESH,
        ).start()
        return carry

    lax.fori_loop(1, far, ask, 0)
    pltpu.make_async_copy(req.at[my_g], passed.at[my_g], req_recv.at[0]).start()

    for s in range(steps):
        idx[s : s + 1, :] = places[s]
    idx_copy = pltpu.make_async_copy(idx, idx_s, small_sem.at[0])
    idx_copy.start()

    first, last = pl.ds(0, HALO), pl.ds(here - HALO, HALO)
    front, back = pl.ds(PAD - HALO, HALO), pl.ds(PAD + here, HALO)
    halos = []
    for a, (src, dst) in enumerate(((d_hbm, d0), (v_hbm, vel), (m_hbm, cm), (k_hbm, kq))):
        three = len(src.shape) == 3
        for side, (rows, place, to) in enumerate(((last, front, following), (first, back, previous))):
            copy = pltpu.make_async_remote_copy(
                src.at[:, rows] if three else src.at[rows],
                dst.at[:, place] if three else dst.at[place],
                halo_send.at[2 * a + side], halo_recv.at[2 * a + side],
                device_id=device(to), device_id_type=MESH,
            )
            copy.start()
            halos.append(copy)

    for copy in loads:
        copy.wait()

    def prepare(base, size):
        at = pl.ds(base, size)
        col = lax.broadcasted_iota(jnp.int32, (size, ncol), 1)
        kq[at, :] = jnp.where(col < ncol - 1, kq[at, :] * 0.25, 0.0)
        cm[at, :] = time_step / cm[at, :]

    def prepare_block(b, carry):
        prepare(pl.multiple_of(PAD + b * last_block, 8), last_block)
        return carry

    lax.fori_loop(0, here // last_block, prepare_block, 0)

    pltpu.make_async_copy(req, passed, req_recv.at[0]).wait()

    def hand_on(t, carry):
        w = other_member(t)
        pltpu.make_async_remote_copy(
            passed.at[:, w], asked.at[my_w], req_send.at[1], req_recv.at[1],
            device_id=device_at(my_g, w), device_id_type=MESH,
        ).start()
        return carry

    lax.fori_loop(1, near, hand_on, 0)
    pltpu.make_async_copy(passed.at[:, my_w], asked.at[my_w], req_recv.at[1]).start()

    for copy in halos:
        copy.wait()
    prepare(PAD - HALO, HALO)
    prepare(PAD + here, HALO)

    @pl.when(me == 0)
    def _():
        kq[front, :] = jnp.zeros((HALO, ncol), jnp.float32)

    @pl.when(me == n - 1)
    def _():
        tail = pl.ds(PAD + here - HALO, HALO)
        row = lax.broadcasted_iota(jnp.int32, (HALO, ncol), 0)
        kq[tail, :] = jnp.where(row == HALO - 1, 0.0, kq[tail, :])

    blocks = (here + 2 * HALO) // block
    assert blocks * block == here + 2 * HALO

    def weights(b, carry):
        base = pl.multiple_of(PAD - HALO + b * block, 8)
        both = kq[pl.ds(base, block), :] + kq[pl.ds(base - 1, block), :]
        w4[pl.ds(base, block), :] = 4.0 * (both + prev_col(both))
        return carry

    lax.fori_loop(0, blocks, weights, 0)

    pltpu.make_async_copy(asked, asked, req_recv.at[1]).wait()
    asked_rows[...] = asked[...].reshape(n, 128).T[:lists_rows]
    to_scalar = pltpu.make_async_copy(asked_rows, asked_s, small_sem.at[1])
    to_scalar.start()
    to_scalar.wait()
    idx_copy.wait()

    def gather(w, g, dst, at):
        for s in range(steps):
            for k in range(cap):
                dst[at + (s * cap + k)] = die[s, jnp.clip(asked_s[s * cap + k, w * far + g], 0, patches - 1)]

    layers = max(1, near // 2)
    cores = near // layers
    per_layer = n // layers
    my_layer, my_core = lax.div(my_w, cores), lax.rem(my_w, cores)
    my_place = (lax.div(my_g, n_sub) * cores + my_core) * n_sub + sub

    def reply(layer, turn):
        place = lax.rem(my_place + turn * 13, per_layer)
        line, x = lax.div(place, n_sub), lax.rem(place, n_sub)
        w = layer * cores + lax.rem(line, cores)
        g = lax.div(line, cores) * n_sub + x
        to = device_at(g, w)
        p = to[0] * n_sub + to[1]

        @pl.when((turn >= 0) & (turn < per_layer) & (p != me))
        def _():
            gather(w, g, answer, p * slots)
            pltpu.make_async_remote_copy(
                answer.at[pl.ds(p * slots, slots)], got.at[pl.ds(me * slots, slots)], ans_send, ans_recv,
                device_id=to, device_id_type=MESH,
            ).start()

    def reply_round(i, carry):
        for layer in range(layers):
            reply(layer, i - lead * layer)
        return carry

    lax.fori_loop(0, per_layer + lead * (layers - 1), reply_round, 0)
    gather(my_w, my_g, got, me * slots)

    def free_step(src, d_to, v_to, first_row, count, size):
        def part(b, carry):
            base = pl.multiple_of(first_row + b * size, 8)
            top_row = lax.broadcasted_iota(jnp.int32, (8, ncol), 0) == 0
            shifted = [None] * 3
            for i in range(size // 8 + 1):
                at = pl.ds(base + 8 * (i - 1), 8)
                below = pl.ds(base + 8 * (i - 1) + 1, 8)
                for c in range(3):
                    d = src[c, at, :]
                    box = d + src[c, below, :]
                    t = kq[at, :] * (box + next_col(box))
                    down = pltpu.roll(t, 1, 0)
                    if i:
                        t = t + jnp.where(top_row, shifted[c], down)
                        force = t + prev_col(t) - w4[at, :] * d
                        v = vel[c, at, :] + cm[at, :] * force
                        v_to(base, size)[c, 8 * (i - 1) : 8 * i, :] = v
                        d_to(base, size)[c, 8 * (i - 1) : 8 * i, :] = d + time_step * v
                    shifted[c] = down
            return carry

        lax.fori_loop(0, count, part, 0)

    def same_rows(ref):
        return lambda base, size: ref.at[:, pl.ds(base, size)]

    def own_rows(ref):
        return lambda base, size: ref.at[:, pl.ds(pl.multiple_of(base - PAD, 8), size)]

    free_step(d0, same_rows(d1), same_rows(vel), PAD - HALO, blocks, block)
    free_step(d1, same_rows(d2), same_rows(vel), PAD - HALO, blocks, block)
    free_step(d2, own_rows(od_ref), own_rows(ov_ref), PAD, here // last_block, last_block)

    wire = pl.ds(0, (n - 1) * slots)
    pltpu.make_async_copy(answer.at[wire], got.at[wire], ans_recv).wait()

    for s in range(steps):
        first_patch[s] = got[idx_s[s, 0]]
    ghost_copy = pltpu.make_async_remote_copy(
        first_patch, ghost, ghost_sem.at[0], ghost_sem.at[1],
        device_id=device(previous), device_id_type=MESH,
    )
    ghost_copy.start()

    def place(j, carry):
        for s in range(steps):
            planes[s, pl.ds(j * 4, 4), :] = got[idx_s[s, j]]
        return carry

    lax.fori_loop(0, seg, place, 0, unroll=8)

    flat = {"cm": cm, "kq": kq, "w4": w4}
    deep = {"d0": d0, "d1": d1, "d2": d2}
    chunk = width * stride

    def correct(q, carry):
        base = PAD + q * chunk

        def rows(name, o):
            at = pl.ds(base + o, width, stride=stride)
            if name in flat:
                return flat[name][at, :]
            return [deep[name][c, at, :] for c in range(3)]

        nearby = [[planes[s, pl.ds(q * width * 4 + c, width, stride=4), :] for c in range(4)] for s in range(steps)]
        u, z = contact_response(nearby, rows)
        for c in range(3):
            for o in range(0, 3):
                at = pl.ds(q * chunk + o, width, stride=stride)
                od_ref[c, at, :] += u[o][c]
                ov_ref[c, at, :] += z[o][c]
            for o in (-2, -1):
                at = pl.ds(pl.multiple_of(q * width, 8), width)
                above_u[o + 2, c, at, :] = u[o][c]
                above_z[o + 2, c, at, :] = z[o][c]
        return carry

    lax.fori_loop(0, seg // width, correct, 0)

    ghost_copy.wait()

    def ghost_rows(name, o):
        at = pl.ds(PAD + here + o, 1)
        if name in flat:
            return flat[name][at, :]
        return [deep[name][c, at, :] for c in range(3)]

    nearby = [[ghost[s, pl.ds(c, 1), :] for c in range(4)] for s in range(steps)]
    u, z = contact_response(nearby, ghost_rows)
    for o in (-2, -1):
        for c in range(3):
            above_u[o + 2, c, pl.ds(seg, 1), :] = u[o][c]
            above_z[o + 2, c, pl.ds(seg, 1), :] = z[o][c]

    def correct_above(q, carry):
        for o in (-2, -1):
            at = pl.ds(q * chunk + stride + o, width, stride=stride)
            block_after = pl.ds(q * width + 1, width)
            for c in range(3):
                od_ref[c, at, :] += above_u[o + 2, c, block_after, :]
                ov_ref[c, at, :] += above_z[o + 2, c, block_after, :]
        return carry

    lax.fori_loop(0, seg // width, correct_above, 0)

    pltpu.make_async_copy(answer.at[wire], got.at[wire], ans_send).wait()
    pltpu.make_async_copy(req.at[pl.ds(0, far - 1)], passed.at[pl.ds(0, far - 1)], req_send.at[0]).wait()
    pltpu.make_async_copy(asked.at[pl.ds(0, near - 1)], asked.at[pl.ds(0, near - 1)], req_send.at[1]).wait()


def body(n_dom, n_sub, displace, velocity, nodal_mass, stiffness, die_planes, owners, pairs):
    n = n_dom * n_sub
    here, ncol = displace.shape[1:]
    steps, seg = pairs.shape
    cap = max(2, 2 * seg // n)
    slots = steps * cap
    ext = here + 2 * PAD
    tiles = (here + 2 * HALO) // 8
    block = 8 * max(b for b in range(1, 44) if tiles % b == 0)
    last_block = 8 * max(b for b in range(1, 33) if here // 8 % b == 0)
    width = min(32, seg)
    near = min(8, n_dom // 2)
    far = n // near
    f32, i32 = jnp.float32, jnp.int32
    any_spec = pl.BlockSpec(memory_space=pl.ANY)
    vmem_spec = pl.BlockSpec(memory_space=pltpu.VMEM)
    dma = pltpu.SemaphoreType.DMA
    return pl.pallas_call(
        functools.partial(kernel, n_dom, n_sub, cap, near, LEAD, block, last_block, width),
        out_shape=[pltpu.VMEM(displace.shape, f32)] * 2,
        in_specs=[any_spec] * 7,
        out_specs=[vmem_spec] * 2,
        scratch_shapes=[
            pltpu.VMEM((steps, 1, seg), i32),
            pltpu.VMEM((steps, seg), i32),
            pltpu.VMEM((3, ext, ncol), f32),
            pltpu.VMEM((3, ext, ncol), f32),
            pltpu.VMEM((3, ext, ncol), f32),
            pltpu.VMEM((3, ext, ncol), f32),
            pltpu.VMEM((ext, ncol), f32),
            pltpu.VMEM((ext, ncol), f32),
            pltpu.VMEM((ext, ncol), f32),
            pltpu.VMEM(die_planes.shape, f32),
            pltpu.VMEM((far, near, 128), i32),
            pltpu.VMEM((far, near, 128), i32),
            pltpu.VMEM((near, far, 128), i32),
            pltpu.VMEM((-(-slots // 8) * 8, n), i32),
            pltpu.SMEM((-(-slots // 8) * 8, n), i32),
            pltpu.VMEM((8, seg), i32),
            pltpu.SMEM((8, seg), i32),
            pltpu.VMEM((n * slots, 4, ncol), f32),
            pltpu.VMEM((n * slots, 4, ncol), f32),
            pltpu.VMEM((steps, seg * 4 + 32, ncol), f32),
            pltpu.VMEM((steps, 4, ncol), f32),
            pltpu.VMEM((steps, 4, ncol), f32),
            pltpu.VMEM((2, 3, seg + 8, ncol), f32),
            pltpu.VMEM((2, 3, seg + 8, ncol), f32),
            dma((7,)), dma((8,)), dma((8,)), dma((2,)), dma((2,)), dma, dma, dma((2,)), dma((2,)),
        ],
        compiler_params=pltpu.CompilerParams(
            collective_id=0, has_side_effects=True, vmem_limit_bytes=40 * 1024 * 1024
        ),
        name="stamp",
    )(*[
        pltpu.with_memory_space_constraint(x, pltpu.HBM)
        for x in (jnp.swapaxes(owners, 1, 2), pairs, displace, velocity, nodal_mass, stiffness, die_planes)
    ])


def solution(mesh):
    in_specs = (
        P(None, ("dom", "sub"), None),
        P(None, ("dom", "sub"), None),
        P(("dom", "sub"), None),
        P(("dom", "sub"), None),
        P(None, ("dom", "sub"), None, None),
        P(None, ("dom", "sub"), None),
        P(None, ("dom", "sub")),
    )
    out_specs = (P(None, ("dom", "sub"), None), P(None, ("dom", "sub"), None))
    run = functools.partial(body, mesh.shape["dom"], mesh.shape["sub"])
    return jax.shard_map(run, mesh=mesh, in_specs=in_specs, out_specs=out_specs, check_vma=False)
```

```python
import functools

import jax
import jax.numpy as jnp
from jax import lax
from jax.experimental import pallas as pl
from jax.experimental.pallas import tpu as pltpu
from jax.sharding import PartitionSpec as P

STEPS = 3
time_step = 0.2
penalty = 1.0

MESH = pl.DeviceIdType.MESH
PAD = 16
HALO = 8
CORES = 2
LEAD = 1


def next_col(x):
    return pltpu.roll(x, x.shape[-1] - 1, x.ndim - 1)


def prev_col(x):
    return pltpu.roll(x, 1, x.ndim - 1)


def contact(planes, position):
    normal, height = planes[:3], planes[3]
    depth = height - (normal[0] * position[0] + normal[1] * position[1] + normal[2] * position[2])
    push = penalty * jnp.maximum(depth, 0.0)
    return [push * normal[c] for c in range(3)]


def contact_response(planes, rows):
    cm = {o: rows("cm", o) for o in range(-2, 3)}
    kq = {o: rows("kq", o) for o in range(-2, 2)}
    w4 = {o: rows("w4", o) for o in range(-1, 2)}
    u = {}
    z = {}
    for step in range(STEPS):
        free = rows("d%d" % step, 0)
        position = [free[c] + u[0][c] if step else free[c] for c in range(3)]
        push = contact(planes[step], position)
        new_u, new_z = {}, {}
        for o in range(-step, step + 1):
            new_u[o], new_z[o] = [], []
        for c in range(3):
            spread = {}
            for o in range(-step, step):
                parts = [u[r][c] for r in (o, o + 1) if r in u]
                box = parts[0] if len(parts) == 1 else parts[0] + parts[1]
                t = kq[o] * (box + next_col(box))
                spread[o] = t + prev_col(t)
            for o in range(-step, step + 1):
                terms = [spread[r] for r in (o - 1, o) if r in spread]
                if o in u:
                    terms.append(-(w4[o] * u[o][c]))
                if o == 0:
                    terms.append(push[c])
                force = terms[0]
                for term in terms[1:]:
                    force = force + term
                dz = cm[o] * force
                zc = z[o][c] + dz if o in z else dz
                uc = time_step * zc
                if o in u:
                    uc = u[o][c] + uc
                new_z[o].append(zc)
                new_u[o].append(uc)
        u, z = new_u, new_z
    return u, z


def kernel(
    n_dom, n_sub, cap, near, lead, block, last_block, width,
    own_hbm, pair_hbm, d_hbm, v_hbm, m_hbm, k_hbm, die_hbm,
    od_ref, ov_ref,
    own_ref, pair_ref, d0, d1, d2, vel, cm, kq, w4, die_x, die_y, die_z, req, passed, asked, asked_rows, asked_s, idx, idx_s, answer, got, planes, first_patch, ghost, above_u, above_z,
    load_sem, halo_send, halo_recv, die_send, die_recv, req_send, req_recv, ans_send, ans_recv, small_sem, ghost_sem,
):
    n = n_dom * n_sub
    steps, seg = pair_hbm.shape
    here = d_hbm.shape[1]
    stride = here // seg
    ncol = d_hbm.shape[2]
    assert steps == 3
    lists_rows = asked_s.shape[0]
    patches = die_hbm.shape[1]
    dom, sub = lax.axis_index("dom"), lax.axis_index("sub")
    me = dom * n_sub + sub

    def device(i):
        return (lax.div(i, n_sub), lax.rem(i, n_sub))

    far = n // near
    lines = (n_sub, far // n_sub, near // CORES)
    my_w = lax.rem(dom, near)
    my_x, my_y, my_z, my_core = sub, lax.div(dom, near), lax.div(my_w, CORES), lax.rem(my_w, CORES)
    my_g = my_y * n_sub + my_x

    def device_at(g, w):
        return (lax.div(g, n_sub) * near + w, lax.rem(g, n_sub))

    def other_group(t):
        return lax.rem(my_g + t, far)

    def other_member(t):
        return lax.rem(my_w + t, near)

    following, previous = lax.rem(me + 1, n), lax.rem(me + n - 1, n)

    inner = pl.ds(PAD, here)
    lists = [
        pltpu.make_async_copy(own_hbm, own_ref, load_sem.at[5]),
        pltpu.make_async_copy(pair_hbm, pair_ref, load_sem.at[6]),
    ]
    loads = [
        pltpu.make_async_copy(d_hbm, d0.at[:, inner], load_sem.at[0]),
        pltpu.make_async_copy(v_hbm, vel.at[:, inner], load_sem.at[1]),
        pltpu.make_async_copy(m_hbm, cm.at[inner], load_sem.at[2]),
        pltpu.make_async_copy(k_hbm, kq.at[inner], load_sem.at[3]),
        pltpu.make_async_copy(die_hbm.at[0], die_x.at[my_x], load_sem.at[4]),
        pltpu.make_async_copy(die_hbm.at[1], die_y.at[my_y], load_sem.at[7]),
        pltpu.make_async_copy(die_hbm.at[2], die_z.at[0], load_sem.at[8]),
    ]
    for copy in lists + loads:
        copy.start()

    barrier = pltpu.get_barrier_semaphore()

    def greet(to):
        pl.semaphore_signal(barrier, inc=1, device_id=to, device_id_type=MESH)

    def greet_groups(t, carry):
        greet(device_at(other_group(t), my_w))
        return carry

    def greet_members(t, carry):
        greet(device_at(my_g, other_member(t)))
        return carry

    lax.fori_loop(1, far, greet_groups, 0)
    lax.fori_loop(1, near, greet_members, 0)
    greet(device(following))
    greet(device(previous))

    pl.semaphore_wait(barrier, far + near)

    for axis, (count, mine, copies) in enumerate(zip(lines, (my_x, my_y, my_z), (die_x, die_y, die_z))):
        for t in range(1, count):
            there = lax.rem(mine + t, count)
            to = (
                device_at(my_y * n_sub + there, my_w),
                device_at(there * n_sub + my_x, my_w),
                device_at(my_g, there * CORES + my_core),
            )[axis]
            pltpu.make_async_remote_copy(
                die_hbm.at[axis], copies.at[count - t if axis == 2 else mine],
                die_send.at[axis], die_recv.at[axis], device_id=to, device_id_type=MESH,
            ).start()

    lane_of = lax.broadcasted_iota(jnp.int32, (n, 128), 1)
    row = lax.broadcasted_iota(jnp.int32, (n, seg), 0)
    row_g, row_w = lax.div(row, near), lax.rem(row, near)
    owner_of = (lax.div(row_g, n_sub) * near + row_w) * n_sub + lax.rem(row_g, n_sub)
    before = lax.broadcasted_iota(jnp.int32, (seg, seg), 0) < lax.broadcasted_iota(jnp.int32, (seg, seg), 1)
    table = jnp.zeros((n, 128), jnp.int32)
    places = []
    for copy in lists:
        copy.wait()
    for s in range(steps):
        own = own_ref[s]
        wide = jnp.broadcast_to(own, (seg, seg))
        same = (wide == wide.T) & before
        slot = jnp.minimum(jnp.sum(same.astype(jnp.int32), axis=0, keepdims=True), cap - 1)
        own_dom, own_x = lax.div(own, n_sub), lax.rem(own, n_sub)
        own_y, own_w = lax.div(own_dom, near), lax.rem(own_dom, near)
        own_z, own_core = lax.div(own_w, CORES), lax.rem(own_w, CORES)
        line, at_line = (
            (own_y * near + own_w, own_x),
            (own_x * near + own_w, own_y),
            ((own_y * n_sub + own_x) * CORES + own_core, lax.rem(own_z + (lines[2] - my_z), lines[2])),
        )[s]
        places.append((s * n + line * lines[s] + at_line) * cap + slot)
        pair = pair_ref[s : s + 1, :]
        mine = owner_of == own
        for k in range(cap):
            chosen = jnp.where(mine & (slot == k), pair, 0)
            table = jnp.where(lane_of == s * cap + k, jnp.sum(chosen, axis=1, keepdims=True), table)
    by_group = [table[near * g : near * (g + 1)] for g in range(far)]
    lane = lax.broadcasted_iota(jnp.int32, (near, 128), 1)

    def lanes_of(s, value, to):
        value = jnp.where((lane >= s * cap) & (lane < (s + 1) * cap), value, 0)
        shift = to - s * cap
        return pltpu.roll(value, shift, 1) if shift else value

    firsts = (0, lines[0] * cap, (lines[0] + lines[1]) * cap)
    along_x = [
        sum(lanes_of(0, by_group[y * n_sub + x], firsts[0] + x * cap) for x in range(lines[0])) for y in range(lines[1])
    ]
    along_y = [
        sum(lanes_of(1, by_group[y * n_sub + x], firsts[1] + y * cap) for y in range(lines[1])) for x in range(lines[0])
    ]
    for g in range(far):
        along_z = 0
        for z in range(lines[2]):
            turned = pltpu.roll(by_group[g], near - z * CORES, 0) if z else by_group[g]
            along_z = along_z + lanes_of(2, turned, firsts[2] + z * cap)
        req[g] = along_x[g // n_sub] + along_y[g % n_sub] + along_z
    def ask(t, carry):
        g = other_group(t)
        pltpu.make_async_remote_copy(
            req.at[g], passed.at[my_g], req_send.at[0], req_recv.at[0],
            device_id=device_at(g, my_w), device_id_type=MESH,
        ).start()
        return carry

    lax.fori_loop(1, far, ask, 0)
    pltpu.make_async_copy(req.at[my_g], passed.at[my_g], req_recv.at[0]).start()

    for s in range(steps):
        idx[s : s + 1, :] = places[s]
    idx_copy = pltpu.make_async_copy(idx, idx_s, small_sem.at[0])
    idx_copy.start()

    first, last = pl.ds(0, HALO), pl.ds(here - HALO, HALO)
    front, back = pl.ds(PAD - HALO, HALO), pl.ds(PAD + here, HALO)
    halos = []
    for a, (src, dst) in enumerate(((d_hbm, d0), (v_hbm, vel), (m_hbm, cm), (k_hbm, kq))):
        three = len(src.shape) == 3
        for side, (rows, place, to) in enumerate(((last, front, following), (first, back, previous))):
            copy = pltpu.make_async_remote_copy(
                src.at[:, rows] if three else src.at[rows],
                dst.at[:, place] if three else dst.at[place],
                halo_send.at[2 * a + side], halo_recv.at[2 * a + side],
                device_id=device(to), device_id_type=MESH,
            )
            copy.start()
            halos.append(copy)

    for copy in loads:
        copy.wait()

    def prepare(base, size):
        at = pl.ds(base, size)
        col = lax.broadcasted_iota(jnp.int32, (size, ncol), 1)
        kq[at, :] = jnp.where(col < ncol - 1, kq[at, :] * 0.25, 0.0)
        cm[at, :] = time_step / cm[at, :]

    def prepare_block(b, carry):
        prepare(pl.multiple_of(PAD + b * last_block, 8), last_block)
        return carry

    lax.fori_loop(0, here // last_block, prepare_block, 0)

    pltpu.make_async_copy(req, passed, req_recv.at[0]).wait()

    def hand_on(t, carry):
        w = other_member(t)
        pltpu.make_async_remote_copy(
            passed.at[:, w], asked.at[my_w], req_send.at[1], req_recv.at[1],
            device_id=device_at(my_g, w), device_id_type=MESH,
        ).start()
        return carry

    lax.fori_loop(1, near, hand_on, 0)
    pltpu.make_async_copy(passed.at[:, my_w], asked.at[my_w], req_recv.at[1]).start()

    for copy in halos:
        copy.wait()
    prepare(PAD - HALO, HALO)
    prepare(PAD + here, HALO)

    @pl.when(me == 0)
    def _():
        kq[front, :] = jnp.zeros((HALO, ncol), jnp.float32)

    @pl.when(me == n - 1)
    def _():
        tail = pl.ds(PAD + here - HALO, HALO)
        row = lax.broadcasted_iota(jnp.int32, (HALO, ncol), 0)
        kq[tail, :] = jnp.where(row == HALO - 1, 0.0, kq[tail, :])

    blocks = (here + 2 * HALO) // block
    assert blocks * block == here + 2 * HALO

    def weights(b, carry):
        base = pl.multiple_of(PAD - HALO + b * block, 8)
        both = kq[pl.ds(base, block), :] + kq[pl.ds(base - 1, block), :]
        w4[pl.ds(base, block), :] = 4.0 * (both + prev_col(both))
        return carry

    lax.fori_loop(0, blocks, weights, 0)

    pltpu.make_async_copy(asked, asked, req_recv.at[1]).wait()
    asked_rows[...] = asked[...].reshape(n, 128).T[:lists_rows]
    to_scalar = pltpu.make_async_copy(asked_rows, asked_s, small_sem.at[1])
    to_scalar.start()
    to_scalar.wait()
    idx_copy.wait()

    for axis, copies in enumerate((die_x, die_y, die_z)):
        others = copies.at[pl.ds(0, lines[axis] - 1)]
        pltpu.make_async_copy(others, others, die_recv.at[axis]).wait()

    def gather(axis, w, g, dst, at):
        copies = (die_x, die_y, die_z)[axis]
        for i in range(lines[axis] * cap):
            patch = jnp.clip(asked_s[firsts[axis] + i, w * far + g], 0, patches - 1)
            dst[at + i] = copies[i // cap, patch]

    def line_of(axis, y, x, w):
        return (y * near + w, x * near + w, (y * n_sub + x) * CORES + lax.rem(w, CORES))[axis]

    def planes_at(axis, y, x, w):
        return (axis * n + line_of(axis, y, x, w) * lines[axis]) * cap

    def reply(axis, y, x, w, wanted):
        g = y * n_sub + x

        @pl.when(wanted & ((g != my_g) | (w != my_w)))
        def _():
            size = lines[axis] * cap
            there, here_at = planes_at(axis, y, x, w), planes_at(axis, my_y, my_x, my_w)
            gather(axis, w, g, answer, there)
            pltpu.make_async_remote_copy(
                answer.at[pl.ds(there, size)], got.at[pl.ds(here_at, size)], ans_send, ans_recv,
                device_id=device_at(g, w), device_id_type=MESH,
            ).start()

    rounds = lines[0] * CORES
    assert lines[0] == lines[1]

    def in_round(i):
        return (i >= 0) & (i < rounds)

    def reply_round(r, carry):
        for layer in range(lines[2]):
            i = r - lead * layer
            at_y = lax.rem(my_y * CORES + my_core + 3 * (i + rounds), rounds)
            at_x = lax.rem(my_x * CORES + my_core + 3 * (i + rounds), rounds)
            w_y = layer * CORES + lax.rem(at_y, CORES)
            w_x = layer * CORES + lax.rem(at_x, CORES)
            reply(0, lax.div(at_y, CORES), my_x, w_y, in_round(i))
            reply(1, my_y, lax.div(at_x, CORES), w_x, in_round(i))
        i = r - lead * my_z
        for part in range(lines[0]):
            at = lax.rem(my_g * CORES + my_core + 13 * ((i + rounds) * lines[0] + part), far * CORES)
            g = lax.div(at, CORES)
            reply(2, lax.div(g, n_sub), lax.rem(g, n_sub), my_z * CORES + lax.rem(at, CORES), in_round(i))
        return carry

    assert lead * (lines[2] - 1) <= rounds
    lax.fori_loop(0, rounds + lead * (lines[2] - 1), reply_round, 0)
    for axis in range(3):
        gather(axis, my_w, my_g, got, planes_at(axis, my_y, my_x, my_w))

    def free_step(src, d_to, v_to, first_row, count, size):
        def part(b, carry):
            base = pl.multiple_of(first_row + b * size, 8)
            top_row = lax.broadcasted_iota(jnp.int32, (8, ncol), 0) == 0
            shifted = [None] * 3
            for i in range(size // 8 + 1):
                at = pl.ds(base + 8 * (i - 1), 8)
                below = pl.ds(base + 8 * (i - 1) + 1, 8)
                for c in range(3):
                    d = src[c, at, :]
                    box = d + src[c, below, :]
                    t = kq[at, :] * (box + next_col(box))
                    down = pltpu.roll(t, 1, 0)
                    if i:
                        t = t + jnp.where(top_row, shifted[c], down)
                        force = t + prev_col(t) - w4[at, :] * d
                        v = vel[c, at, :] + cm[at, :] * force
                        v_to(base, size)[c, 8 * (i - 1) : 8 * i, :] = v
                        d_to(base, size)[c, 8 * (i - 1) : 8 * i, :] = d + time_step * v
                    shifted[c] = down
            return carry

        lax.fori_loop(0, count, part, 0)

    def same_rows(ref):
        return lambda base, size: ref.at[:, pl.ds(base, size)]

    def own_rows(ref):
        return lambda base, size: ref.at[:, pl.ds(pl.multiple_of(base - PAD, 8), size)]

    free_step(d0, same_rows(d1), same_rows(vel), PAD - HALO, blocks, block)
    free_step(d1, same_rows(d2), same_rows(vel), PAD - HALO, blocks, block)
    free_step(d2, own_rows(od_ref), own_rows(ov_ref), PAD, here // last_block, last_block)

    wire = pl.ds(0, (3 * n - sum(lines)) * cap)
    pltpu.make_async_copy(answer.at[wire], got.at[wire], ans_recv).wait()

    for s in range(steps):
        first_patch[s] = got[idx_s[s, 0]]
    ghost_copy = pltpu.make_async_remote_copy(
        first_patch, ghost, ghost_sem.at[0], ghost_sem.at[1],
        device_id=device(previous), device_id_type=MESH,
    )
    ghost_copy.start()

    def place(j, carry):
        for s in range(steps):
            planes[s, pl.ds(j * 4, 4), :] = got[idx_s[s, j]]
        return carry

    lax.fori_loop(0, seg, place, 0, unroll=8)

    flat = {"cm": cm, "kq": kq, "w4": w4}
    deep = {"d0": d0, "d1": d1, "d2": d2}
    chunk = width * stride

    def correct(q, carry):
        base = PAD + q * chunk

        def rows(name, o):
            at = pl.ds(base + o, width, stride=stride)
            if name in flat:
                return flat[name][at, :]
            return [deep[name][c, at, :] for c in range(3)]

        nearby = [[planes[s, pl.ds(q * width * 4 + c, width, stride=4), :] for c in range(4)] for s in range(steps)]
        u, z = contact_response(nearby, rows)
        for c in range(3):
            for o in range(0, 3):
                at = pl.ds(q * chunk + o, width, stride=stride)
                od_ref[c, at, :] += u[o][c]
                ov_ref[c, at, :] += z[o][c]
            for o in (-2, -1):
                at = pl.ds(pl.multiple_of(q * width, 8), width)
                above_u[o + 2, c, at, :] = u[o][c]
                above_z[o + 2, c, at, :] = z[o][c]
        return carry

    lax.fori_loop(0, seg // width, correct, 0)

    ghost_copy.wait()

    def ghost_rows(name, o):
        at = pl.ds(PAD + here + o, 1)
        if name in flat:
            return flat[name][at, :]
        return [deep[name][c, at, :] for c in range(3)]

    nearby = [[ghost[s, pl.ds(c, 1), :] for c in range(4)] for s in range(steps)]
    u, z = contact_response(nearby, ghost_rows)
    for o in (-2, -1):
        for c in range(3):
            above_u[o + 2, c, pl.ds(seg, 1), :] = u[o][c]
            above_z[o + 2, c, pl.ds(seg, 1), :] = z[o][c]

    def correct_above(q, carry):
        for o in (-2, -1):
            at = pl.ds(q * chunk + stride + o, width, stride=stride)
            block_after = pl.ds(q * width + 1, width)
            for c in range(3):
                od_ref[c, at, :] += above_u[o + 2, c, block_after, :]
                ov_ref[c, at, :] += above_z[o + 2, c, block_after, :]
        return carry

    lax.fori_loop(0, seg // width, correct_above, 0)

    pltpu.make_async_copy(answer.at[wire], got.at[wire], ans_send).wait()
    for axis, copies in enumerate((die_x, die_y, die_z)):
        others = copies.at[pl.ds(0, lines[axis] - 1)]
        pltpu.make_async_copy(others, others, die_send.at[axis]).wait()
    pltpu.make_async_copy(req.at[pl.ds(0, far - 1)], passed.at[pl.ds(0, far - 1)], req_send.at[0]).wait()
    pltpu.make_async_copy(asked.at[pl.ds(0, near - 1)], asked.at[pl.ds(0, near - 1)], req_send.at[1]).wait()


def body(n_dom, n_sub, displace, velocity, nodal_mass, stiffness, die_planes, owners, pairs):
    n = n_dom * n_sub
    here, ncol = displace.shape[1:]
    steps, seg = pairs.shape
    cap = max(2, 2 * seg // n)
    ext = here + 2 * PAD
    tiles = (here + 2 * HALO) // 8
    block = 8 * max(b for b in range(1, 44) if tiles % b == 0)
    last_block = 8 * max(b for b in range(1, 33) if here // 8 % b == 0)
    width = min(32, seg)
    near = min(8, n_dom // 2)
    far = n // near
    lanes = (n_sub + far // n_sub + near // CORES) * cap
    f32, i32 = jnp.float32, jnp.int32
    any_spec = pl.BlockSpec(memory_space=pl.ANY)
    vmem_spec = pl.BlockSpec(memory_space=pltpu.VMEM)
    dma = pltpu.SemaphoreType.DMA
    return pl.pallas_call(
        functools.partial(kernel, n_dom, n_sub, cap, near, LEAD, block, last_block, width),
        out_shape=[pltpu.VMEM(displace.shape, f32)] * 2,
        in_specs=[any_spec] * 7,
        out_specs=[vmem_spec] * 2,
        scratch_shapes=[
            pltpu.VMEM((steps, 1, seg), i32),
            pltpu.VMEM((steps, seg), i32),
            pltpu.VMEM((3, ext, ncol), f32),
            pltpu.VMEM((3, ext, ncol), f32),
            pltpu.VMEM((3, ext, ncol), f32),
            pltpu.VMEM((3, ext, ncol), f32),
            pltpu.VMEM((ext, ncol), f32),
            pltpu.VMEM((ext, ncol), f32),
            pltpu.VMEM((ext, ncol), f32),
            pltpu.VMEM((n_sub,) + die_planes.shape[1:], f32),
            pltpu.VMEM((far // n_sub,) + die_planes.shape[1:], f32),
            pltpu.VMEM((near // CORES,) + die_planes.shape[1:], f32),
            pltpu.VMEM((far, near, 128), i32),
            pltpu.VMEM((far, near, 128), i32),
            pltpu.VMEM((near, far, 128), i32),
            pltpu.VMEM((-(-lanes // 8) * 8, n), i32),
            pltpu.SMEM((-(-lanes // 8) * 8, n), i32),
            pltpu.VMEM((8, seg), i32),
            pltpu.SMEM((8, seg), i32),
            pltpu.VMEM((n * steps * cap, 4, ncol), f32),
            pltpu.VMEM((n * steps * cap, 4, ncol), f32),
            pltpu.VMEM((steps, seg * 4 + 32, ncol), f32),
            pltpu.VMEM((steps, 4, ncol), f32),
            pltpu.VMEM((steps, 4, ncol), f32),
            pltpu.VMEM((2, 3, seg + 8, ncol), f32),
            pltpu.VMEM((2, 3, seg + 8, ncol), f32),
            dma((9,)), dma((8,)), dma((8,)), dma((3,)), dma((3,)), dma((2,)), dma((2,)), dma, dma, dma((2,)), dma((2,)),
        ],
        compiler_params=pltpu.CompilerParams(
            collective_id=0, has_side_effects=True, vmem_limit_bytes=40 * 1024 * 1024
        ),
        name="stamp",
    )(*[
        pltpu.with_memory_space_constraint(x, pltpu.HBM)
        for x in (jnp.swapaxes(owners, 1, 2), pairs, displace, velocity, nodal_mass, stiffness, die_planes)
    ])


def solution(mesh):
    in_specs = (
        P(None, ("dom", "sub"), None),
        P(None, ("dom", "sub"), None),
        P(("dom", "sub"), None),
        P(("dom", "sub"), None),
        P(None, ("dom", "sub"), None, None),
        P(None, ("dom", "sub"), None),
        P(None, ("dom", "sub")),
    )
    out_specs = (P(None, ("dom", "sub"), None), P(None, ("dom", "sub"), None))
    run = functools.partial(body, mesh.shape["dom"], mesh.shape["sub"])
    return jax.shard_map(run, mesh=mesh, in_specs=in_specs, out_specs=out_specs, check_vma=False)
```

```python
import functools

import jax
import jax.numpy as jnp
from jax import lax
from jax.experimental import pallas as pl
from jax.experimental.pallas import tpu as pltpu
from jax.sharding import PartitionSpec as P

STEPS = 3
time_step = 0.2
penalty = 1.0

MESH = pl.DeviceIdType.MESH
PAD = 16
HALO = 8
CORES = 2
LEAD = 1


def next_col(x):
    return pltpu.roll(x, x.shape[-1] - 1, x.ndim - 1)


def prev_col(x):
    return pltpu.roll(x, 1, x.ndim - 1)


def contact(planes, position):
    normal, height = planes[:3], planes[3]
    depth = height - (normal[0] * position[0] + normal[1] * position[1] + normal[2] * position[2])
    push = penalty * jnp.maximum(depth, 0.0)
    return [push * normal[c] for c in range(3)]


def contact_response(planes, rows):
    cm = {o: rows("cm", o) for o in range(-2, 3)}
    kq = {o: rows("kq", o) for o in range(-2, 2)}
    w4 = {o: rows("w4", o) for o in range(-1, 2)}
    u = {}
    z = {}
    for step in range(STEPS):
        free = rows("d%d" % step, 0)
        position = [free[c] + u[0][c] if step else free[c] for c in range(3)]
        push = contact(planes[step], position)
        new_u, new_z = {}, {}
        for o in range(-step, step + 1):
            new_u[o], new_z[o] = [], []
        for c in range(3):
            spread = {}
            for o in range(-step, step):
                parts = [u[r][c] for r in (o, o + 1) if r in u]
                box = parts[0] if len(parts) == 1 else parts[0] + parts[1]
                t = kq[o] * (box + next_col(box))
                spread[o] = t + prev_col(t)
            for o in range(-step, step + 1):
                terms = [spread[r] for r in (o - 1, o) if r in spread]
                if o in u:
                    terms.append(-(w4[o] * u[o][c]))
                if o == 0:
                    terms.append(push[c])
                force = terms[0]
                for term in terms[1:]:
                    force = force + term
                dz = cm[o] * force
                zc = z[o][c] + dz if o in z else dz
                uc = time_step * zc
                if o in u:
                    uc = u[o][c] + uc
                new_z[o].append(zc)
                new_u[o].append(uc)
        u, z = new_u, new_z
    return u, z


def kernel(
    n_dom, n_sub, cap, near, lead, block, last_block, width,
    own_hbm, pair_hbm, d_hbm, v_hbm, m_hbm, k_hbm, die_hbm,
    od_ref, ov_ref,
    own_ref, pair_ref, d0, d1, d2, vel, cm, kq, w4, die_x, die_y, die_z, req, passed, asked, asked_rows, asked_s, idx, idx_s, answer, got, planes, first_patch, ghost, above_u, above_z, term,
    load_sem, halo_send, halo_recv, die_send, die_recv, req_send, req_recv, ans_send, ans_recv, small_sem, ghost_sem,
):
    n = n_dom * n_sub
    steps, seg = pair_hbm.shape
    here = d_hbm.shape[1]
    stride = here // seg
    ncol = d_hbm.shape[2]
    assert steps == 3
    lists_rows = asked_s.shape[0]
    patches = die_hbm.shape[1]
    dom, sub = lax.axis_index("dom"), lax.axis_index("sub")
    me = dom * n_sub + sub

    def device(i):
        return (lax.div(i, n_sub), lax.rem(i, n_sub))

    far = n // near
    lines = (n_sub, far // n_sub, near // CORES)
    my_w = lax.rem(dom, near)
    my_x, my_y, my_z, my_core = sub, lax.div(dom, near), lax.div(my_w, CORES), lax.rem(my_w, CORES)
    my_g = my_y * n_sub + my_x

    def device_at(g, w):
        return (lax.div(g, n_sub) * near + w, lax.rem(g, n_sub))

    def other_group(t):
        return lax.rem(my_g + t, far)

    def other_member(t):
        return lax.rem(my_w + t, near)

    following, previous = lax.rem(me + 1, n), lax.rem(me + n - 1, n)

    inner = pl.ds(PAD, here)
    lists = [
        pltpu.make_async_copy(own_hbm, own_ref, load_sem.at[5]),
        pltpu.make_async_copy(pair_hbm, pair_ref, load_sem.at[6]),
    ]
    loads = [
        pltpu.make_async_copy(d_hbm, d0.at[:, inner], load_sem.at[0]),
        pltpu.make_async_copy(v_hbm, vel.at[:, inner], load_sem.at[1]),
        pltpu.make_async_copy(m_hbm, cm.at[inner], load_sem.at[2]),
        pltpu.make_async_copy(k_hbm, kq.at[inner], load_sem.at[3]),
        pltpu.make_async_copy(die_hbm.at[0], die_x.at[my_x], load_sem.at[4]),
        pltpu.make_async_copy(die_hbm.at[1], die_y.at[my_y], load_sem.at[7]),
        pltpu.make_async_copy(die_hbm.at[2], die_z.at[0], load_sem.at[8]),
    ]
    for copy in lists + loads:
        copy.start()

    barrier = pltpu.get_barrier_semaphore()

    def greet(to):
        pl.semaphore_signal(barrier, inc=1, device_id=to, device_id_type=MESH)

    def greet_groups(t, carry):
        greet(device_at(other_group(t), my_w))
        return carry

    def greet_members(t, carry):
        greet(device_at(my_g, other_member(t)))
        return carry

    lax.fori_loop(1, far, greet_groups, 0)
    lax.fori_loop(1, near, greet_members, 0)
    greet(device(following))
    greet(device(previous))

    pl.semaphore_wait(barrier, far + near)

    for axis, (count, mine, copies) in enumerate(zip(lines, (my_x, my_y, my_z), (die_x, die_y, die_z))):
        for t in range(1, count):
            there = lax.rem(mine + t, count)
            to = (
                device_at(my_y * n_sub + there, my_w),
                device_at(there * n_sub + my_x, my_w),
                device_at(my_g, there * CORES + my_core),
            )[axis]
            pltpu.make_async_remote_copy(
                die_hbm.at[axis], copies.at[count - t if axis == 2 else mine],
                die_send.at[axis], die_recv.at[axis], device_id=to, device_id_type=MESH,
            ).start()

    lane_of = lax.broadcasted_iota(jnp.int32, (n, 128), 1)
    row = lax.broadcasted_iota(jnp.int32, (n, seg), 0)
    row_g, row_w = lax.div(row, near), lax.rem(row, near)
    owner_of = (lax.div(row_g, n_sub) * near + row_w) * n_sub + lax.rem(row_g, n_sub)
    before = lax.broadcasted_iota(jnp.int32, (seg, seg), 0) < lax.broadcasted_iota(jnp.int32, (seg, seg), 1)
    table = jnp.zeros((n, 128), jnp.int32)
    places = []
    for copy in lists:
        copy.wait()
    for s in range(steps):
        own = own_ref[s]
        wide = jnp.broadcast_to(own, (seg, seg))
        same = (wide == wide.T) & before
        slot = jnp.minimum(jnp.sum(same.astype(jnp.int32), axis=0, keepdims=True), cap - 1)
        own_dom, own_x = lax.div(own, n_sub), lax.rem(own, n_sub)
        own_y, own_w = lax.div(own_dom, near), lax.rem(own_dom, near)
        own_z, own_core = lax.div(own_w, CORES), lax.rem(own_w, CORES)
        line, at_line = (
            (own_y * near + own_w, own_x),
            (own_x * near + own_w, own_y),
            ((own_y * n_sub + own_x) * CORES + own_core, lax.rem(own_z + (lines[2] - my_z), lines[2])),
        )[s]
        places.append((s * n + line * lines[s] + at_line) * cap + slot)
        pair = pair_ref[s : s + 1, :]
        mine = owner_of == own
        for k in range(cap):
            chosen = jnp.where(mine & (slot == k), pair, 0)
            table = jnp.where(lane_of == s * cap + k, jnp.sum(chosen, axis=1, keepdims=True), table)
    by_group = [table[near * g : near * (g + 1)] for g in range(far)]
    lane = lax.broadcasted_iota(jnp.int32, (near, 128), 1)

    def lanes_of(s, value, to):
        value = jnp.where((lane >= s * cap) & (lane < (s + 1) * cap), value, 0)
        shift = to - s * cap
        return pltpu.roll(value, shift, 1) if shift else value

    firsts = (0, lines[0] * cap, (lines[0] + lines[1]) * cap)
    along_x = [
        sum(lanes_of(0, by_group[y * n_sub + x], firsts[0] + x * cap) for x in range(lines[0])) for y in range(lines[1])
    ]
    along_y = [
        sum(lanes_of(1, by_group[y * n_sub + x], firsts[1] + y * cap) for y in range(lines[1])) for x in range(lines[0])
    ]
    for g in range(far):
        along_z = 0
        for z in range(lines[2]):
            turned = pltpu.roll(by_group[g], near - z * CORES, 0) if z else by_group[g]
            along_z = along_z + lanes_of(2, turned, firsts[2] + z * cap)
        req[g] = along_x[g // n_sub] + along_y[g % n_sub] + along_z
    def ask(t, carry):
        g = other_group(t)
        pltpu.make_async_remote_copy(
            req.at[g], passed.at[my_g], req_send.at[0], req_recv.at[0],
            device_id=device_at(g, my_w), device_id_type=MESH,
        ).start()
        return carry

    lax.fori_loop(1, far, ask, 0)
    pltpu.make_async_copy(req.at[my_g], passed.at[my_g], req_recv.at[0]).start()

    for s in range(steps):
        idx[s : s + 1, :] = places[s]
    idx_copy = pltpu.make_async_copy(idx, idx_s, small_sem.at[0])
    idx_copy.start()

    first, last = pl.ds(0, HALO), pl.ds(here - HALO, HALO)
    front, back = pl.ds(PAD - HALO, HALO), pl.ds(PAD + here, HALO)
    halos = []
    for a, (src, dst) in enumerate(((d_hbm, d0), (v_hbm, vel), (m_hbm, cm), (k_hbm, kq))):
        three = len(src.shape) == 3
        for side, (rows, place, to) in enumerate(((last, front, following), (first, back, previous))):
            copy = pltpu.make_async_remote_copy(
                src.at[:, rows] if three else src.at[rows],
                dst.at[:, place] if three else dst.at[place],
                halo_send.at[2 * a + side], halo_recv.at[2 * a + side],
                device_id=device(to), device_id_type=MESH,
            )
            copy.start()
            halos.append(copy)

    for copy in loads:
        copy.wait()

    def prepare(base, size):
        at = pl.ds(base, size)
        col = lax.broadcasted_iota(jnp.int32, (size, ncol), 1)
        kq[at, :] = jnp.where(col < ncol - 1, kq[at, :] * 0.25, 0.0)
        cm[at, :] = time_step / cm[at, :]

    def prepare_block(b, carry):
        prepare(pl.multiple_of(PAD + b * last_block, 8), last_block)
        return carry

    lax.fori_loop(0, here // last_block, prepare_block, 0)

    pltpu.make_async_copy(req, passed, req_recv.at[0]).wait()

    def hand_on(t, carry):
        w = other_member(t)
        pltpu.make_async_remote_copy(
            passed.at[:, w], asked.at[my_w], req_send.at[1], req_recv.at[1],
            device_id=device_at(my_g, w), device_id_type=MESH,
        ).start()
        return carry

    lax.fori_loop(1, near, hand_on, 0)
    pltpu.make_async_copy(passed.at[:, my_w], asked.at[my_w], req_recv.at[1]).start()

    for copy in halos:
        copy.wait()
    prepare(PAD - HALO, HALO)
    prepare(PAD + here, HALO)

    @pl.when(me == 0)
    def _():
        kq[front, :] = jnp.zeros((HALO, ncol), jnp.float32)

    @pl.when(me == n - 1)
    def _():
        tail = pl.ds(PAD + here - HALO, HALO)
        row = lax.broadcasted_iota(jnp.int32, (HALO, ncol), 0)
        kq[tail, :] = jnp.where(row == HALO - 1, 0.0, kq[tail, :])

    blocks = (here + 2 * HALO) // block
    assert blocks * block == here + 2 * HALO

    def weights(b, carry):
        base = pl.multiple_of(PAD - HALO + b * block, 8)
        both = kq[pl.ds(base, block), :] + kq[pl.ds(base - 1, block), :]
        w4[pl.ds(base, block), :] = 4.0 * (both + prev_col(both))
        return carry

    lax.fori_loop(0, blocks, weights, 0)

    def free_step(src, d_to, v_to, first_row, count, size):
        def part(b, carry):
            base = pl.multiple_of(first_row + b * size, 8)
            for i in range(size // 8 + 1):
                at = pl.ds(base + 8 * (i - 1), 8)
                below = pl.ds(base + 8 * (i - 1) + 1, 8)
                for c in range(3):
                    d = src[c, at, :]
                    box = d + src[c, below, :]
                    t = kq[at, :] * (box + next_col(box))
                    term[c, 8 * i : 8 * (i + 1), :] = t
                    if i:
                        t = t + term[c, 8 * i - 1 : 8 * i + 7, :]
                        force = t + prev_col(t) - w4[at, :] * d
                        v = vel[c, at, :] + cm[at, :] * force
                        v_to(base, size)[c, 8 * (i - 1) : 8 * i, :] = v
                        d_to(base, size)[c, 8 * (i - 1) : 8 * i, :] = d + time_step * v
            return carry

        lax.fori_loop(0, count, part, 0)

    def same_rows(ref):
        return lambda base, size: ref.at[:, pl.ds(base, size)]

    def own_rows(ref):
        return lambda base, size: ref.at[:, pl.ds(pl.multiple_of(base - PAD, 8), size)]

    free_step(d0, same_rows(d1), same_rows(vel), PAD - HALO, blocks, block)

    pltpu.make_async_copy(asked, asked, req_recv.at[1]).wait()
    asked_rows[...] = jnp.clip(asked[...].reshape(n, 128).T[:lists_rows], 0, patches - 1)
    to_scalar = pltpu.make_async_copy(asked_rows, asked_s, small_sem.at[1])
    to_scalar.start()
    to_scalar.wait()
    idx_copy.wait()

    for axis, copies in enumerate((die_x, die_y, die_z)):
        others = copies.at[pl.ds(0, lines[axis] - 1)]
        pltpu.make_async_copy(others, others, die_recv.at[axis]).wait()

    def gather(axis, w, g, dst, at):
        copies = (die_x, die_y, die_z)[axis]
        for i in range(lines[axis] * cap):
            dst[at + i] = copies[i // cap, asked_s[firsts[axis] + i, w * far + g]]

    def line_of(axis, y, x, w):
        return (y * near + w, x * near + w, (y * n_sub + x) * CORES + lax.rem(w, CORES))[axis]

    def planes_at(axis, y, x, w):
        return (axis * n + line_of(axis, y, x, w) * lines[axis]) * cap

    def reply(axis, y, x, w, wanted):
        g = y * n_sub + x

        @pl.when(wanted & ((g != my_g) | (w != my_w)))
        def _():
            size = lines[axis] * cap
            there, here_at = planes_at(axis, y, x, w), planes_at(axis, my_y, my_x, my_w)
            gather(axis, w, g, answer, there)
            pltpu.make_async_remote_copy(
                answer.at[pl.ds(there, size)], got.at[pl.ds(here_at, size)], ans_send, ans_recv,
                device_id=device_at(g, w), device_id_type=MESH,
            ).start()

    rounds = lines[0] * CORES
    assert lines[0] == lines[1]

    def in_round(i):
        return (i >= 0) & (i < rounds)

    def reply_round(r, carry):
        for layer in range(lines[2]):
            i = r - lead * layer
            at_y = lax.rem(my_y * CORES + my_core + 3 * (i + rounds), rounds)
            at_x = lax.rem(my_x * CORES + my_core + 3 * (i + rounds), rounds)
            w_y = layer * CORES + lax.rem(at_y, CORES)
            w_x = layer * CORES + lax.rem(at_x, CORES)
            reply(0, lax.div(at_y, CORES), my_x, w_y, in_round(i))
            reply(1, my_y, lax.div(at_x, CORES), w_x, in_round(i))
        i = r - lead * my_z
        for part in range(lines[0]):
            at = lax.rem(my_g * CORES + my_core + 13 * ((i + rounds) * lines[0] + part), far * CORES)
            g = lax.div(at, CORES)
            reply(2, lax.div(g, n_sub), lax.rem(g, n_sub), my_z * CORES + lax.rem(at, CORES), in_round(i))
        return carry

    assert lead * (lines[2] - 1) <= rounds
    lax.fori_loop(0, rounds + lead * (lines[2] - 1), reply_round, 0)
    for axis in range(3):
        gather(axis, my_w, my_g, got, planes_at(axis, my_y, my_x, my_w))

    free_step(d1, same_rows(d2), same_rows(vel), PAD - HALO, blocks, block)
    free_step(d2, own_rows(od_ref), own_rows(ov_ref), PAD, here // last_block, last_block)

    wire = pl.ds(0, (3 * n - sum(lines)) * cap)
    pltpu.make_async_copy(answer.at[wire], got.at[wire], ans_recv).wait()

    for s in range(steps):
        first_patch[s] = got[idx_s[s, 0]]
    ghost_copy = pltpu.make_async_remote_copy(
        first_patch, ghost, ghost_sem.at[0], ghost_sem.at[1],
        device_id=device(previous), device_id_type=MESH,
    )
    ghost_copy.start()

    def place(j, carry):
        for s in range(steps):
            planes[s, pl.ds(j * 4, 4), :] = got[idx_s[s, j]]
        return carry

    lax.fori_loop(0, seg, place, 0, unroll=8)

    flat = {"cm": cm, "kq": kq, "w4": w4}
    deep = {"d0": d0, "d1": d1, "d2": d2}
    chunk = width * stride

    def correct(q, carry):
        base = PAD + q * chunk

        def rows(name, o):
            at = pl.ds(base + o, width, stride=stride)
            if name in flat:
                return flat[name][at, :]
            return [deep[name][c, at, :] for c in range(3)]

        nearby = [[planes[s, pl.ds(q * width * 4 + c, width, stride=4), :] for c in range(4)] for s in range(steps)]
        u, z = contact_response(nearby, rows)
        for c in range(3):
            for o in range(0, 3):
                at = pl.ds(q * chunk + o, width, stride=stride)
                od_ref[c, at, :] += u[o][c]
                ov_ref[c, at, :] += z[o][c]
            for o in (-2, -1):
                at = pl.ds(pl.multiple_of(q * width, 8), width)
                above_u[o + 2, c, at, :] = u[o][c]
                above_z[o + 2, c, at, :] = z[o][c]
        return carry

    lax.fori_loop(0, seg // width, correct, 0)

    ghost_copy.wait()

    def ghost_rows(name, o):
        at = pl.ds(PAD + here + o, 1)
        if name in flat:
            return flat[name][at, :]
        return [deep[name][c, at, :] for c in range(3)]

    nearby = [[ghost[s, pl.ds(c, 1), :] for c in range(4)] for s in range(steps)]
    u, z = contact_response(nearby, ghost_rows)
    for o in (-2, -1):
        for c in range(3):
            above_u[o + 2, c, pl.ds(seg, 1), :] = u[o][c]
            above_z[o + 2, c, pl.ds(seg, 1), :] = z[o][c]

    def correct_above(q, carry):
        for o in (-2, -1):
            at = pl.ds(q * chunk + stride + o, width, stride=stride)
            block_after = pl.ds(q * width + 1, width)
            for c in range(3):
                od_ref[c, at, :] += above_u[o + 2, c, block_after, :]
                ov_ref[c, at, :] += above_z[o + 2, c, block_after, :]
        return carry

    lax.fori_loop(0, seg // width, correct_above, 0)

    pltpu.make_async_copy(answer.at[wire], got.at[wire], ans_send).wait()
    for axis, copies in enumerate((die_x, die_y, die_z)):
        others = copies.at[pl.ds(0, lines[axis] - 1)]
        pltpu.make_async_copy(others, others, die_send.at[axis]).wait()
    pltpu.make_async_copy(req.at[pl.ds(0, far - 1)], passed.at[pl.ds(0, far - 1)], req_send.at[0]).wait()
    pltpu.make_async_copy(asked.at[pl.ds(0, near - 1)], asked.at[pl.ds(0, near - 1)], req_send.at[1]).wait()


def body(n_dom, n_sub, displace, velocity, nodal_mass, stiffness, die_planes, owners, pairs):
    n = n_dom * n_sub
    here, ncol = displace.shape[1:]
    steps, seg = pairs.shape
    cap = max(2, 2 * seg // n)
    ext = here + 2 * PAD
    tiles = (here + 2 * HALO) // 8
    block = 8 * max(b for b in range(1, 44) if tiles % b == 0)
    last_block = 8 * max(b for b in range(1, 33) if here // 8 % b == 0)
    width = min(32, seg)
    near = min(8, n_dom // 2)
    far = n // near
    lanes = (n_sub + far // n_sub + near // CORES) * cap
    f32, i32 = jnp.float32, jnp.int32
    any_spec = pl.BlockSpec(memory_space=pl.ANY)
    vmem_spec = pl.BlockSpec(memory_space=pltpu.VMEM)
    dma = pltpu.SemaphoreType.DMA
    return pl.pallas_call(
        functools.partial(kernel, n_dom, n_sub, cap, near, LEAD, block, last_block, width),
        out_shape=[pltpu.VMEM(displace.shape, f32)] * 2,
        in_specs=[any_spec] * 7,
        out_specs=[vmem_spec] * 2,
        scratch_shapes=[
            pltpu.VMEM((steps, 1, seg), i32),
            pltpu.VMEM((steps, seg), i32),
            pltpu.VMEM((3, ext, ncol), f32),
            pltpu.VMEM((3, ext, ncol), f32),
            pltpu.VMEM((3, ext, ncol), f32),
            pltpu.VMEM((3, ext, ncol), f32),
            pltpu.VMEM((ext, ncol), f32),
            pltpu.VMEM((ext, ncol), f32),
            pltpu.VMEM((ext, ncol), f32),
            pltpu.VMEM((n_sub,) + die_planes.shape[1:], f32),
            pltpu.VMEM((far // n_sub,) + die_planes.shape[1:], f32),
            pltpu.VMEM((near // CORES,) + die_planes.shape[1:], f32),
            pltpu.VMEM((far, near, 128), i32),
            pltpu.VMEM((far, near, 128), i32),
            pltpu.VMEM((near, far, 128), i32),
            pltpu.VMEM((-(-lanes // 8) * 8, n), i32),
            pltpu.SMEM((-(-lanes // 8) * 8, n), i32),
            pltpu.VMEM((8, seg), i32),
            pltpu.SMEM((8, seg), i32),
            pltpu.VMEM((n * steps * cap, 4, ncol), f32),
            pltpu.VMEM((n * steps * cap, 4, ncol), f32),
            pltpu.VMEM((steps, seg * 4 + 32, ncol), f32),
            pltpu.VMEM((steps, 4, ncol), f32),
            pltpu.VMEM((steps, 4, ncol), f32),
            pltpu.VMEM((2, 3, seg + 8, ncol), f32),
            pltpu.VMEM((2, 3, seg + 8, ncol), f32),
            pltpu.VMEM((3, max(block, last_block) + 8, ncol), f32),
            dma((9,)), dma((8,)), dma((8,)), dma((3,)), dma((3,)), dma((2,)), dma((2,)), dma, dma, dma((2,)), dma((2,)),
        ],
        compiler_params=pltpu.CompilerParams(
            collective_id=0, has_side_effects=True, vmem_limit_bytes=40 * 1024 * 1024
        ),
        name="stamp",
    )(*[
        pltpu.with_memory_space_constraint(x, pltpu.HBM)
        for x in (jnp.swapaxes(owners, 1, 2), pairs, displace, velocity, nodal_mass, stiffness, die_planes)
    ])


def solution(mesh):
    in_specs = (
        P(None, ("dom", "sub"), None),
        P(None, ("dom", "sub"), None),
        P(("dom", "sub"), None),
        P(("dom", "sub"), None),
        P(None, ("dom", "sub"), None, None),
        P(None, ("dom", "sub"), None),
        P(None, ("dom", "sub")),
    )
    out_specs = (P(None, ("dom", "sub"), None), P(None, ("dom", "sub"), None))
    run = functools.partial(body, mesh.shape["dom"], mesh.shape["sub"])
    return jax.shard_map(run, mesh=mesh, in_specs=in_specs, out_specs=out_specs, check_vma=False)
```

```python
import functools

import jax
import jax.numpy as jnp
from jax import lax
from jax.experimental import pallas as pl
from jax.experimental.pallas import tpu as pltpu
from jax.sharding import PartitionSpec as P

STEPS = 3
time_step = 0.2
penalty = 1.0

MESH = pl.DeviceIdType.MESH
PAD = 16
HALO = 8
CORES = 2
LEAD = 1


def next_col(x):
    return pltpu.roll(x, x.shape[-1] - 1, x.ndim - 1)


def prev_col(x):
    return pltpu.roll(x, 1, x.ndim - 1)


def contact(planes, position):
    normal, height = planes[:3], planes[3]
    depth = height - (normal[0] * position[0] + normal[1] * position[1] + normal[2] * position[2])
    push = penalty * jnp.maximum(depth, 0.0)
    return [push * normal[c] for c in range(3)]


def contact_response(planes, rows):
    cm = {o: rows("cm", o) for o in range(-2, 3)}
    kq = {o: rows("kq", o) for o in range(-2, 2)}
    w4 = {o: rows("w4", o) for o in range(-1, 2)}
    u = {}
    z = {}
    for step in range(STEPS):
        free = rows("d%d" % step, 0)
        position = [free[c] + u[0][c] if step else free[c] for c in range(3)]
        push = contact(planes[step], position)
        new_u, new_z = {}, {}
        for o in range(-step, step + 1):
            new_u[o], new_z[o] = [], []
        for c in range(3):
            spread = {}
            for o in range(-step, step):
                parts = [u[r][c] for r in (o, o + 1) if r in u]
                box = parts[0] if len(parts) == 1 else parts[0] + parts[1]
                t = kq[o] * (box + next_col(box))
                spread[o] = t + prev_col(t)
            for o in range(-step, step + 1):
                terms = [spread[r] for r in (o - 1, o) if r in spread]
                if o in u:
                    terms.append(-(w4[o] * u[o][c]))
                if o == 0:
                    terms.append(push[c])
                force = terms[0]
                for term in terms[1:]:
                    force = force + term
                dz = cm[o] * force
                zc = z[o][c] + dz if o in z else dz
                uc = time_step * zc
                if o in u:
                    uc = u[o][c] + uc
                new_z[o].append(zc)
                new_u[o].append(uc)
        u, z = new_u, new_z
    return u, z


def kernel(
    n_dom, n_sub, cap, near, lead, block, last_block, width,
    own_hbm, pair_hbm, d_hbm, v_hbm, m_hbm, k_hbm, die_hbm,
    od_ref, ov_ref, share_u, share_z,
    own_ref, pair_ref, d0, d1, d2, vel, cm, kq, w4, die_x, die_y, die_z, req, passed, asked, asked_rows, asked_s, idx, idx_s, answer, got, planes, first_patch, ghost, term,
    load_sem, halo_send, halo_recv, die_send, die_recv, req_send, req_recv, ans_send, ans_recv, small_sem, ghost_sem,
):
    n = n_dom * n_sub
    steps, seg = pair_hbm.shape
    here = d_hbm.shape[1]
    stride = here // seg
    ncol = d_hbm.shape[2]
    assert steps == 3
    lists_rows = asked_s.shape[0]
    patches = die_hbm.shape[1]
    dom, sub = lax.axis_index("dom"), lax.axis_index("sub")
    me = dom * n_sub + sub

    def device(i):
        return (lax.div(i, n_sub), lax.rem(i, n_sub))

    far = n // near
    lines = (n_sub, far // n_sub, near // CORES)
    my_w = lax.rem(dom, near)
    my_x, my_y, my_z, my_core = sub, lax.div(dom, near), lax.div(my_w, CORES), lax.rem(my_w, CORES)
    my_g = my_y * n_sub + my_x

    def device_at(g, w):
        return (lax.div(g, n_sub) * near + w, lax.rem(g, n_sub))

    def other_group(t):
        return lax.rem(my_g + t, far)

    def other_member(t):
        return lax.rem(my_w + t, near)

    following, previous = lax.rem(me + 1, n), lax.rem(me + n - 1, n)

    inner = pl.ds(PAD, here)
    lists = [
        pltpu.make_async_copy(own_hbm, own_ref, load_sem.at[5]),
        pltpu.make_async_copy(pair_hbm, pair_ref, load_sem.at[6]),
    ]
    loads = [
        pltpu.make_async_copy(d_hbm, d0.at[:, inner], load_sem.at[0]),
        pltpu.make_async_copy(v_hbm, vel.at[:, inner], load_sem.at[1]),
        pltpu.make_async_copy(m_hbm, cm.at[inner], load_sem.at[2]),
        pltpu.make_async_copy(k_hbm, kq.at[inner], load_sem.at[3]),
        pltpu.make_async_copy(die_hbm.at[0], die_x.at[my_x], load_sem.at[4]),
        pltpu.make_async_copy(die_hbm.at[1], die_y.at[my_y], load_sem.at[7]),
        pltpu.make_async_copy(die_hbm.at[2], die_z.at[0], load_sem.at[8]),
    ]
    for copy in lists + loads:
        copy.start()

    barrier = pltpu.get_barrier_semaphore()

    def greet(to):
        pl.semaphore_signal(barrier, inc=1, device_id=to, device_id_type=MESH)

    def greet_groups(t, carry):
        greet(device_at(other_group(t), my_w))
        return carry

    def greet_members(t, carry):
        greet(device_at(my_g, other_member(t)))
        return carry

    lax.fori_loop(1, far, greet_groups, 0)
    lax.fori_loop(1, near, greet_members, 0)
    greet(device(following))
    greet(device(previous))

    pl.semaphore_wait(barrier, far + near)

    for axis, (count, mine, copies) in enumerate(zip(lines, (my_x, my_y, my_z), (die_x, die_y, die_z))):
        for t in range(1, count):
            there = lax.rem(mine + t, count)
            to = (
                device_at(my_y * n_sub + there, my_w),
                device_at(there * n_sub + my_x, my_w),
                device_at(my_g, there * CORES + my_core),
            )[axis]
            pltpu.make_async_remote_copy(
                die_hbm.at[axis], copies.at[count - t if axis == 2 else mine],
                die_send.at[axis], die_recv.at[axis], device_id=to, device_id_type=MESH,
            ).start()

    lane_of = lax.broadcasted_iota(jnp.int32, (n, 128), 1)
    row = lax.broadcasted_iota(jnp.int32, (n, seg), 0)
    row_g, row_w = lax.div(row, near), lax.rem(row, near)
    owner_of = (lax.div(row_g, n_sub) * near + row_w) * n_sub + lax.rem(row_g, n_sub)
    before = lax.broadcasted_iota(jnp.int32, (seg, seg), 0) < lax.broadcasted_iota(jnp.int32, (seg, seg), 1)
    table = jnp.zeros((n, 128), jnp.int32)
    places = []
    for copy in lists:
        copy.wait()
    for s in range(steps):
        own = own_ref[s]
        wide = jnp.broadcast_to(own, (seg, seg))
        same = (wide == wide.T) & before
        slot = jnp.minimum(jnp.sum(same.astype(jnp.int32), axis=0, keepdims=True), cap - 1)
        own_dom, own_x = lax.div(own, n_sub), lax.rem(own, n_sub)
        own_y, own_w = lax.div(own_dom, near), lax.rem(own_dom, near)
        own_z, own_core = lax.div(own_w, CORES), lax.rem(own_w, CORES)
        line, at_line = (
            (own_y * near + own_w, own_x),
            (own_x * near + own_w, own_y),
            ((own_y * n_sub + own_x) * CORES + own_core, lax.rem(own_z + (lines[2] - my_z), lines[2])),
        )[s]
        places.append((s * n + line * lines[s] + at_line) * cap + slot)
        pair = pair_ref[s : s + 1, :]
        mine = owner_of == own
        for k in range(cap):
            chosen = jnp.where(mine & (slot == k), pair, 0)
            table = jnp.where(lane_of == s * cap + k, jnp.sum(chosen, axis=1, keepdims=True), table)
    by_group = [table[near * g : near * (g + 1)] for g in range(far)]
    lane = lax.broadcasted_iota(jnp.int32, (near, 128), 1)

    def lanes_of(s, value, to):
        value = jnp.where((lane >= s * cap) & (lane < (s + 1) * cap), value, 0)
        shift = to - s * cap
        return pltpu.roll(value, shift, 1) if shift else value

    firsts = (0, lines[0] * cap, (lines[0] + lines[1]) * cap)
    along_x = [
        sum(lanes_of(0, by_group[y * n_sub + x], firsts[0] + x * cap) for x in range(lines[0])) for y in range(lines[1])
    ]
    along_y = [
        sum(lanes_of(1, by_group[y * n_sub + x], firsts[1] + y * cap) for y in range(lines[1])) for x in range(lines[0])
    ]
    for g in range(far):
        along_z = 0
        for z in range(lines[2]):
            turned = pltpu.roll(by_group[g], near - z * CORES, 0) if z else by_group[g]
            along_z = along_z + lanes_of(2, turned, firsts[2] + z * cap)
        req[g] = along_x[g // n_sub] + along_y[g % n_sub] + along_z
    def ask(t, carry):
        g = other_group(t)
        pltpu.make_async_remote_copy(
            req.at[g], passed.at[my_g], req_send.at[0], req_recv.at[0],
            device_id=device_at(g, my_w), device_id_type=MESH,
        ).start()
        return carry

    lax.fori_loop(1, far, ask, 0)
    pltpu.make_async_copy(req.at[my_g], passed.at[my_g], req_recv.at[0]).start()

    for s in range(steps):
        idx[s : s + 1, :] = places[s]
    idx_copy = pltpu.make_async_copy(idx, idx_s, small_sem.at[0])
    idx_copy.start()

    first, last = pl.ds(0, HALO), pl.ds(here - HALO, HALO)
    front, back = pl.ds(PAD - HALO, HALO), pl.ds(PAD + here, HALO)
    halos = []
    for a, (src, dst) in enumerate(((d_hbm, d0), (v_hbm, vel), (m_hbm, cm), (k_hbm, kq))):
        three = len(src.shape) == 3
        for side, (rows, place, to) in enumerate(((last, front, following), (first, back, previous))):
            copy = pltpu.make_async_remote_copy(
                src.at[:, rows] if three else src.at[rows],
                dst.at[:, place] if three else dst.at[place],
                halo_send.at[2 * a + side], halo_recv.at[2 * a + side],
                device_id=device(to), device_id_type=MESH,
            )
            copy.start()
            halos.append(copy)

    for copy in loads:
        copy.wait()

    def prepare(base, size):
        at = pl.ds(base, size)
        col = lax.broadcasted_iota(jnp.int32, (size, ncol), 1)
        kq[at, :] = jnp.where(col < ncol - 1, kq[at, :] * 0.25, 0.0)
        cm[at, :] = time_step / cm[at, :]

    def prepare_block(b, carry):
        prepare(pl.multiple_of(PAD + b * last_block, 8), last_block)
        return carry

    lax.fori_loop(0, here // last_block, prepare_block, 0)

    pltpu.make_async_copy(req, passed, req_recv.at[0]).wait()

    def hand_on(t, carry):
        w = other_member(t)
        pltpu.make_async_remote_copy(
            passed.at[:, w], asked.at[my_w], req_send.at[1], req_recv.at[1],
            device_id=device_at(my_g, w), device_id_type=MESH,
        ).start()
        return carry

    lax.fori_loop(1, near, hand_on, 0)
    pltpu.make_async_copy(passed.at[:, my_w], asked.at[my_w], req_recv.at[1]).start()

    for copy in halos:
        copy.wait()
    prepare(PAD - HALO, HALO)
    prepare(PAD + here, HALO)

    @pl.when(me == 0)
    def _():
        kq[front, :] = jnp.zeros((HALO, ncol), jnp.float32)

    @pl.when(me == n - 1)
    def _():
        tail = pl.ds(PAD + here - HALO, HALO)
        row = lax.broadcasted_iota(jnp.int32, (HALO, ncol), 0)
        kq[tail, :] = jnp.where(row == HALO - 1, 0.0, kq[tail, :])

    blocks = (here + 2 * HALO) // block
    assert blocks * block == here + 2 * HALO

    def weights(b, carry):
        base = pl.multiple_of(PAD - HALO + b * block, 8)
        both = kq[pl.ds(base, block), :] + kq[pl.ds(base - 1, block), :]
        w4[pl.ds(base, block), :] = 4.0 * (both + prev_col(both))
        return carry

    lax.fori_loop(0, blocks, weights, 0)

    def free_step(src, d_to, v_to, first_row, count, size):
        def part(b, carry):
            base = pl.multiple_of(first_row + b * size, 8)
            for i in range(size // 8 + 1):
                at = pl.ds(base + 8 * (i - 1), 8)
                below = pl.ds(base + 8 * (i - 1) + 1, 8)
                for c in range(3):
                    d = src[c, at, :]
                    box = d + src[c, below, :]
                    t = kq[at, :] * (box + next_col(box))
                    term[c, 8 * i : 8 * (i + 1), :] = t
                    if i:
                        t = t + term[c, 8 * i - 1 : 8 * i + 7, :]
                        force = t + prev_col(t) - w4[at, :] * d
                        v = vel[c, at, :] + cm[at, :] * force
                        v_to(base, size)[c, 8 * (i - 1) : 8 * i, :] = v
                        d_to(base, size)[c, 8 * (i - 1) : 8 * i, :] = d + time_step * v
            return carry

        lax.fori_loop(0, count, part, 0)

    def same_rows(ref):
        return lambda base, size: ref.at[:, pl.ds(base, size)]

    def own_rows(ref):
        return lambda base, size: ref.at[:, pl.ds(pl.multiple_of(base - PAD, 8), size)]

    free_step(d0, same_rows(d1), same_rows(vel), PAD - HALO, blocks, block)

    pltpu.make_async_copy(asked, asked, req_recv.at[1]).wait()
    asked_rows[...] = jnp.clip(asked[...].reshape(n, 128).T[:lists_rows], 0, patches - 1)
    to_scalar = pltpu.make_async_copy(asked_rows, asked_s, small_sem.at[1])
    to_scalar.start()
    to_scalar.wait()
    idx_copy.wait()

    for axis, copies in enumerate((die_x, die_y, die_z)):
        others = copies.at[pl.ds(0, lines[axis] - 1)]
        pltpu.make_async_copy(others, others, die_recv.at[axis]).wait()

    def gather(axis, w, g, dst, at):
        copies = (die_x, die_y, die_z)[axis]
        for i in range(lines[axis] * cap):
            dst[at + i] = copies[i // cap, asked_s[firsts[axis] + i, w * far + g]]

    def line_of(axis, y, x, w):
        return (y * near + w, x * near + w, (y * n_sub + x) * CORES + lax.rem(w, CORES))[axis]

    def planes_at(axis, y, x, w):
        return (axis * n + line_of(axis, y, x, w) * lines[axis]) * cap

    def reply(axis, y, x, w, wanted):
        g = y * n_sub + x

        @pl.when(wanted & ((g != my_g) | (w != my_w)))
        def _():
            size = lines[axis] * cap
            there, here_at = planes_at(axis, y, x, w), planes_at(axis, my_y, my_x, my_w)
            gather(axis, w, g, answer, there)
            pltpu.make_async_remote_copy(
                answer.at[pl.ds(there, size)], got.at[pl.ds(here_at, size)], ans_send, ans_recv,
                device_id=device_at(g, w), device_id_type=MESH,
            ).start()

    rounds = lines[0] * CORES
    assert lines[0] == lines[1]

    def in_round(i):
        return (i >= 0) & (i < rounds)

    def reply_round(r, carry):
        for layer in range(lines[2]):
            i = r - lead * layer
            at_y = lax.rem(my_y * CORES + my_core + 3 * (i + rounds), rounds)
            at_x = lax.rem(my_x * CORES + my_core + 3 * (i + rounds), rounds)
            w_y = layer * CORES + lax.rem(at_y, CORES)
            w_x = layer * CORES + lax.rem(at_x, CORES)
            reply(0, lax.div(at_y, CORES), my_x, w_y, in_round(i))
            reply(1, my_y, lax.div(at_x, CORES), w_x, in_round(i))
        i = r - lead * my_z
        for part in range(lines[0]):
            at = lax.rem(my_g * CORES + my_core + 13 * ((i + rounds) * lines[0] + part), far * CORES)
            g = lax.div(at, CORES)
            reply(2, lax.div(g, n_sub), lax.rem(g, n_sub), my_z * CORES + lax.rem(at, CORES), in_round(i))
        return carry

    assert lead * (lines[2] - 1) <= rounds
    lax.fori_loop(0, rounds + lead * (lines[2] - 1), reply_round, 0)
    for axis in range(3):
        gather(axis, my_w, my_g, got, planes_at(axis, my_y, my_x, my_w))

    free_step(d1, same_rows(d2), same_rows(vel), PAD - HALO, blocks, block)
    free_step(d2, own_rows(od_ref), own_rows(ov_ref), PAD, here // last_block, last_block)

    wire = pl.ds(0, (3 * n - sum(lines)) * cap)
    pltpu.make_async_copy(answer.at[wire], got.at[wire], ans_recv).wait()

    for s in range(steps):
        first_patch[s] = got[idx_s[s, 0]]
    ghost_copy = pltpu.make_async_remote_copy(
        first_patch, ghost, ghost_sem.at[0], ghost_sem.at[1],
        device_id=device(previous), device_id_type=MESH,
    )
    ghost_copy.start()

    def place(j, carry):
        for s in range(steps):
            planes[s, pl.ds(j * 4, 4), :] = got[idx_s[s, j]]
        return carry

    lax.fori_loop(0, seg, place, 0, unroll=8)

    flat = {"cm": cm, "kq": kq, "w4": w4}
    deep = {"d0": d0, "d1": d1, "d2": d2}
    chunk = width * stride

    def correct(q, carry):
        base = PAD + q * chunk

        def rows(name, o):
            at = pl.ds(base + o, width, stride=stride)
            if name in flat:
                return flat[name][at, :]
            return [deep[name][c, at, :] for c in range(3)]

        nearby = [[planes[s, pl.ds(q * width * 4 + c, width, stride=4), :] for c in range(4)] for s in range(steps)]
        u, z = contact_response(nearby, rows)
        at = pl.ds(pl.multiple_of(q * width, 8), width)
        for o in range(-2, 3):
            for c in range(3):
                share_u[o + 2, c, at, :] = u[o][c]
                share_z[o + 2, c, at, :] = z[o][c]
        return carry

    lax.fori_loop(0, seg // width, correct, 0)

    ghost_copy.wait()

    def ghost_rows(name, o):
        at = pl.ds(PAD + here + o, 1)
        if name in flat:
            return flat[name][at, :]
        return [deep[name][c, at, :] for c in range(3)]

    nearby = [[ghost[s, pl.ds(c, 1), :] for c in range(4)] for s in range(steps)]
    u, z = contact_response(nearby, ghost_rows)
    for o in (-2, -1):
        for c in range(3):
            share_u[o + 2, c, pl.ds(seg, 1), :] = u[o][c]
            share_z[o + 2, c, pl.ds(seg, 1), :] = z[o][c]

    pltpu.make_async_copy(answer.at[wire], got.at[wire], ans_send).wait()
    for axis, copies in enumerate((die_x, die_y, die_z)):
        others = copies.at[pl.ds(0, lines[axis] - 1)]
        pltpu.make_async_copy(others, others, die_send.at[axis]).wait()
    pltpu.make_async_copy(req.at[pl.ds(0, far - 1)], passed.at[pl.ds(0, far - 1)], req_send.at[0]).wait()
    pltpu.make_async_copy(asked.at[pl.ds(0, near - 1)], asked.at[pl.ds(0, near - 1)], req_send.at[1]).wait()


def add_share(parts, stride, d_ref, v_ref, share_u, share_z, od_hbm, ov_hbm, d_sum, v_sum, sem):
    here = d_ref.shape[1]
    chunk = here // parts
    width = chunk // stride
    copies = []
    for q in range(parts):
        rows = pl.ds(q * chunk, chunk)
        for a, (src, share, total, dst) in enumerate(
            ((d_ref, share_u, d_sum, od_hbm), (v_ref, share_z, v_sum, ov_hbm))
        ):
            total[:, rows, :] = src[:, rows, :]
            for o in range(-2, 3):
                at = pl.ds(q * chunk + (o + stride if o < 0 else o), width, stride=stride)
                block = pl.ds(q * width + (1 if o < 0 else 0), width)
                for c in range(3):
                    total[c, at, :] += share[o + 2, c, block, :]
            copy = pltpu.make_async_copy(total.at[:, rows], dst.at[:, rows], sem.at[a, q])
            copy.start()
            copies.append(copy)
    for copy in copies:
        copy.wait()


def body(n_dom, n_sub, displace, velocity, nodal_mass, stiffness, die_planes, owners, pairs):
    n = n_dom * n_sub
    here, ncol = displace.shape[1:]
    steps, seg = pairs.shape
    cap = max(2, 2 * seg // n)
    ext = here + 2 * PAD
    tiles = (here + 2 * HALO) // 8
    block = 8 * max(b for b in range(1, 44) if tiles % b == 0)
    last_block = 8 * max(b for b in range(1, 33) if here // 8 % b == 0)
    width = min(32, seg)
    near = min(8, n_dom // 2)
    far = n // near
    lanes = (n_sub + far // n_sub + near // CORES) * cap
    f32, i32 = jnp.float32, jnp.int32
    any_spec = pl.BlockSpec(memory_space=pl.ANY)
    vmem_spec = pl.BlockSpec(memory_space=pltpu.VMEM)
    dma = pltpu.SemaphoreType.DMA
    share = pltpu.VMEM((5, 3, seg + 8, ncol), f32)
    results = pl.pallas_call(
        functools.partial(kernel, n_dom, n_sub, cap, near, LEAD, block, last_block, width),
        out_shape=[pltpu.VMEM(displace.shape, f32)] * 2 + [share] * 2,
        in_specs=[any_spec] * 7,
        out_specs=[vmem_spec] * 4,
        scratch_shapes=[
            pltpu.VMEM((steps, 1, seg), i32),
            pltpu.VMEM((steps, seg), i32),
            pltpu.VMEM((3, ext, ncol), f32),
            pltpu.VMEM((3, ext, ncol), f32),
            pltpu.VMEM((3, ext, ncol), f32),
            pltpu.VMEM((3, ext, ncol), f32),
            pltpu.VMEM((ext, ncol), f32),
            pltpu.VMEM((ext, ncol), f32),
            pltpu.VMEM((ext, ncol), f32),
            pltpu.VMEM((n_sub,) + die_planes.shape[1:], f32),
            pltpu.VMEM((far // n_sub,) + die_planes.shape[1:], f32),
            pltpu.VMEM((near // CORES,) + die_planes.shape[1:], f32),
            pltpu.VMEM((far, near, 128), i32),
            pltpu.VMEM((far, near, 128), i32),
            pltpu.VMEM((near, far, 128), i32),
            pltpu.VMEM((-(-lanes // 8) * 8, n), i32),
            pltpu.SMEM((-(-lanes // 8) * 8, n), i32),
            pltpu.VMEM((8, seg), i32),
            pltpu.SMEM((8, seg), i32),
            pltpu.VMEM((n * steps * cap, 4, ncol), f32),
            pltpu.VMEM((n * steps * cap, 4, ncol), f32),
            pltpu.VMEM((steps, seg * 4 + 32, ncol), f32),
            pltpu.VMEM((steps, 4, ncol), f32),
            pltpu.VMEM((steps, 4, ncol), f32),
            pltpu.VMEM((3, max(block, last_block) + 8, ncol), f32),
            dma((9,)), dma((8,)), dma((8,)), dma((3,)), dma((3,)), dma((2,)), dma((2,)), dma, dma, dma((2,)), dma((2,)),
        ],
        compiler_params=pltpu.CompilerParams(
            collective_id=0, has_side_effects=True, vmem_limit_bytes=40 * 1024 * 1024
        ),
        name="stamp",
    )(*[
        pltpu.with_memory_space_constraint(x, pltpu.HBM)
        for x in (jnp.swapaxes(owners, 1, 2), pairs, displace, velocity, nodal_mass, stiffness, die_planes)
    ])
    parts = 4
    return pl.pallas_call(
        functools.partial(add_share, parts, here // seg),
        out_shape=[jax.ShapeDtypeStruct(displace.shape, f32)] * 2,
        in_specs=[vmem_spec] * 4,
        out_specs=[any_spec] * 2,
        scratch_shapes=[pltpu.VMEM(displace.shape, f32), pltpu.VMEM(displace.shape, f32), dma((2, parts))],
        compiler_params=pltpu.CompilerParams(vmem_limit_bytes=40 * 1024 * 1024),
        name="add_share",
    )(*[pltpu.with_memory_space_constraint(x, pltpu.VMEM) for x in results])


def solution(mesh):
    in_specs = (
        P(None, ("dom", "sub"), None),
        P(None, ("dom", "sub"), None),
        P(("dom", "sub"), None),
        P(("dom", "sub"), None),
        P(None, ("dom", "sub"), None, None),
        P(None, ("dom", "sub"), None),
        P(None, ("dom", "sub")),
    )
    out_specs = (P(None, ("dom", "sub"), None), P(None, ("dom", "sub"), None))
    run = functools.partial(body, mesh.shape["dom"], mesh.shape["sub"])
    return jax.shard_map(run, mesh=mesh, in_specs=in_specs, out_specs=out_specs, check_vma=False)
```

```python
import functools

import jax
import jax.numpy as jnp
from jax import lax
from jax.experimental import pallas as pl
from jax.experimental.pallas import tpu as pltpu
from jax.sharding import PartitionSpec as P

STEPS = 3
time_step = 0.2
penalty = 1.0

MESH = pl.DeviceIdType.MESH
PAD = 16
HALO = 8
CORES = 2
LEAD = 1


def next_col(x):
    return pltpu.roll(x, x.shape[-1] - 1, x.ndim - 1)


def prev_col(x):
    return pltpu.roll(x, 1, x.ndim - 1)


def contact(planes, position):
    normal, height = planes[:3], planes[3]
    depth = height - (normal[0] * position[0] + normal[1] * position[1] + normal[2] * position[2])
    push = penalty * jnp.maximum(depth, 0.0)
    return [push * normal[c] for c in range(3)]


def contact_response(planes, rows):
    cm = {o: rows("cm", o) for o in range(-2, 3)}
    kq = {o: rows("kq", o) for o in range(-2, 2)}
    w4 = {o: rows("w4", o) for o in range(-1, 2)}
    u = {}
    z = {}
    for step in range(STEPS):
        free = rows("d%d" % step, 0)
        position = [free[c] + u[0][c] if step else free[c] for c in range(3)]
        push = contact(planes[step], position)
        new_u, new_z = {}, {}
        for o in range(-step, step + 1):
            new_u[o], new_z[o] = [], []
        for c in range(3):
            spread = {}
            for o in range(-step, step):
                parts = [u[r][c] for r in (o, o + 1) if r in u]
                box = parts[0] if len(parts) == 1 else parts[0] + parts[1]
                t = kq[o] * (box + next_col(box))
                spread[o] = t + prev_col(t)
            for o in range(-step, step + 1):
                terms = [spread[r] for r in (o - 1, o) if r in spread]
                if o in u:
                    terms.append(-(w4[o] * u[o][c]))
                if o == 0:
                    terms.append(push[c])
                force = terms[0]
                for term in terms[1:]:
                    force = force + term
                dz = cm[o] * force
                zc = z[o][c] + dz if o in z else dz
                uc = time_step * zc
                if o in u:
                    uc = u[o][c] + uc
                new_z[o].append(zc)
                new_u[o].append(uc)
        u, z = new_u, new_z
    return u, z


def kernel(
    n_dom, n_sub, cap, near, lead, block, last_block, width,
    own_hbm, pair_hbm, d_hbm, v_hbm, m_hbm, k_hbm, die_hbm,
    od_ref, ov_ref, share_u, share_z,
    own_ref, pair_ref, d0, d1, d2, vel, cm, kq, w4, die_x, die_y, die_z, req, passed, asked, asked_rows, asked_s, idx, idx_s, answer, got, planes, first_patch, ghost, term,
    load_sem, halo_send, halo_recv, die_send, die_recv, req_send, req_recv, ans_send, ans_recv, small_sem, ghost_sem,
):
    n = n_dom * n_sub
    steps, seg = pair_hbm.shape
    here = d_hbm.shape[1]
    stride = here // seg
    ncol = d_hbm.shape[2]
    assert steps == 3
    lists_rows = asked_s.shape[0]
    patches = die_hbm.shape[1]
    dom, sub = lax.axis_index("dom"), lax.axis_index("sub")
    me = dom * n_sub + sub

    def device(i):
        return (lax.div(i, n_sub), lax.rem(i, n_sub))

    far = n // near
    lines = (n_sub, far // n_sub, near // CORES)
    my_w = lax.rem(dom, near)
    my_x, my_y, my_z, my_core = sub, lax.div(dom, near), lax.div(my_w, CORES), lax.rem(my_w, CORES)
    my_g = my_y * n_sub + my_x

    def device_at(g, w):
        return (lax.div(g, n_sub) * near + w, lax.rem(g, n_sub))

    def other_group(t):
        return lax.rem(my_g + t, far)

    def other_member(t):
        return lax.rem(my_w + t, near)

    following, previous = lax.rem(me + 1, n), lax.rem(me + n - 1, n)

    inner = pl.ds(PAD, here)
    lists = [
        pltpu.make_async_copy(own_hbm, own_ref, load_sem.at[5]),
        pltpu.make_async_copy(pair_hbm, pair_ref, load_sem.at[6]),
    ]
    loads = [
        pltpu.make_async_copy(d_hbm, d0.at[:, inner], load_sem.at[0]),
        pltpu.make_async_copy(v_hbm, vel.at[:, inner], load_sem.at[1]),
        pltpu.make_async_copy(m_hbm, cm.at[inner], load_sem.at[2]),
        pltpu.make_async_copy(k_hbm, kq.at[inner], load_sem.at[3]),
        pltpu.make_async_copy(die_hbm.at[0], die_x.at[my_x], load_sem.at[4]),
        pltpu.make_async_copy(die_hbm.at[1], die_y.at[my_y], load_sem.at[7]),
        pltpu.make_async_copy(die_hbm.at[2], die_z.at[0], load_sem.at[8]),
    ]
    for copy in lists + loads:
        copy.start()

    barrier = pltpu.get_barrier_semaphore()

    def greet(to):
        pl.semaphore_signal(barrier, inc=1, device_id=to, device_id_type=MESH)

    def greet_groups(t, carry):
        greet(device_at(other_group(t), my_w))
        return carry

    def greet_members(t, carry):
        greet(device_at(my_g, other_member(t)))
        return carry

    lax.fori_loop(1, far, greet_groups, 0)
    lax.fori_loop(1, near, greet_members, 0)
    greet(device(following))
    greet(device(previous))

    pl.semaphore_wait(barrier, far + near)

    sets = (die_x, die_y, die_z)
    half = patches // 2

    def along(axis, t):
        return lax.rem((my_x, my_y, my_z)[axis] + t, lines[axis])

    def device_along(axis, t):
        there = along(axis, t)
        return (
            device_at(my_y * n_sub + there, my_w),
            device_at(there * n_sub + my_x, my_w),
            device_at(my_g, there * CORES + my_core),
        )[axis]

    def set_of(axis, t, seen):
        return (t - seen) % lines[axis] if axis == 2 else along(axis, t)

    def set_copy(axis, t, to, src, rows, number):
        place = sets[axis].at[set_of(axis, t, to), rows]
        return pltpu.make_async_remote_copy(
            src, place, die_send.at[axis, number], die_recv.at[axis, number],
            device_id=device_along(axis, to), device_id_type=MESH,
        )

    first_legs, second_legs = [], []
    every = pl.ds(0, patches)
    for axis, count in enumerate(lines):
        assert count in (2, 4)
        for number, to in enumerate((1, count - 1)[: count - 2 or 1]):
            copy = set_copy(axis, 0, to, die_hbm.at[axis], every, number)
            copy.start()
            first_legs.append(copy)

    def hand_sets_on():
        for copy in first_legs:
            copy.wait_recv()
        for axis, count in enumerate(lines):
            if count == 4:
                for number, (came, to, rows) in enumerate(((3, 1, pl.ds(0, half)), (1, 3, pl.ds(half, half)))):
                    src = sets[axis].at[set_of(axis, came, 0), rows]
                    copy = set_copy(axis, came, to, src, rows, 2 + number)
                    copy.start()
                    second_legs.append(copy)

    lane_of = lax.broadcasted_iota(jnp.int32, (n, 128), 1)
    row = lax.broadcasted_iota(jnp.int32, (n, seg), 0)
    row_g, row_w = lax.div(row, near), lax.rem(row, near)
    owner_of = (lax.div(row_g, n_sub) * near + row_w) * n_sub + lax.rem(row_g, n_sub)
    before = lax.broadcasted_iota(jnp.int32, (seg, seg), 0) < lax.broadcasted_iota(jnp.int32, (seg, seg), 1)
    table = jnp.zeros((n, 128), jnp.int32)
    places = []
    for copy in lists:
        copy.wait()
    for s in range(steps):
        own = own_ref[s]
        wide = jnp.broadcast_to(own, (seg, seg))
        same = (wide == wide.T) & before
        slot = jnp.minimum(jnp.sum(same.astype(jnp.int32), axis=0, keepdims=True), cap - 1)
        own_dom, own_x = lax.div(own, n_sub), lax.rem(own, n_sub)
        own_y, own_w = lax.div(own_dom, near), lax.rem(own_dom, near)
        own_z, own_core = lax.div(own_w, CORES), lax.rem(own_w, CORES)
        line, at_line = (
            (own_y * near + own_w, own_x),
            (own_x * near + own_w, own_y),
            ((own_y * n_sub + own_x) * CORES + own_core, lax.rem(own_z + (lines[2] - my_z), lines[2])),
        )[s]
        places.append((s * n + line * lines[s] + at_line) * cap + slot)
        pair = pair_ref[s : s + 1, :]
        mine = owner_of == own
        for k in range(cap):
            chosen = jnp.where(mine & (slot == k), pair, 0)
            table = jnp.where(lane_of == s * cap + k, jnp.sum(chosen, axis=1, keepdims=True), table)
    by_group = [table[near * g : near * (g + 1)] for g in range(far)]
    lane = lax.broadcasted_iota(jnp.int32, (near, 128), 1)

    def lanes_of(s, value, to):
        value = jnp.where((lane >= s * cap) & (lane < (s + 1) * cap), value, 0)
        shift = to - s * cap
        return pltpu.roll(value, shift, 1) if shift else value

    firsts = (0, lines[0] * cap, (lines[0] + lines[1]) * cap)
    along_x = [
        sum(lanes_of(0, by_group[y * n_sub + x], firsts[0] + x * cap) for x in range(lines[0])) for y in range(lines[1])
    ]
    along_y = [
        sum(lanes_of(1, by_group[y * n_sub + x], firsts[1] + y * cap) for y in range(lines[1])) for x in range(lines[0])
    ]
    for g in range(far):
        along_z = 0
        for z in range(lines[2]):
            turned = pltpu.roll(by_group[g], near - z * CORES, 0) if z else by_group[g]
            along_z = along_z + lanes_of(2, turned, firsts[2] + z * cap)
        req[g] = along_x[g // n_sub] + along_y[g % n_sub] + along_z
    def ask(t, carry):
        g = other_group(t)
        pltpu.make_async_remote_copy(
            req.at[g], passed.at[my_g], req_send.at[0], req_recv.at[0],
            device_id=device_at(g, my_w), device_id_type=MESH,
        ).start()
        return carry

    lax.fori_loop(1, far, ask, 0)
    pltpu.make_async_copy(req.at[my_g], passed.at[my_g], req_recv.at[0]).start()

    for s in range(steps):
        idx[s : s + 1, :] = places[s]
    idx_copy = pltpu.make_async_copy(idx, idx_s, small_sem.at[0])
    idx_copy.start()

    first, last = pl.ds(0, HALO), pl.ds(here - HALO, HALO)
    front, back = pl.ds(PAD - HALO, HALO), pl.ds(PAD + here, HALO)
    halos = []
    for a, (src, dst) in enumerate(((d_hbm, d0), (v_hbm, vel), (m_hbm, cm), (k_hbm, kq))):
        three = len(src.shape) == 3
        for side, (rows, place, to) in enumerate(((last, front, following), (first, back, previous))):
            copy = pltpu.make_async_remote_copy(
                src.at[:, rows] if three else src.at[rows],
                dst.at[:, place] if three else dst.at[place],
                halo_send.at[2 * a + side], halo_recv.at[2 * a + side],
                device_id=device(to), device_id_type=MESH,
            )
            copy.start()
            halos.append(copy)

    for copy in loads:
        copy.wait()

    def prepare(base, size):
        at = pl.ds(base, size)
        col = lax.broadcasted_iota(jnp.int32, (size, ncol), 1)
        kq[at, :] = jnp.where(col < ncol - 1, kq[at, :] * 0.25, 0.0)
        cm[at, :] = time_step / cm[at, :]

    def prepare_block(b, carry):
        prepare(pl.multiple_of(PAD + b * last_block, 8), last_block)
        return carry

    lax.fori_loop(0, here // last_block, prepare_block, 0)

    pltpu.make_async_copy(req, passed, req_recv.at[0]).wait()

    def hand_on(t, carry):
        w = other_member(t)
        pltpu.make_async_remote_copy(
            passed.at[:, w], asked.at[my_w], req_send.at[1], req_recv.at[1],
            device_id=device_at(my_g, w), device_id_type=MESH,
        ).start()
        return carry

    lax.fori_loop(1, near, hand_on, 0)
    pltpu.make_async_copy(passed.at[:, my_w], asked.at[my_w], req_recv.at[1]).start()
    hand_sets_on()

    for copy in halos:
        copy.wait()
    prepare(PAD - HALO, HALO)
    prepare(PAD + here, HALO)

    @pl.when(me == 0)
    def _():
        kq[front, :] = jnp.zeros((HALO, ncol), jnp.float32)

    @pl.when(me == n - 1)
    def _():
        tail = pl.ds(PAD + here - HALO, HALO)
        row = lax.broadcasted_iota(jnp.int32, (HALO, ncol), 0)
        kq[tail, :] = jnp.where(row == HALO - 1, 0.0, kq[tail, :])

    blocks = (here + 2 * HALO) // block
    assert blocks * block == here + 2 * HALO

    def weights(b, carry):
        base = pl.multiple_of(PAD - HALO + b * block, 8)
        both = kq[pl.ds(base, block), :] + kq[pl.ds(base - 1, block), :]
        w4[pl.ds(base, block), :] = 4.0 * (both + prev_col(both))
        return carry

    lax.fori_loop(0, blocks, weights, 0)

    def free_step(src, d_to, v_to, first_row, count, size):
        def part(b, carry):
            base = pl.multiple_of(first_row + b * size, 8)
            for i in range(size // 8 + 1):
                at = pl.ds(base + 8 * (i - 1), 8)
                below = pl.ds(base + 8 * (i - 1) + 1, 8)
                for c in range(3):
                    d = src[c, at, :]
                    box = d + src[c, below, :]
                    t = kq[at, :] * (box + next_col(box))
                    term[c, 8 * i : 8 * (i + 1), :] = t
                    if i:
                        t = t + term[c, 8 * i - 1 : 8 * i + 7, :]
                        force = t + prev_col(t) - w4[at, :] * d
                        v = vel[c, at, :] + cm[at, :] * force
                        v_to(base, size)[c, 8 * (i - 1) : 8 * i, :] = v
                        d_to(base, size)[c, 8 * (i - 1) : 8 * i, :] = d + time_step * v
            return carry

        lax.fori_loop(0, count, part, 0)

    def same_rows(ref):
        return lambda base, size: ref.at[:, pl.ds(base, size)]

    def own_rows(ref):
        return lambda base, size: ref.at[:, pl.ds(pl.multiple_of(base - PAD, 8), size)]

    free_step(d0, same_rows(d1), same_rows(vel), PAD - HALO, blocks, block)

    pltpu.make_async_copy(asked, asked, req_recv.at[1]).wait()
    asked_rows[...] = jnp.clip(asked[...].reshape(n, 128).T[:lists_rows], 0, patches - 1)
    to_scalar = pltpu.make_async_copy(asked_rows, asked_s, small_sem.at[1])
    to_scalar.start()
    to_scalar.wait()
    idx_copy.wait()

    for copy in second_legs:
        copy.wait_recv()

    def gather(axis, w, g, dst, at):
        copies = (die_x, die_y, die_z)[axis]
        for i in range(lines[axis] * cap):
            dst[at + i] = copies[i // cap, asked_s[firsts[axis] + i, w * far + g]]

    def line_of(axis, y, x, w):
        return (y * near + w, x * near + w, (y * n_sub + x) * CORES + lax.rem(w, CORES))[axis]

    def planes_at(axis, y, x, w):
        return (axis * n + line_of(axis, y, x, w) * lines[axis]) * cap

    def reply(axis, y, x, w, wanted):
        g = y * n_sub + x

        @pl.when(wanted & ((g != my_g) | (w != my_w)))
        def _():
            size = lines[axis] * cap
            there, here_at = planes_at(axis, y, x, w), planes_at(axis, my_y, my_x, my_w)
            gather(axis, w, g, answer, there)
            pltpu.make_async_remote_copy(
                answer.at[pl.ds(there, size)], got.at[pl.ds(here_at, size)], ans_send, ans_recv,
                device_id=device_at(g, w), device_id_type=MESH,
            ).start()

    rounds = lines[0] * CORES
    assert lines[0] == lines[1]

    def in_round(i):
        return (i >= 0) & (i < rounds)

    def reply_round(r, carry):
        for layer in range(lines[2]):
            i = r - lead * layer
            at_y = lax.rem(my_y * CORES + my_core + 3 * (i + rounds), rounds)
            at_x = lax.rem(my_x * CORES + my_core + 3 * (i + rounds), rounds)
            w_y = layer * CORES + lax.rem(at_y, CORES)
            w_x = layer * CORES + lax.rem(at_x, CORES)
            reply(0, lax.div(at_y, CORES), my_x, w_y, in_round(i))
            reply(1, my_y, lax.div(at_x, CORES), w_x, in_round(i))
        i = r - lead * my_z
        for part in range(lines[0]):
            at = lax.rem(my_g * CORES + my_core + 13 * ((i + rounds) * lines[0] + part), far * CORES)
            g = lax.div(at, CORES)
            reply(2, lax.div(g, n_sub), lax.rem(g, n_sub), my_z * CORES + lax.rem(at, CORES), in_round(i))
        return carry

    assert lead * (lines[2] - 1) <= rounds
    lax.fori_loop(0, rounds + lead * (lines[2] - 1), reply_round, 0)
    for axis in range(3):
        gather(axis, my_w, my_g, got, planes_at(axis, my_y, my_x, my_w))

    free_step(d1, same_rows(d2), same_rows(vel), PAD - HALO, blocks, block)
    free_step(d2, own_rows(od_ref), own_rows(ov_ref), PAD, here // last_block, last_block)

    wire = pl.ds(0, (3 * n - sum(lines)) * cap)
    pltpu.make_async_copy(answer.at[wire], got.at[wire], ans_recv).wait()

    for s in range(steps):
        first_patch[s] = got[idx_s[s, 0]]
    ghost_copy = pltpu.make_async_remote_copy(
        first_patch, ghost, ghost_sem.at[0], ghost_sem.at[1],
        device_id=device(previous), device_id_type=MESH,
    )
    ghost_copy.start()

    def place(j, carry):
        for s in range(steps):
            planes[s, pl.ds(j * 4, 4), :] = got[idx_s[s, j]]
        return carry

    lax.fori_loop(0, seg, place, 0, unroll=8)

    flat = {"cm": cm, "kq": kq, "w4": w4}
    deep = {"d0": d0, "d1": d1, "d2": d2}
    chunk = width * stride

    def correct(q, carry):
        base = PAD + q * chunk

        def rows(name, o):
            at = pl.ds(base + o, width, stride=stride)
            if name in flat:
                return flat[name][at, :]
            return [deep[name][c, at, :] for c in range(3)]

        nearby = [[planes[s, pl.ds(q * width * 4 + c, width, stride=4), :] for c in range(4)] for s in range(steps)]
        u, z = contact_response(nearby, rows)
        at = pl.ds(pl.multiple_of(q * width, 8), width)
        for o in range(-2, 3):
            for c in range(3):
                share_u[o + 2, c, at, :] = u[o][c]
                share_z[o + 2, c, at, :] = z[o][c]
        return carry

    lax.fori_loop(0, seg // width, correct, 0)

    ghost_copy.wait()

    def ghost_rows(name, o):
        at = pl.ds(PAD + here + o, 1)
        if name in flat:
            return flat[name][at, :]
        return [deep[name][c, at, :] for c in range(3)]

    nearby = [[ghost[s, pl.ds(c, 1), :] for c in range(4)] for s in range(steps)]
    u, z = contact_response(nearby, ghost_rows)
    for o in (-2, -1):
        for c in range(3):
            share_u[o + 2, c, pl.ds(seg, 1), :] = u[o][c]
            share_z[o + 2, c, pl.ds(seg, 1), :] = z[o][c]

    pltpu.make_async_copy(answer.at[wire], got.at[wire], ans_send).wait()
    for copy in first_legs + second_legs:
        copy.wait_send()
    pltpu.make_async_copy(req.at[pl.ds(0, far - 1)], passed.at[pl.ds(0, far - 1)], req_send.at[0]).wait()
    pltpu.make_async_copy(asked.at[pl.ds(0, near - 1)], asked.at[pl.ds(0, near - 1)], req_send.at[1]).wait()


def add_share(parts, stride, d_ref, v_ref, share_u, share_z, od_hbm, ov_hbm, d_sum, v_sum, sem):
    here = d_ref.shape[1]
    chunk = here // parts
    width = chunk // stride
    copies = []
    for q in range(parts):
        rows = pl.ds(q * chunk, chunk)
        for a, (src, share, total, dst) in enumerate(
            ((d_ref, share_u, d_sum, od_hbm), (v_ref, share_z, v_sum, ov_hbm))
        ):
            total[:, rows, :] = src[:, rows, :]
            for o in range(-2, 3):
                at = pl.ds(q * chunk + (o + stride if o < 0 else o), width, stride=stride)
                block = pl.ds(q * width + (1 if o < 0 else 0), width)
                for c in range(3):
                    total[c, at, :] += share[o + 2, c, block, :]
            copy = pltpu.make_async_copy(total.at[:, rows], dst.at[:, rows], sem.at[a, q])
            copy.start()
            copies.append(copy)
    for copy in copies:
        copy.wait()


def body(n_dom, n_sub, displace, velocity, nodal_mass, stiffness, die_planes, owners, pairs):
    n = n_dom * n_sub
    here, ncol = displace.shape[1:]
    steps, seg = pairs.shape
    cap = max(2, 2 * seg // n)
    ext = here + 2 * PAD
    tiles = (here + 2 * HALO) // 8
    block = 8 * max(b for b in range(1, 44) if tiles % b == 0)
    last_block = 8 * max(b for b in range(1, 33) if here // 8 % b == 0)
    width = min(32, seg)
    near = min(8, n_dom // 2)
    far = n // near
    lanes = (n_sub + far // n_sub + near // CORES) * cap
    f32, i32 = jnp.float32, jnp.int32
    any_spec = pl.BlockSpec(memory_space=pl.ANY)
    vmem_spec = pl.BlockSpec(memory_space=pltpu.VMEM)
    dma = pltpu.SemaphoreType.DMA
    share = pltpu.VMEM((5, 3, seg + 8, ncol), f32)
    results = pl.pallas_call(
        functools.partial(kernel, n_dom, n_sub, cap, near, LEAD, block, last_block, width),
        out_shape=[pltpu.VMEM(displace.shape, f32)] * 2 + [share] * 2,
        in_specs=[any_spec] * 7,
        out_specs=[vmem_spec] * 4,
        scratch_shapes=[
            pltpu.VMEM((steps, 1, seg), i32),
            pltpu.VMEM((steps, seg), i32),
            pltpu.VMEM((3, ext, ncol), f32),
            pltpu.VMEM((3, ext, ncol), f32),
            pltpu.VMEM((3, ext, ncol), f32),
            pltpu.VMEM((3, ext, ncol), f32),
            pltpu.VMEM((ext, ncol), f32),
            pltpu.VMEM((ext, ncol), f32),
            pltpu.VMEM((ext, ncol), f32),
            pltpu.VMEM((n_sub,) + die_planes.shape[1:], f32),
            pltpu.VMEM((far // n_sub,) + die_planes.shape[1:], f32),
            pltpu.VMEM((near // CORES,) + die_planes.shape[1:], f32),
            pltpu.VMEM((far, near, 128), i32),
            pltpu.VMEM((far, near, 128), i32),
            pltpu.VMEM((near, far, 128), i32),
            pltpu.VMEM((-(-lanes // 8) * 8, n), i32),
            pltpu.SMEM((-(-lanes // 8) * 8, n), i32),
            pltpu.VMEM((8, seg), i32),
            pltpu.SMEM((8, seg), i32),
            pltpu.VMEM((n * steps * cap, 4, ncol), f32),
            pltpu.VMEM((n * steps * cap, 4, ncol), f32),
            pltpu.VMEM((steps, seg * 4 + 32, ncol), f32),
            pltpu.VMEM((steps, 4, ncol), f32),
            pltpu.VMEM((steps, 4, ncol), f32),
            pltpu.VMEM((3, max(block, last_block) + 8, ncol), f32),
            dma((9,)), dma((8,)), dma((8,)), dma((3, 4)), dma((3, 4)), dma((2,)), dma((2,)), dma, dma, dma((2,)), dma((2,)),
        ],
        compiler_params=pltpu.CompilerParams(
            collective_id=0, has_side_effects=True, vmem_limit_bytes=40 * 1024 * 1024
        ),
        name="stamp",
    )(*[
        pltpu.with_memory_space_constraint(x, pltpu.HBM)
        for x in (jnp.swapaxes(owners, 1, 2), pairs, displace, velocity, nodal_mass, stiffness, die_planes)
    ])
    parts = 4
    return pl.pallas_call(
        functools.partial(add_share, parts, here // seg),
        out_shape=[jax.ShapeDtypeStruct(displace.shape, f32)] * 2,
        in_specs=[vmem_spec] * 4,
        out_specs=[any_spec] * 2,
        scratch_shapes=[pltpu.VMEM(displace.shape, f32), pltpu.VMEM(displace.shape, f32), dma((2, parts))],
        compiler_params=pltpu.CompilerParams(vmem_limit_bytes=40 * 1024 * 1024),
        name="add_share",
    )(*[pltpu.with_memory_space_constraint(x, pltpu.VMEM) for x in results])


def solution(mesh):
    in_specs = (
        P(None, ("dom", "sub"), None),
        P(None, ("dom", "sub"), None),
        P(("dom", "sub"), None),
        P(("dom", "sub"), None),
        P(None, ("dom", "sub"), None, None),
        P(None, ("dom", "sub"), None),
        P(None, ("dom", "sub")),
    )
    out_specs = (P(None, ("dom", "sub"), None), P(None, ("dom", "sub"), None))
    run = functools.partial(body, mesh.shape["dom"], mesh.shape["sub"])
    return jax.shard_map(run, mesh=mesh, in_specs=in_specs, out_specs=out_specs, check_vma=False)
```

```python
import functools

import jax
import jax.numpy as jnp
from jax import lax
from jax.experimental import pallas as pl
from jax.experimental.pallas import tpu as pltpu
from jax.sharding import PartitionSpec as P

STEPS = 3
time_step = 0.2
penalty = 1.0

MESH = pl.DeviceIdType.MESH
PAD = 16
HALO = 8
CORES = 2
LEAD = 1


def next_col(x):
    return pltpu.roll(x, x.shape[-1] - 1, x.ndim - 1)


def prev_col(x):
    return pltpu.roll(x, 1, x.ndim - 1)


def contact(planes, position):
    normal, height = planes[:3], planes[3]
    depth = height - (normal[0] * position[0] + normal[1] * position[1] + normal[2] * position[2])
    push = penalty * jnp.maximum(depth, 0.0)
    return [push * normal[c] for c in range(3)]


def contact_response(planes, rows):
    cm = {o: rows("cm", o) for o in range(-2, 3)}
    kq = {o: rows("kq", o) for o in range(-2, 2)}
    w4 = {o: rows("w4", o) for o in range(-1, 2)}
    u = {}
    z = {}
    for step in range(STEPS):
        free = rows("d%d" % step, 0)
        position = [free[c] + u[0][c] if step else free[c] for c in range(3)]
        push = contact(planes[step], position)
        new_u, new_z = {}, {}
        for o in range(-step, step + 1):
            new_u[o], new_z[o] = [], []
        for c in range(3):
            spread = {}
            for o in range(-step, step):
                parts = [u[r][c] for r in (o, o + 1) if r in u]
                box = parts[0] if len(parts) == 1 else parts[0] + parts[1]
                t = kq[o] * (box + next_col(box))
                spread[o] = t + prev_col(t)
            for o in range(-step, step + 1):
                terms = [spread[r] for r in (o - 1, o) if r in spread]
                if o in u:
                    terms.append(-(w4[o] * u[o][c]))
                if o == 0:
                    terms.append(push[c])
                force = terms[0]
                for term in terms[1:]:
                    force = force + term
                dz = cm[o] * force
                zc = z[o][c] + dz if o in z else dz
                uc = time_step * zc
                if o in u:
                    uc = u[o][c] + uc
                new_z[o].append(zc)
                new_u[o].append(uc)
        u, z = new_u, new_z
    return u, z


def kernel(
    n_dom, n_sub, cap, near, lead, block, last_block, width,
    own_hbm, pair_hbm, d_hbm, v_hbm, m_hbm, k_hbm, die_hbm,
    od_ref, ov_ref, share_u, share_z,
    own_ref, pair_ref, d0, d1, d2, vel, cm, kq, w4, die_x, die_y, die_z, req, passed, asked, asked_rows, asked_s, idx, idx_s, answer, got, planes, first_patch, ghost, term,
    load_sem, halo_send, halo_recv, die_send, die_recv, req_send, req_recv, ans_send, ans_recv, small_sem, ghost_sem,
):
    n = n_dom * n_sub
    steps, seg = pair_hbm.shape
    here = d_hbm.shape[1]
    stride = here // seg
    ncol = d_hbm.shape[2]
    assert steps == 3
    lists_rows = asked_s.shape[0]
    patches = die_hbm.shape[1]
    dom, sub = lax.axis_index("dom"), lax.axis_index("sub")
    me = dom * n_sub + sub

    def device(i):
        return (lax.div(i, n_sub), lax.rem(i, n_sub))

    far = n // near
    lines = (n_sub, far // n_sub, near // CORES)
    my_w = lax.rem(dom, near)
    my_x, my_y, my_z, my_core = sub, lax.div(dom, near), lax.div(my_w, CORES), lax.rem(my_w, CORES)
    my_g = my_y * n_sub + my_x

    def device_at(g, w):
        return (lax.div(g, n_sub) * near + w, lax.rem(g, n_sub))

    def other_group(t):
        return lax.rem(my_g + t, far)

    def other_member(t):
        return lax.rem(my_w + t, near)

    following, previous = lax.rem(me + 1, n), lax.rem(me + n - 1, n)

    inner = pl.ds(PAD, here)
    lists = [
        pltpu.make_async_copy(own_hbm, own_ref, load_sem.at[5]),
        pltpu.make_async_copy(pair_hbm, pair_ref, load_sem.at[6]),
    ]
    loads = [
        pltpu.make_async_copy(d_hbm, d0.at[:, inner], load_sem.at[0]),
        pltpu.make_async_copy(v_hbm, vel.at[:, inner], load_sem.at[1]),
        pltpu.make_async_copy(m_hbm, cm.at[inner], load_sem.at[2]),
        pltpu.make_async_copy(k_hbm, kq.at[inner], load_sem.at[3]),
        pltpu.make_async_copy(die_hbm.at[0], die_x.at[my_x], load_sem.at[4]),
        pltpu.make_async_copy(die_hbm.at[1], die_y.at[my_y], load_sem.at[7]),
        pltpu.make_async_copy(die_hbm.at[2], die_z.at[0], load_sem.at[8]),
    ]
    for copy in lists + loads:
        copy.start()

    barrier = pltpu.get_barrier_semaphore()

    def greet(to):
        pl.semaphore_signal(barrier, inc=1, device_id=to, device_id_type=MESH)

    def greet_groups(t, carry):
        greet(device_at(other_group(t), my_w))
        return carry

    def greet_members(t, carry):
        greet(device_at(my_g, other_member(t)))
        return carry

    lax.fori_loop(1, far, greet_groups, 0)
    lax.fori_loop(1, near, greet_members, 0)
    greet(device(following))
    greet(device(previous))

    pl.semaphore_wait(barrier, far + near)

    sets = (die_x, die_y, die_z)
    half = patches // 2

    def along(axis, t):
        return lax.rem((my_x, my_y, my_z)[axis] + t, lines[axis])

    def device_along(axis, t):
        there = along(axis, t)
        return (
            device_at(my_y * n_sub + there, my_w),
            device_at(there * n_sub + my_x, my_w),
            device_at(my_g, there * CORES + my_core),
        )[axis]

    def set_of(axis, t, seen):
        return (t - seen) % lines[axis] if axis == 2 else along(axis, t)

    def set_copy(axis, t, to, src, rows, number):
        place = sets[axis].at[set_of(axis, t, to), rows]
        return pltpu.make_async_remote_copy(
            src, place, die_send.at[axis, number], die_recv.at[axis, number],
            device_id=device_along(axis, to), device_id_type=MESH,
        )

    first_legs, second_legs = [], []
    every = pl.ds(0, patches)
    for axis, count in enumerate(lines):
        assert count in (2, 4)
        for number, to in enumerate((1, count - 1)[: count - 2 or 1]):
            copy = set_copy(axis, 0, to, die_hbm.at[axis], every, number)
            copy.start()
            first_legs.append(copy)

    def hand_sets_on():
        for copy in first_legs:
            copy.wait_recv()
        for axis, count in enumerate(lines):
            if count == 4:
                for number, (came, to, rows) in enumerate(((3, 1, pl.ds(0, half)), (1, 3, pl.ds(half, half)))):
                    src = sets[axis].at[set_of(axis, came, 0), rows]
                    copy = set_copy(axis, came, to, src, rows, 2 + number)
                    copy.start()
                    second_legs.append(copy)

    lane_of = lax.broadcasted_iota(jnp.int32, (n, 128), 1)
    row = lax.broadcasted_iota(jnp.int32, (n, seg), 0)
    row_g, row_w = lax.div(row, near), lax.rem(row, near)
    owner_of = (lax.div(row_g, n_sub) * near + row_w) * n_sub + lax.rem(row_g, n_sub)
    before = lax.broadcasted_iota(jnp.int32, (seg, seg), 0) < lax.broadcasted_iota(jnp.int32, (seg, seg), 1)
    table = jnp.zeros((n, 128), jnp.int32)
    places = []
    for copy in lists:
        copy.wait()
    for s in range(steps):
        own = own_ref[s]
        wide = jnp.broadcast_to(own, (seg, seg))
        same = (wide == wide.T) & before
        slot = jnp.minimum(jnp.sum(same.astype(jnp.int32), axis=0, keepdims=True), cap - 1)
        own_dom, own_x = lax.div(own, n_sub), lax.rem(own, n_sub)
        own_y, own_w = lax.div(own_dom, near), lax.rem(own_dom, near)
        own_z, own_core = lax.div(own_w, CORES), lax.rem(own_w, CORES)
        line, at_line = (
            (own_y * near + own_w, own_x),
            (own_x * near + own_w, own_y),
            ((own_y * n_sub + own_x) * CORES + own_core, lax.rem(own_z + (lines[2] - my_z), lines[2])),
        )[s]
        places.append((s * n + line * lines[s] + at_line) * cap + slot)
        pair = pair_ref[s : s + 1, :]
        mine = owner_of == own
        for k in range(cap):
            chosen = jnp.where(mine & (slot == k), pair, 0)
            table = jnp.where(lane_of == s * cap + k, jnp.sum(chosen, axis=1, keepdims=True), table)
    by_group = [table[near * g : near * (g + 1)] for g in range(far)]
    lane = lax.broadcasted_iota(jnp.int32, (near, 128), 1)

    def lanes_of(s, value, to):
        value = jnp.where((lane >= s * cap) & (lane < (s + 1) * cap), value, 0)
        shift = to - s * cap
        return pltpu.roll(value, shift, 1) if shift else value

    firsts = (0, lines[0] * cap, (lines[0] + lines[1]) * cap)
    along_x = [
        sum(lanes_of(0, by_group[y * n_sub + x], firsts[0] + x * cap) for x in range(lines[0])) for y in range(lines[1])
    ]
    along_y = [
        sum(lanes_of(1, by_group[y * n_sub + x], firsts[1] + y * cap) for y in range(lines[1])) for x in range(lines[0])
    ]
    for g in range(far):
        along_z = 0
        for z in range(lines[2]):
            turned = pltpu.roll(by_group[g], near - z * CORES, 0) if z else by_group[g]
            along_z = along_z + lanes_of(2, turned, firsts[2] + z * cap)
        req[g] = along_x[g // n_sub] + along_y[g % n_sub] + along_z
    def ask(t, carry):
        g = other_group(t)
        pltpu.make_async_remote_copy(
            req.at[g], passed.at[my_g], req_send.at[0], req_recv.at[0],
            device_id=device_at(g, my_w), device_id_type=MESH,
        ).start()
        return carry

    lax.fori_loop(1, far, ask, 0)
    pltpu.make_async_copy(req.at[my_g], passed.at[my_g], req_recv.at[0]).start()

    for s in range(steps):
        idx[s : s + 1, :] = places[s]
    idx_copy = pltpu.make_async_copy(idx, idx_s, small_sem.at[0])
    idx_copy.start()

    first, last = pl.ds(0, HALO), pl.ds(here - HALO, HALO)
    front, back = pl.ds(PAD - HALO, HALO), pl.ds(PAD + here, HALO)
    halos = []
    for a, (src, dst) in enumerate(((d_hbm, d0), (v_hbm, vel), (m_hbm, cm), (k_hbm, kq))):
        three = len(src.shape) == 3
        for side, (rows, place, to) in enumerate(((last, front, following), (first, back, previous))):
            copy = pltpu.make_async_remote_copy(
                src.at[:, rows] if three else src.at[rows],
                dst.at[:, place] if three else dst.at[place],
                halo_send.at[2 * a + side], halo_recv.at[2 * a + side],
                device_id=device(to), device_id_type=MESH,
            )
            copy.start()
            halos.append(copy)

    for copy in loads:
        copy.wait()

    def prepare(base, size):
        at = pl.ds(base, size)
        col = lax.broadcasted_iota(jnp.int32, (size, ncol), 1)
        kq[at, :] = jnp.where(col < ncol - 1, kq[at, :] * 0.25, 0.0)
        cm[at, :] = time_step / cm[at, :]

    def prepare_block(b, carry):
        prepare(pl.multiple_of(PAD + b * last_block, 8), last_block)
        return carry

    lax.fori_loop(0, here // last_block, prepare_block, 0)

    pltpu.make_async_copy(req, passed, req_recv.at[0]).wait()

    def hand_on(t, carry):
        w = other_member(t)
        pltpu.make_async_remote_copy(
            passed.at[:, w], asked.at[my_w], req_send.at[1], req_recv.at[1],
            device_id=device_at(my_g, w), device_id_type=MESH,
        ).start()
        return carry

    lax.fori_loop(1, near, hand_on, 0)
    pltpu.make_async_copy(passed.at[:, my_w], asked.at[my_w], req_recv.at[1]).start()
    hand_sets_on()

    for copy in halos:
        copy.wait()
    prepare(PAD - HALO, HALO)
    prepare(PAD + here, HALO)

    @pl.when(me == 0)
    def _():
        kq[front, :] = jnp.zeros((HALO, ncol), jnp.float32)

    @pl.when(me == n - 1)
    def _():
        tail = pl.ds(PAD + here - HALO, HALO)
        row = lax.broadcasted_iota(jnp.int32, (HALO, ncol), 0)
        kq[tail, :] = jnp.where(row == HALO - 1, 0.0, kq[tail, :])

    blocks = (here + 2 * HALO) // block
    assert blocks * block == here + 2 * HALO

    def weights(b, carry):
        base = pl.multiple_of(PAD - HALO + b * block, 8)
        both = kq[pl.ds(base, block), :] + kq[pl.ds(base - 1, block), :]
        w4[pl.ds(base, block), :] = 4.0 * (both + prev_col(both))
        return carry

    lax.fori_loop(0, blocks, weights, 0)

    def free_step(src, d_to, v_to, first_row, count, size):
        def part(b, carry):
            base = pl.multiple_of(first_row + b * size, 8)
            for i in range(size // 8 + 1):
                at = pl.ds(base + 8 * (i - 1), 8)
                below = pl.ds(base + 8 * (i - 1) + 1, 8)
                k_here = kq[at, :]
                if i:
                    w_here, cm_here = w4[at, :], cm[at, :]
                for c in range(3):
                    d = src[c, at, :]
                    box = d + src[c, below, :]
                    t = k_here * (box + next_col(box))
                    term[c, 8 * i : 8 * (i + 1), :] = t
                    if i:
                        t = t + term[c, 8 * i - 1 : 8 * i + 7, :]
                        force = t + prev_col(t) - w_here * d
                        v = vel[c, at, :] + cm_here * force
                        v_to(base, size)[c, 8 * (i - 1) : 8 * i, :] = v
                        d_to(base, size)[c, 8 * (i - 1) : 8 * i, :] = d + time_step * v
            return carry

        lax.fori_loop(0, count, part, 0)

    def same_rows(ref):
        return lambda base, size: ref.at[:, pl.ds(base, size)]

    def own_rows(ref):
        return lambda base, size: ref.at[:, pl.ds(pl.multiple_of(base - PAD, 8), size)]

    part_one = blocks // 2
    free_step(d0, same_rows(d1), same_rows(vel), PAD - HALO, part_one, block)

    pltpu.make_async_copy(asked, asked, req_recv.at[1]).wait()
    asked_rows[...] = jnp.clip(asked[...].reshape(n, 128).T[:lists_rows], 0, patches - 1)
    to_scalar = pltpu.make_async_copy(asked_rows, asked_s, small_sem.at[1])
    to_scalar.start()
    free_step(d0, same_rows(d1), same_rows(vel), PAD - HALO + part_one * block, blocks - part_one, block)
    to_scalar.wait()
    idx_copy.wait()

    for copy in second_legs:
        copy.wait_recv()

    def gather(axis, w, g, dst, at):
        copies = (die_x, die_y, die_z)[axis]
        for i in range(lines[axis] * cap):
            dst[at + i] = copies[i // cap, asked_s[firsts[axis] + i, w * far + g]]

    def line_of(axis, y, x, w):
        return (y * near + w, x * near + w, (y * n_sub + x) * CORES + lax.rem(w, CORES))[axis]

    def planes_at(axis, y, x, w):
        return (axis * n + line_of(axis, y, x, w) * lines[axis]) * cap

    def reply(axis, y, x, w, wanted):
        g = y * n_sub + x

        @pl.when(wanted & ((g != my_g) | (w != my_w)))
        def _():
            size = lines[axis] * cap
            there, here_at = planes_at(axis, y, x, w), planes_at(axis, my_y, my_x, my_w)
            gather(axis, w, g, answer, there)
            pltpu.make_async_remote_copy(
                answer.at[pl.ds(there, size)], got.at[pl.ds(here_at, size)], ans_send, ans_recv,
                device_id=device_at(g, w), device_id_type=MESH,
            ).start()

    rounds = lines[0] * CORES
    assert lines[0] == lines[1]

    def in_round(i):
        return (i >= 0) & (i < rounds)

    def reply_round(r, carry):
        for layer in range(lines[2]):
            i = r - lead * layer
            at_y = lax.rem(my_y * CORES + my_core + 3 * (i + rounds), rounds)
            at_x = lax.rem(my_x * CORES + my_core + 3 * (i + rounds), rounds)
            w_y = layer * CORES + lax.rem(at_y, CORES)
            w_x = layer * CORES + lax.rem(at_x, CORES)
            reply(0, lax.div(at_y, CORES), my_x, w_y, in_round(i))
            reply(1, my_y, lax.div(at_x, CORES), w_x, in_round(i))
        i = r - lead * my_z
        for part in range(lines[0]):
            at = lax.rem(my_g * CORES + my_core + 13 * ((i + rounds) * lines[0] + part), far * CORES)
            g = lax.div(at, CORES)
            reply(2, lax.div(g, n_sub), lax.rem(g, n_sub), my_z * CORES + lax.rem(at, CORES), in_round(i))
        return carry

    assert lead * (lines[2] - 1) <= rounds
    lax.fori_loop(0, rounds + lead * (lines[2] - 1), reply_round, 0)
    for axis in range(3):
        gather(axis, my_w, my_g, got, planes_at(axis, my_y, my_x, my_w))

    free_step(d1, same_rows(d2), same_rows(vel), PAD - HALO, blocks, block)
    free_step(d2, own_rows(od_ref), own_rows(ov_ref), PAD, here // last_block, last_block)

    wire = pl.ds(0, (3 * n - sum(lines)) * cap)
    pltpu.make_async_copy(answer.at[wire], got.at[wire], ans_recv).wait()

    for s in range(steps):
        first_patch[s] = got[idx_s[s, 0]]
    ghost_copy = pltpu.make_async_remote_copy(
        first_patch, ghost, ghost_sem.at[0], ghost_sem.at[1],
        device_id=device(previous), device_id_type=MESH,
    )
    ghost_copy.start()

    def place(j, carry):
        for s in range(steps):
            planes[s, pl.ds(j * 4, 4), :] = got[idx_s[s, j]]
        return carry

    lax.fori_loop(0, seg, place, 0, unroll=8)

    flat = {"cm": cm, "kq": kq, "w4": w4}
    deep = {"d0": d0, "d1": d1, "d2": d2}
    chunk = width * stride

    def correct(q, carry):
        base = PAD + q * chunk

        def rows(name, o):
            at = pl.ds(base + o, width, stride=stride)
            if name in flat:
                return flat[name][at, :]
            return [deep[name][c, at, :] for c in range(3)]

        nearby = [[planes[s, pl.ds(q * width * 4 + c, width, stride=4), :] for c in range(4)] for s in range(steps)]
        u, z = contact_response(nearby, rows)
        at = pl.ds(pl.multiple_of(q * width, 8), width)
        for o in range(-2, 3):
            for c in range(3):
                share_u[o + 2, c, at, :] = u[o][c]
                share_z[o + 2, c, at, :] = z[o][c]
        return carry

    lax.fori_loop(0, seg // width, correct, 0)

    ghost_copy.wait()

    def ghost_rows(name, o):
        at = pl.ds(PAD + here + o, 1)
        if name in flat:
            return flat[name][at, :]
        return [deep[name][c, at, :] for c in range(3)]

    nearby = [[ghost[s, pl.ds(c, 1), :] for c in range(4)] for s in range(steps)]
    u, z = contact_response(nearby, ghost_rows)
    for o in (-2, -1):
        for c in range(3):
            share_u[o + 2, c, pl.ds(seg, 1), :] = u[o][c]
            share_z[o + 2, c, pl.ds(seg, 1), :] = z[o][c]

    pltpu.make_async_copy(answer.at[wire], got.at[wire], ans_send).wait()
    for copy in first_legs + second_legs:
        copy.wait_send()
    pltpu.make_async_copy(req.at[pl.ds(0, far - 1)], passed.at[pl.ds(0, far - 1)], req_send.at[0]).wait()
    pltpu.make_async_copy(asked.at[pl.ds(0, near - 1)], asked.at[pl.ds(0, near - 1)], req_send.at[1]).wait()


def add_share(parts, stride, d_ref, v_ref, share_u, share_z, od_hbm, ov_hbm, d_sum, v_sum, sem):
    here = d_ref.shape[1]
    chunk = here // parts
    width = chunk // stride
    copies = []
    for q in range(parts):
        rows = pl.ds(q * chunk, chunk)
        for a, (src, share, total, dst) in enumerate(
            ((d_ref, share_u, d_sum, od_hbm), (v_ref, share_z, v_sum, ov_hbm))
        ):
            total[:, rows, :] = src[:, rows, :]
            for o in range(-2, 3):
                at = pl.ds(q * chunk + (o + stride if o < 0 else o), width, stride=stride)
                block = pl.ds(q * width + (1 if o < 0 else 0), width)
                for c in range(3):
                    total[c, at, :] += share[o + 2, c, block, :]
            copy = pltpu.make_async_copy(total.at[:, rows], dst.at[:, rows], sem.at[a, q])
            copy.start()
            copies.append(copy)
    for copy in copies:
        copy.wait()


def body(n_dom, n_sub, displace, velocity, nodal_mass, stiffness, die_planes, owners, pairs):
    n = n_dom * n_sub
    here, ncol = displace.shape[1:]
    steps, seg = pairs.shape
    cap = max(2, 2 * seg // n)
    ext = here + 2 * PAD
    tiles = (here + 2 * HALO) // 8
    block = 8 * max(b for b in range(1, 44) if tiles % b == 0)
    last_block = 8 * max(b for b in range(1, 33) if here // 8 % b == 0)
    width = min(32, seg)
    near = min(8, n_dom // 2)
    far = n // near
    lanes = (n_sub + far // n_sub + near // CORES) * cap
    f32, i32 = jnp.float32, jnp.int32
    any_spec = pl.BlockSpec(memory_space=pl.ANY)
    vmem_spec = pl.BlockSpec(memory_space=pltpu.VMEM)
    dma = pltpu.SemaphoreType.DMA
    share = pltpu.VMEM((5, 3, seg + 8, ncol), f32)
    results = pl.pallas_call(
        functools.partial(kernel, n_dom, n_sub, cap, near, LEAD, block, last_block, width),
        out_shape=[pltpu.VMEM(displace.shape, f32)] * 2 + [share] * 2,
        in_specs=[any_spec] * 7,
        out_specs=[vmem_spec] * 4,
        scratch_shapes=[
            pltpu.VMEM((steps, 1, seg), i32),
            pltpu.VMEM((steps, seg), i32),
            pltpu.VMEM((3, ext, ncol), f32),
            pltpu.VMEM((3, ext, ncol), f32),
            pltpu.VMEM((3, ext, ncol), f32),
            pltpu.VMEM((3, ext, ncol), f32),
            pltpu.VMEM((ext, ncol), f32),
            pltpu.VMEM((ext, ncol), f32),
            pltpu.VMEM((ext, ncol), f32),
            pltpu.VMEM((n_sub,) + die_planes.shape[1:], f32),
            pltpu.VMEM((far // n_sub,) + die_planes.shape[1:], f32),
            pltpu.VMEM((near // CORES,) + die_planes.shape[1:], f32),
            pltpu.VMEM((far, near, 128), i32),
            pltpu.VMEM((far, near, 128), i32),
            pltpu.VMEM((near, far, 128), i32),
            pltpu.VMEM((-(-lanes // 8) * 8, n), i32),
            pltpu.SMEM((-(-lanes // 8) * 8, n), i32),
            pltpu.VMEM((8, seg), i32),
            pltpu.SMEM((8, seg), i32),
            pltpu.VMEM((n * steps * cap, 4, ncol), f32),
            pltpu.VMEM((n * steps * cap, 4, ncol), f32),
            pltpu.VMEM((steps, seg * 4 + 32, ncol), f32),
            pltpu.VMEM((steps, 4, ncol), f32),
            pltpu.VMEM((steps, 4, ncol), f32),
            pltpu.VMEM((3, max(block, last_block) + 8, ncol), f32),
            dma((9,)), dma((8,)), dma((8,)), dma((3, 4)), dma((3, 4)), dma((2,)), dma((2,)), dma, dma, dma((2,)), dma((2,)),
        ],
        compiler_params=pltpu.CompilerParams(
            collective_id=0, has_side_effects=True, vmem_limit_bytes=40 * 1024 * 1024
        ),
        name="stamp",
    )(*[
        pltpu.with_memory_space_constraint(x, pltpu.HBM)
        for x in (jnp.swapaxes(owners, 1, 2), pairs, displace, velocity, nodal_mass, stiffness, die_planes)
    ])
    parts = 8 if seg >= 64 else 2
    return pl.pallas_call(
        functools.partial(add_share, parts, here // seg),
        out_shape=[jax.ShapeDtypeStruct(displace.shape, f32)] * 2,
        in_specs=[vmem_spec] * 4,
        out_specs=[any_spec] * 2,
        scratch_shapes=[pltpu.VMEM(displace.shape, f32), pltpu.VMEM(displace.shape, f32), dma((2, parts))],
        compiler_params=pltpu.CompilerParams(vmem_limit_bytes=40 * 1024 * 1024),
        name="add_share",
    )(*[pltpu.with_memory_space_constraint(x, pltpu.VMEM) for x in results])


def solution(mesh):
    in_specs = (
        P(None, ("dom", "sub"), None),
        P(None, ("dom", "sub"), None),
        P(("dom", "sub"), None),
        P(("dom", "sub"), None),
        P(None, ("dom", "sub"), None, None),
        P(None, ("dom", "sub"), None),
        P(None, ("dom", "sub")),
    )
    out_specs = (P(None, ("dom", "sub"), None), P(None, ("dom", "sub"), None))
    run = functools.partial(body, mesh.shape["dom"], mesh.shape["sub"])
    return jax.shard_map(run, mesh=mesh, in_specs=in_specs, out_specs=out_specs, check_vma=False)
```

```python
import functools

import jax
import jax.numpy as jnp
from jax import lax
from jax.experimental import pallas as pl
from jax.experimental.pallas import tpu as pltpu
from jax.sharding import PartitionSpec as P

STEPS = 3
time_step = 0.2
penalty = 1.0

MESH = pl.DeviceIdType.MESH
PAD = 16
HALO = 8
CORES = 2
LEAD = 1


def next_col(x):
    return pltpu.roll(x, x.shape[-1] - 1, x.ndim - 1)


def prev_col(x):
    return pltpu.roll(x, 1, x.ndim - 1)


def contact(planes, position):
    normal, height = planes[:3], planes[3]
    depth = height - (normal[0] * position[0] + normal[1] * position[1] + normal[2] * position[2])
    push = penalty * jnp.maximum(depth, 0.0)
    return [push * normal[c] for c in range(3)]


def contact_response(planes, rows):
    cm = {o: rows("cm", o) for o in range(-2, 3)}
    kq = {o: rows("kq", o) for o in range(-2, 2)}
    w4 = {o: rows("w4", o) for o in range(-1, 2)}
    u = {}
    z = {}
    for step in range(STEPS):
        free = rows("d%d" % step, 0)
        position = [free[c] + u[0][c] if step else free[c] for c in range(3)]
        push = contact(planes[step], position)
        new_u, new_z = {}, {}
        for o in range(-step, step + 1):
            new_u[o], new_z[o] = [], []
        for c in range(3):
            spread = {}
            for o in range(-step, step):
                parts = [u[r][c] for r in (o, o + 1) if r in u]
                box = parts[0] if len(parts) == 1 else parts[0] + parts[1]
                t = kq[o] * (box + next_col(box))
                spread[o] = t + prev_col(t)
            for o in range(-step, step + 1):
                terms = [spread[r] for r in (o - 1, o) if r in spread]
                if o in u:
                    terms.append(-(w4[o] * u[o][c]))
                if o == 0:
                    terms.append(push[c])
                force = terms[0]
                for term in terms[1:]:
                    force = force + term
                dz = cm[o] * force
                zc = z[o][c] + dz if o in z else dz
                uc = time_step * zc
                if o in u:
                    uc = u[o][c] + uc
                new_z[o].append(zc)
                new_u[o].append(uc)
        u, z = new_u, new_z
    return u, z


def kernel(
    n_dom, n_sub, cap, near, lead, block, last_block, width,
    own_hbm, pair_hbm, d_hbm, v_hbm, m_hbm, k_hbm, die_hbm,
    od_ref, ov_ref, share_u, share_z,
    own_ref, pair_ref, d0, d1, d2, vel, cm, kq, w4, die_x, die_y, die_z, req, passed, asked, asked_rows, asked_s, idx, idx_s, answer, got, planes, first_patch, ghost, term,
    load_sem, halo_send, halo_recv, die_send, die_recv, req_send, req_recv, ans_send, ans_recv, small_sem, ghost_sem,
):
    n = n_dom * n_sub
    steps, seg = pair_hbm.shape
    here = d_hbm.shape[1]
    stride = here // seg
    ncol = d_hbm.shape[2]
    assert steps == 3
    lists_rows = asked_s.shape[0]
    patches = die_hbm.shape[1]
    dom, sub = lax.axis_index("dom"), lax.axis_index("sub")
    me = dom * n_sub + sub

    def device(i):
        return (lax.div(i, n_sub), lax.rem(i, n_sub))

    far = n // near
    lines = (n_sub, far // n_sub, near // CORES)
    my_w = lax.rem(dom, near)
    my_x, my_y, my_z, my_core = sub, lax.div(dom, near), lax.div(my_w, CORES), lax.rem(my_w, CORES)
    my_g = my_y * n_sub + my_x

    def device_at(g, w):
        return (lax.div(g, n_sub) * near + w, lax.rem(g, n_sub))

    def other_group(t):
        return lax.rem(my_g + t, far)

    def other_member(t):
        return lax.rem(my_w + t, near)

    following, previous = lax.rem(me + 1, n), lax.rem(me + n - 1, n)

    inner = pl.ds(PAD, here)
    lists = [
        pltpu.make_async_copy(own_hbm, own_ref, load_sem.at[5]),
        pltpu.make_async_copy(pair_hbm, pair_ref, load_sem.at[6]),
    ]
    loads = [
        pltpu.make_async_copy(d_hbm, d0.at[:, inner], load_sem.at[0]),
        pltpu.make_async_copy(v_hbm, vel.at[:, inner], load_sem.at[1]),
        pltpu.make_async_copy(m_hbm, cm.at[inner], load_sem.at[2]),
        pltpu.make_async_copy(k_hbm, kq.at[inner], load_sem.at[3]),
        pltpu.make_async_copy(die_hbm.at[0], die_x.at[my_x], load_sem.at[4]),
        pltpu.make_async_copy(die_hbm.at[1], die_y.at[my_y], load_sem.at[7]),
        pltpu.make_async_copy(die_hbm.at[2], die_z.at[0], load_sem.at[8]),
    ]
    for copy in lists + loads:
        copy.start()

    barrier = pltpu.get_barrier_semaphore()

    def greet(to):
        pl.semaphore_signal(barrier, inc=1, device_id=to, device_id_type=MESH)

    def greet_groups(t, carry):
        greet(device_at(other_group(t), my_w))
        return carry

    def greet_members(t, carry):
        greet(device_at(my_g, other_member(t)))
        return carry

    lax.fori_loop(1, far, greet_groups, 0)
    lax.fori_loop(1, near, greet_members, 0)
    greet(device(following))
    greet(device(previous))

    pl.semaphore_wait(barrier, far + near)

    sets = (die_x, die_y, die_z)
    half = patches // 2

    def along(axis, t):
        return lax.rem((my_x, my_y, my_z)[axis] + t, lines[axis])

    def device_along(axis, t):
        there = along(axis, t)
        return (
            device_at(my_y * n_sub + there, my_w),
            device_at(there * n_sub + my_x, my_w),
            device_at(my_g, there * CORES + my_core),
        )[axis]

    def set_of(axis, t, seen):
        return (t - seen) % lines[axis] if axis == 2 else along(axis, t)

    def set_copy(axis, t, to, src, rows, number):
        place = sets[axis].at[set_of(axis, t, to), rows]
        return pltpu.make_async_remote_copy(
            src, place, die_send.at[axis, number], die_recv.at[axis, number],
            device_id=device_along(axis, to), device_id_type=MESH,
        )

    first_legs, second_legs = [], []
    every = pl.ds(0, patches)

    def send_set(axis):
        count = lines[axis]
        assert count in (2, 4)
        for number, to in enumerate((1, count - 1)[: count - 2 or 1]):
            copy = set_copy(axis, 0, to, die_hbm.at[axis], every, number)
            copy.start()
            first_legs.append(copy)

    send_set(2)

    def hand_sets_on():
        for copy in first_legs:
            copy.wait_recv()
        for axis, count in enumerate(lines):
            if count == 4:
                for number, (came, to, rows) in enumerate(((3, 1, pl.ds(0, half)), (1, 3, pl.ds(half, half)))):
                    src = sets[axis].at[set_of(axis, came, 0), rows]
                    copy = set_copy(axis, came, to, src, rows, 2 + number)
                    copy.start()
                    second_legs.append(copy)

    lane_of = lax.broadcasted_iota(jnp.int32, (n, 128), 1)
    row = lax.broadcasted_iota(jnp.int32, (n, seg), 0)
    row_g, row_w = lax.div(row, near), lax.rem(row, near)
    owner_of = (lax.div(row_g, n_sub) * near + row_w) * n_sub + lax.rem(row_g, n_sub)
    before = lax.broadcasted_iota(jnp.int32, (seg, seg), 0) < lax.broadcasted_iota(jnp.int32, (seg, seg), 1)
    table = jnp.zeros((n, 128), jnp.int32)
    places = []
    for copy in lists:
        copy.wait()
    for s in range(steps):
        own = own_ref[s]
        wide = jnp.broadcast_to(own, (seg, seg))
        same = (wide == wide.T) & before
        slot = jnp.minimum(jnp.sum(same.astype(jnp.int32), axis=0, keepdims=True), cap - 1)
        own_dom, own_x = lax.div(own, n_sub), lax.rem(own, n_sub)
        own_y, own_w = lax.div(own_dom, near), lax.rem(own_dom, near)
        own_z, own_core = lax.div(own_w, CORES), lax.rem(own_w, CORES)
        line, at_line = (
            (own_y * near + own_w, own_x),
            (own_x * near + own_w, own_y),
            ((own_y * n_sub + own_x) * CORES + own_core, lax.rem(own_z + (lines[2] - my_z), lines[2])),
        )[s]
        places.append((s * n + line * lines[s] + at_line) * cap + slot)
        pair = pair_ref[s : s + 1, :]
        mine = owner_of == own
        for k in range(cap):
            chosen = jnp.where(mine & (slot == k), pair, 0)
            table = jnp.where(lane_of == s * cap + k, jnp.sum(chosen, axis=1, keepdims=True), table)
    by_group = [table[near * g : near * (g + 1)] for g in range(far)]
    lane = lax.broadcasted_iota(jnp.int32, (near, 128), 1)

    def lanes_of(s, value, to):
        value = jnp.where((lane >= s * cap) & (lane < (s + 1) * cap), value, 0)
        shift = to - s * cap
        return pltpu.roll(value, shift, 1) if shift else value

    firsts = (0, lines[0] * cap, (lines[0] + lines[1]) * cap)
    along_x = [
        sum(lanes_of(0, by_group[y * n_sub + x], firsts[0] + x * cap) for x in range(lines[0])) for y in range(lines[1])
    ]
    along_y = [
        sum(lanes_of(1, by_group[y * n_sub + x], firsts[1] + y * cap) for y in range(lines[1])) for x in range(lines[0])
    ]
    for g in range(far):
        along_z = 0
        for z in range(lines[2]):
            turned = pltpu.roll(by_group[g], near - z * CORES, 0) if z else by_group[g]
            along_z = along_z + lanes_of(2, turned, firsts[2] + z * cap)
        req[g] = along_x[g // n_sub] + along_y[g % n_sub] + along_z
    def ask(t, carry):
        g = other_group(t)
        pltpu.make_async_remote_copy(
            req.at[g], passed.at[my_g], req_send.at[0], req_recv.at[0],
            device_id=device_at(g, my_w), device_id_type=MESH,
        ).start()
        return carry

    lax.fori_loop(1, far, ask, 0)
    send_set(0)
    send_set(1)
    pltpu.make_async_copy(req.at[my_g], passed.at[my_g], req_recv.at[0]).start()

    for s in range(steps):
        idx[s : s + 1, :] = places[s]
    idx_copy = pltpu.make_async_copy(idx, idx_s, small_sem.at[0])
    idx_copy.start()

    first, last = pl.ds(0, HALO), pl.ds(here - HALO, HALO)
    front, back = pl.ds(PAD - HALO, HALO), pl.ds(PAD + here, HALO)
    halos = []
    for a, (src, dst) in enumerate(((d_hbm, d0), (v_hbm, vel), (m_hbm, cm), (k_hbm, kq))):
        three = len(src.shape) == 3
        for side, (rows, place, to) in enumerate(((last, front, following), (first, back, previous))):
            copy = pltpu.make_async_remote_copy(
                src.at[:, rows] if three else src.at[rows],
                dst.at[:, place] if three else dst.at[place],
                halo_send.at[2 * a + side], halo_recv.at[2 * a + side],
                device_id=device(to), device_id_type=MESH,
            )
            copy.start()
            halos.append(copy)

    for copy in loads:
        copy.wait()

    def prepare(base, size):
        at = pl.ds(base, size)
        col = lax.broadcasted_iota(jnp.int32, (size, ncol), 1)
        kq[at, :] = jnp.where(col < ncol - 1, kq[at, :] * 0.25, 0.0)
        cm[at, :] = time_step / cm[at, :]

    def prepare_block(b, carry):
        prepare(pl.multiple_of(PAD + b * last_block, 8), last_block)
        return carry

    lax.fori_loop(0, here // last_block, prepare_block, 0)

    pltpu.make_async_copy(req, passed, req_recv.at[0]).wait()

    def hand_on(t, carry):
        w = other_member(t)
        pltpu.make_async_remote_copy(
            passed.at[:, w], asked.at[my_w], req_send.at[1], req_recv.at[1],
            device_id=device_at(my_g, w), device_id_type=MESH,
        ).start()
        return carry

    lax.fori_loop(1, near, hand_on, 0)
    pltpu.make_async_copy(passed.at[:, my_w], asked.at[my_w], req_recv.at[1]).start()
    hand_sets_on()

    for copy in halos:
        copy.wait()
    prepare(PAD - HALO, HALO)
    prepare(PAD + here, HALO)

    @pl.when(me == 0)
    def _():
        kq[front, :] = jnp.zeros((HALO, ncol), jnp.float32)

    @pl.when(me == n - 1)
    def _():
        tail = pl.ds(PAD + here - HALO, HALO)
        row = lax.broadcasted_iota(jnp.int32, (HALO, ncol), 0)
        kq[tail, :] = jnp.where(row == HALO - 1, 0.0, kq[tail, :])

    blocks = (here + 2 * HALO) // block
    assert blocks * block == here + 2 * HALO

    def weights(b, carry):
        base = pl.multiple_of(PAD - HALO + b * block, 8)
        both = kq[pl.ds(base, block), :] + kq[pl.ds(base - 1, block), :]
        w4[pl.ds(base, block), :] = 4.0 * (both + prev_col(both))
        return carry

    lax.fori_loop(0, blocks, weights, 0)

    def free_step(src, d_to, v_to, first_row, count, size):
        def part(b, carry):
            base = pl.multiple_of(first_row + b * size, 8)
            for i in range(size // 8 + 1):
                at = pl.ds(base + 8 * (i - 1), 8)
                below = pl.ds(base + 8 * (i - 1) + 1, 8)
                for c in range(3):
                    d = src[c, at, :]
                    box = d + src[c, below, :]
                    t = kq[at, :] * (box + next_col(box))
                    term[c, 8 * i : 8 * (i + 1), :] = t
                    if i:
                        t = t + term[c, 8 * i - 1 : 8 * i + 7, :]
                        force = t + prev_col(t) - w4[at, :] * d
                        v = vel[c, at, :] + cm[at, :] * force
                        v_to(base, size)[c, 8 * (i - 1) : 8 * i, :] = v
                        d_to(base, size)[c, 8 * (i - 1) : 8 * i, :] = d + time_step * v
            return carry

        lax.fori_loop(0, count, part, 0)

    def same_rows(ref):
        return lambda base, size: ref.at[:, pl.ds(base, size)]

    def own_rows(ref):
        return lambda base, size: ref.at[:, pl.ds(pl.multiple_of(base - PAD, 8), size)]

    free_step(d0, same_rows(d1), same_rows(vel), PAD - HALO, blocks, block)

    pltpu.make_async_copy(asked, asked, req_recv.at[1]).wait()
    asked_rows[...] = jnp.clip(asked[...].reshape(n, 128).T[:lists_rows], 0, patches - 1)
    to_scalar = pltpu.make_async_copy(asked_rows, asked_s, small_sem.at[1])
    to_scalar.start()
    to_scalar.wait()
    idx_copy.wait()

    for copy in second_legs:
        copy.wait_recv()

    def gather(axis, w, g, dst, at):
        copies = (die_x, die_y, die_z)[axis]
        for i in range(lines[axis] * cap):
            dst[at + i] = copies[i // cap, asked_s[firsts[axis] + i, w * far + g]]

    def line_of(axis, y, x, w):
        return (y * near + w, x * near + w, (y * n_sub + x) * CORES + lax.rem(w, CORES))[axis]

    def planes_at(axis, y, x, w):
        return (axis * n + line_of(axis, y, x, w) * lines[axis]) * cap

    def reply(axis, y, x, w, wanted):
        g = y * n_sub + x

        @pl.when(wanted & ((g != my_g) | (w != my_w)))
        def _():
            size = lines[axis] * cap
            there, here_at = planes_at(axis, y, x, w), planes_at(axis, my_y, my_x, my_w)
            gather(axis, w, g, answer, there)
            pltpu.make_async_remote_copy(
                answer.at[pl.ds(there, size)], got.at[pl.ds(here_at, size)], ans_send, ans_recv,
                device_id=device_at(g, w), device_id_type=MESH,
            ).start()

    rounds = lines[0] * CORES
    assert lines[0] == lines[1]

    def in_round(i):
        return (i >= 0) & (i < rounds)

    def reply_round(r, carry):
        for layer in range(lines[2]):
            i = r - lead * layer
            at_y = lax.rem(my_y * CORES + my_core + 3 * (i + rounds), rounds)
            at_x = lax.rem(my_x * CORES + my_core + 3 * (i + rounds), rounds)
            w_y = layer * CORES + lax.rem(at_y, CORES)
            w_x = layer * CORES + lax.rem(at_x, CORES)
            reply(0, lax.div(at_y, CORES), my_x, w_y, in_round(i))
            reply(1, my_y, lax.div(at_x, CORES), w_x, in_round(i))
        i = r - lead * my_z
        for part in range(lines[0]):
            at = lax.rem(my_g * CORES + my_core + 13 * ((i + rounds) * lines[0] + part), far * CORES)
            g = lax.div(at, CORES)
            reply(2, lax.div(g, n_sub), lax.rem(g, n_sub), my_z * CORES + lax.rem(at, CORES), in_round(i))
        return carry

    assert lead * (lines[2] - 1) <= rounds
    lax.fori_loop(0, rounds + lead * (lines[2] - 1), reply_round, 0)
    for axis in range(3):
        gather(axis, my_w, my_g, got, planes_at(axis, my_y, my_x, my_w))

    free_step(d1, same_rows(d2), same_rows(vel), PAD - HALO, blocks, block)
    free_step(d2, own_rows(od_ref), own_rows(ov_ref), PAD, here // last_block, last_block)

    wire = pl.ds(0, (3 * n - sum(lines)) * cap)
    pltpu.make_async_copy(answer.at[wire], got.at[wire], ans_recv).wait()

    for s in range(steps):
        first_patch[s] = got[idx_s[s, 0]]
    ghost_copy = pltpu.make_async_remote_copy(
        first_patch, ghost, ghost_sem.at[0], ghost_sem.at[1],
        device_id=device(previous), device_id_type=MESH,
    )
    ghost_copy.start()

    def place(j, carry):
        for s in range(steps):
            planes[s, pl.ds(j * 4, 4), :] = got[idx_s[s, j]]
        return carry

    lax.fori_loop(0, seg, place, 0, unroll=8)

    flat = {"cm": cm, "kq": kq, "w4": w4}
    deep = {"d0": d0, "d1": d1, "d2": d2}
    chunk = width * stride

    def correct(q, carry):
        base = PAD + q * chunk

        def rows(name, o):
            at = pl.ds(base + o, width, stride=stride)
            if name in flat:
                return flat[name][at, :]
            return [deep[name][c, at, :] for c in range(3)]

        nearby = [[planes[s, pl.ds(q * width * 4 + c, width, stride=4), :] for c in range(4)] for s in range(steps)]
        u, z = contact_response(nearby, rows)
        at = pl.ds(pl.multiple_of(q * width, 8), width)
        for o in range(-2, 3):
            for c in range(3):
                share_u[o + 2, c, at, :] = u[o][c]
                share_z[o + 2, c, at, :] = z[o][c]
        return carry

    lax.fori_loop(0, seg // width, correct, 0)

    ghost_copy.wait()

    def ghost_rows(name, o):
        at = pl.ds(PAD + here + o, 1)
        if name in flat:
            return flat[name][at, :]
        return [deep[name][c, at, :] for c in range(3)]

    nearby = [[ghost[s, pl.ds(c, 1), :] for c in range(4)] for s in range(steps)]
    u, z = contact_response(nearby, ghost_rows)
    for o in (-2, -1):
        for c in range(3):
            share_u[o + 2, c, pl.ds(seg, 1), :] = u[o][c]
            share_z[o + 2, c, pl.ds(seg, 1), :] = z[o][c]

    pltpu.make_async_copy(answer.at[wire], got.at[wire], ans_send).wait()
    for copy in first_legs + second_legs:
        copy.wait_send()
    pltpu.make_async_copy(req.at[pl.ds(0, far - 1)], passed.at[pl.ds(0, far - 1)], req_send.at[0]).wait()
    pltpu.make_async_copy(asked.at[pl.ds(0, near - 1)], asked.at[pl.ds(0, near - 1)], req_send.at[1]).wait()


def add_share(parts, stride, d_ref, v_ref, share_u, share_z, od_hbm, ov_hbm, d_sum, v_sum, sem):
    here = d_ref.shape[1]
    chunk = here // parts
    width = chunk // stride
    copies = []
    for q in range(parts):
        rows = pl.ds(q * chunk, chunk)
        for a, (src, share, total, dst) in enumerate(
            ((d_ref, share_u, d_sum, od_hbm), (v_ref, share_z, v_sum, ov_hbm))
        ):
            total[:, rows, :] = src[:, rows, :]
            for o in range(-2, 3):
                at = pl.ds(q * chunk + (o + stride if o < 0 else o), width, stride=stride)
                block = pl.ds(q * width + (1 if o < 0 else 0), width)
                for c in range(3):
                    total[c, at, :] += share[o + 2, c, block, :]
            copy = pltpu.make_async_copy(total.at[:, rows], dst.at[:, rows], sem.at[a, q])
            copy.start()
            copies.append(copy)
    for copy in copies:
        copy.wait()


def body(n_dom, n_sub, displace, velocity, nodal_mass, stiffness, die_planes, owners, pairs):
    n = n_dom * n_sub
    here, ncol = displace.shape[1:]
    steps, seg = pairs.shape
    cap = max(2, 2 * seg // n)
    ext = here + 2 * PAD
    tiles = (here + 2 * HALO) // 8
    block = 8 * max(b for b in range(1, 44) if tiles % b == 0)
    last_block = 8 * max(b for b in range(1, 33) if here // 8 % b == 0)
    width = min(32, seg)
    near = min(8, n_dom // 2)
    far = n // near
    lanes = (n_sub + far // n_sub + near // CORES) * cap
    f32, i32 = jnp.float32, jnp.int32
    any_spec = pl.BlockSpec(memory_space=pl.ANY)
    vmem_spec = pl.BlockSpec(memory_space=pltpu.VMEM)
    dma = pltpu.SemaphoreType.DMA
    share = pltpu.VMEM((5, 3, seg + 8, ncol), f32)
    results = pl.pallas_call(
        functools.partial(kernel, n_dom, n_sub, cap, near, LEAD, block, last_block, width),
        out_shape=[pltpu.VMEM(displace.shape, f32)] * 2 + [share] * 2,
        in_specs=[any_spec] * 7,
        out_specs=[vmem_spec] * 4,
        scratch_shapes=[
            pltpu.VMEM((steps, 1, seg), i32),
            pltpu.VMEM((steps, seg), i32),
            pltpu.VMEM((3, ext, ncol), f32),
            pltpu.VMEM((3, ext, ncol), f32),
            pltpu.VMEM((3, ext, ncol), f32),
            pltpu.VMEM((3, ext, ncol), f32),
            pltpu.VMEM((ext, ncol), f32),
            pltpu.VMEM((ext, ncol), f32),
            pltpu.VMEM((ext, ncol), f32),
            pltpu.VMEM((n_sub,) + die_planes.shape[1:], f32),
            pltpu.VMEM((far // n_sub,) + die_planes.shape[1:], f32),
            pltpu.VMEM((near // CORES,) + die_planes.shape[1:], f32),
            pltpu.VMEM((far, near, 128), i32),
            pltpu.VMEM((far, near, 128), i32),
            pltpu.VMEM((near, far, 128), i32),
            pltpu.VMEM((-(-lanes // 8) * 8, n), i32),
            pltpu.SMEM((-(-lanes // 8) * 8, n), i32),
            pltpu.VMEM((8, seg), i32),
            pltpu.SMEM((8, seg), i32),
            pltpu.VMEM((n * steps * cap, 4, ncol), f32),
            pltpu.VMEM((n * steps * cap, 4, ncol), f32),
            pltpu.VMEM((steps, seg * 4 + 32, ncol), f32),
            pltpu.VMEM((steps, 4, ncol), f32),
            pltpu.VMEM((steps, 4, ncol), f32),
            pltpu.VMEM((3, max(block, last_block) + 8, ncol), f32),
            dma((9,)), dma((8,)), dma((8,)), dma((3, 4)), dma((3, 4)), dma((2,)), dma((2,)), dma, dma, dma((2,)), dma((2,)),
        ],
        compiler_params=pltpu.CompilerParams(
            collective_id=0, has_side_effects=True, vmem_limit_bytes=40 * 1024 * 1024
        ),
        name="stamp",
    )(*[
        pltpu.with_memory_space_constraint(x, pltpu.HBM)
        for x in (jnp.swapaxes(owners, 1, 2), pairs, displace, velocity, nodal_mass, stiffness, die_planes)
    ])
    parts = 8 if seg >= 64 else 2
    return pl.pallas_call(
        functools.partial(add_share, parts, here // seg),
        out_shape=[jax.ShapeDtypeStruct(displace.shape, f32)] * 2,
        in_specs=[vmem_spec] * 4,
        out_specs=[any_spec] * 2,
        scratch_shapes=[pltpu.VMEM(displace.shape, f32), pltpu.VMEM(displace.shape, f32), dma((2, parts))],
        compiler_params=pltpu.CompilerParams(vmem_limit_bytes=40 * 1024 * 1024),
        name="add_share",
    )(*[pltpu.with_memory_space_constraint(x, pltpu.VMEM) for x in results])


def solution(mesh):
    in_specs = (
        P(None, ("dom", "sub"), None),
        P(None, ("dom", "sub"), None),
        P(("dom", "sub"), None),
        P(("dom", "sub"), None),
        P(None, ("dom", "sub"), None, None),
        P(None, ("dom", "sub"), None),
        P(None, ("dom", "sub")),
    )
    out_specs = (P(None, ("dom", "sub"), None), P(None, ("dom", "sub"), None))
    run = functools.partial(body, mesh.shape["dom"], mesh.shape["sub"])
    return jax.shard_map(run, mesh=mesh, in_specs=in_specs, out_specs=out_specs, check_vma=False)
```

```python
import functools

import jax
import jax.numpy as jnp
from jax import lax
from jax.experimental import pallas as pl
from jax.experimental.pallas import tpu as pltpu
from jax.sharding import PartitionSpec as P

STEPS = 3
time_step = 0.2
penalty = 1.0

MESH = pl.DeviceIdType.MESH
PAD = 16
HALO = 8
CORES = 2
LEAD = 1


def next_col(x):
    return pltpu.roll(x, x.shape[-1] - 1, x.ndim - 1)


def prev_col(x):
    return pltpu.roll(x, 1, x.ndim - 1)


def contact(planes, position):
    normal, height = planes[:3], planes[3]
    depth = height - (normal[0] * position[0] + normal[1] * position[1] + normal[2] * position[2])
    push = penalty * jnp.maximum(depth, 0.0)
    return [push * normal[c] for c in range(3)]


def contact_response(planes, rows):
    cm = {o: rows("cm", o) for o in range(-2, 3)}
    kq = {o: rows("kq", o) for o in range(-2, 2)}
    w4 = {o: rows("w4", o) for o in range(-1, 2)}
    u = {}
    z = {}
    for step in range(STEPS):
        free = rows("d%d" % step, 0)
        position = [free[c] + u[0][c] if step else free[c] for c in range(3)]
        push = contact(planes[step], position)
        new_u, new_z = {}, {}
        for o in range(-step, step + 1):
            new_u[o], new_z[o] = [], []
        for c in range(3):
            spread = {}
            for o in range(-step, step):
                parts = [u[r][c] for r in (o, o + 1) if r in u]
                box = parts[0] if len(parts) == 1 else parts[0] + parts[1]
                t = kq[o] * (box + next_col(box))
                spread[o] = t + prev_col(t)
            for o in range(-step, step + 1):
                terms = [spread[r] for r in (o - 1, o) if r in spread]
                if o in u:
                    terms.append(-(w4[o] * u[o][c]))
                if o == 0:
                    terms.append(push[c])
                force = terms[0]
                for term in terms[1:]:
                    force = force + term
                dz = cm[o] * force
                zc = z[o][c] + dz if o in z else dz
                uc = time_step * zc
                if o in u:
                    uc = u[o][c] + uc
                new_z[o].append(zc)
                new_u[o].append(uc)
        u, z = new_u, new_z
    return u, z


def kernel(
    n_dom, n_sub, cap, near, lead, block, last_block, width,
    own_hbm, pair_hbm, d_hbm, v_hbm, m_hbm, k_hbm, die_hbm,
    od_ref, ov_ref, share_u, share_z,
    own_ref, pair_ref, d0, d1, d2, vel, cm, kq, w4, die_x, die_y, die_z, req, passed, asked, asked_rows, asked_s, idx, idx_s, answer, got, planes, first_patch, ghost, term,
    load_sem, halo_send, halo_recv, die_send, die_recv, req_send, req_recv, ans_send, ans_recv, small_sem, ghost_sem,
):
    n = n_dom * n_sub
    steps, seg = pair_hbm.shape
    here = d_hbm.shape[1]
    stride = here // seg
    ncol = d_hbm.shape[2]
    assert steps == 3
    lists_rows = asked_s.shape[0]
    patches = die_hbm.shape[1]
    dom, sub = lax.axis_index("dom"), lax.axis_index("sub")
    me = dom * n_sub + sub

    def device(i):
        return (lax.div(i, n_sub), lax.rem(i, n_sub))

    far = n // near
    lines = (n_sub, far // n_sub, near // CORES)
    my_w = lax.rem(dom, near)
    my_x, my_y, my_z, my_core = sub, lax.div(dom, near), lax.div(my_w, CORES), lax.rem(my_w, CORES)
    my_g = my_y * n_sub + my_x

    def device_at(g, w):
        return (lax.div(g, n_sub) * near + w, lax.rem(g, n_sub))

    def other_group(t):
        return lax.rem(my_g + t, far)

    def other_member(t):
        return lax.rem(my_w + t, near)

    following, previous = lax.rem(me + 1, n), lax.rem(me + n - 1, n)

    inner = pl.ds(PAD, here)
    lists = [
        pltpu.make_async_copy(own_hbm, own_ref, load_sem.at[5]),
        pltpu.make_async_copy(pair_hbm, pair_ref, load_sem.at[6]),
    ]
    loads = [
        pltpu.make_async_copy(d_hbm, d0.at[:, inner], load_sem.at[0]),
        pltpu.make_async_copy(v_hbm, vel.at[:, inner], load_sem.at[1]),
        pltpu.make_async_copy(m_hbm, cm.at[inner], load_sem.at[2]),
        pltpu.make_async_copy(k_hbm, kq.at[inner], load_sem.at[3]),
        pltpu.make_async_copy(die_hbm.at[0], die_x.at[my_x], load_sem.at[4]),
        pltpu.make_async_copy(die_hbm.at[1], die_y.at[my_y], load_sem.at[7]),
        pltpu.make_async_copy(die_hbm.at[2], die_z.at[0], load_sem.at[8]),
    ]
    for copy in lists + loads:
        copy.start()

    barrier = pltpu.get_barrier_semaphore()

    def greet(to):
        pl.semaphore_signal(barrier, inc=1, device_id=to, device_id_type=MESH)

    def greet_groups(t, carry):
        greet(device_at(other_group(t), my_w))
        return carry

    def greet_members(t, carry):
        greet(device_at(my_g, other_member(t)))
        return carry

    lax.fori_loop(1, far, greet_groups, 0)
    lax.fori_loop(1, near, greet_members, 0)
    greet(device(following))
    greet(device(previous))

    pl.semaphore_wait(barrier, far + near)

    sets = (die_x, die_y, die_z)
    half = patches // 2

    def along(axis, t):
        return lax.rem((my_x, my_y, my_z)[axis] + t, lines[axis])

    def device_along(axis, t):
        there = along(axis, t)
        return (
            device_at(my_y * n_sub + there, my_w),
            device_at(there * n_sub + my_x, my_w),
            device_at(my_g, there * CORES + my_core),
        )[axis]

    def set_of(axis, t, seen):
        return (t - seen) % lines[axis] if axis == 2 else along(axis, t)

    def set_copy(axis, t, to, src, rows, number):
        place = sets[axis].at[set_of(axis, t, to), rows]
        return pltpu.make_async_remote_copy(
            src, place, die_send.at[axis, number], die_recv.at[axis, number],
            device_id=device_along(axis, to), device_id_type=MESH,
        )

    first_legs, second_legs = [], []
    every = pl.ds(0, patches)

    def send_set(axis):
        count = lines[axis]
        assert count in (2, 4)
        for number, to in enumerate((1, count - 1)[: count - 2 or 1]):
            copy = set_copy(axis, 0, to, die_hbm.at[axis], every, number)
            copy.start()
            first_legs.append(copy)

    send_set(2)
    z_legs = len(first_legs)

    def hand_sets_on(axes, arrived):
        for copy in arrived:
            copy.wait_recv()
        for axis in axes:
            if lines[axis] == 4:
                for number, (came, to, rows) in enumerate(((3, 1, pl.ds(0, half)), (1, 3, pl.ds(half, half)))):
                    src = sets[axis].at[set_of(axis, came, 0), rows]
                    copy = set_copy(axis, came, to, src, rows, 2 + number)
                    copy.start()
                    second_legs.append(copy)

    lane_of = lax.broadcasted_iota(jnp.int32, (n, 128), 1)
    row = lax.broadcasted_iota(jnp.int32, (n, seg), 0)
    row_g, row_w = lax.div(row, near), lax.rem(row, near)
    owner_of = (lax.div(row_g, n_sub) * near + row_w) * n_sub + lax.rem(row_g, n_sub)
    before = lax.broadcasted_iota(jnp.int32, (seg, seg), 0) < lax.broadcasted_iota(jnp.int32, (seg, seg), 1)
    table = jnp.zeros((n, 128), jnp.int32)
    bits = (patches - 1).bit_length()
    in_word = 30 // bits
    words = [None] * -(-steps * cap // in_word)
    places = []
    for copy in lists:
        copy.wait()
    for s in range(steps):
        own = own_ref[s]
        wide = jnp.broadcast_to(own, (seg, seg))
        same = (wide == wide.T) & before
        slot = jnp.minimum(jnp.sum(same.astype(jnp.int32), axis=0, keepdims=True), cap - 1)
        own_dom, own_x = lax.div(own, n_sub), lax.rem(own, n_sub)
        own_y, own_w = lax.div(own_dom, near), lax.rem(own_dom, near)
        own_z, own_core = lax.div(own_w, CORES), lax.rem(own_w, CORES)
        line, at_line = (
            (own_y * near + own_w, own_x),
            (own_x * near + own_w, own_y),
            ((own_y * n_sub + own_x) * CORES + own_core, lax.rem(own_z + (lines[2] - my_z), lines[2])),
        )[s]
        places.append((s * n + line * lines[s] + at_line) * cap + slot)
        pair = pair_ref[s : s + 1, :]
        mine = owner_of == own
        for k in range(cap):
            word, at = divmod(s * cap + k, in_word)
            chosen = jnp.where(mine & (slot == k), pair * (1 << (bits * at)), 0)
            words[word] = chosen if words[word] is None else words[word] + chosen
    for word, value in enumerate(words):
        total = jnp.sum(value, axis=1, keepdims=True)
        for at in range(min(in_word, steps * cap - word * in_word)):
            field = (total >> (bits * at)) & ((1 << bits) - 1)
            table = jnp.where(lane_of == word * in_word + at, field, table)
    by_group = [table[near * g : near * (g + 1)] for g in range(far)]
    lane = lax.broadcasted_iota(jnp.int32, (near, 128), 1)

    def lanes_of(s, value, to):
        value = jnp.where((lane >= s * cap) & (lane < (s + 1) * cap), value, 0)
        shift = to - s * cap
        return pltpu.roll(value, shift, 1) if shift else value

    firsts = (0, lines[0] * cap, (lines[0] + lines[1]) * cap)
    along_x = [
        sum(lanes_of(0, by_group[y * n_sub + x], firsts[0] + x * cap) for x in range(lines[0])) for y in range(lines[1])
    ]
    along_y = [
        sum(lanes_of(1, by_group[y * n_sub + x], firsts[1] + y * cap) for y in range(lines[1])) for x in range(lines[0])
    ]
    for g in range(far):
        along_z = 0
        for z in range(lines[2]):
            turned = pltpu.roll(by_group[g], near - z * CORES, 0) if z else by_group[g]
            along_z = along_z + lanes_of(2, turned, firsts[2] + z * cap)
        req[g] = along_x[g // n_sub] + along_y[g % n_sub] + along_z
    def ask(t, carry):
        g = other_group(t)
        pltpu.make_async_remote_copy(
            req.at[g], passed.at[my_g], req_send.at[0], req_recv.at[0],
            device_id=device_at(g, my_w), device_id_type=MESH,
        ).start()
        return carry

    lax.fori_loop(1, far, ask, 0)
    send_set(0)
    send_set(1)
    pltpu.make_async_copy(req.at[my_g], passed.at[my_g], req_recv.at[0]).start()

    for s in range(steps):
        idx[s : s + 1, :] = places[s]
    idx_copy = pltpu.make_async_copy(idx, idx_s, small_sem.at[0])
    idx_copy.start()

    first, last = pl.ds(0, HALO), pl.ds(here - HALO, HALO)
    front, back = pl.ds(PAD - HALO, HALO), pl.ds(PAD + here, HALO)
    halos = []
    for a, (src, dst) in enumerate(((d_hbm, d0), (v_hbm, vel), (m_hbm, cm), (k_hbm, kq))):
        three = len(src.shape) == 3
        for side, (rows, place, to) in enumerate(((last, front, following), (first, back, previous))):
            copy = pltpu.make_async_remote_copy(
                src.at[:, rows] if three else src.at[rows],
                dst.at[:, place] if three else dst.at[place],
                halo_send.at[2 * a + side], halo_recv.at[2 * a + side],
                device_id=device(to), device_id_type=MESH,
            )
            copy.start()
            halos.append(copy)

    for copy in loads:
        copy.wait()

    def prepare(base, size):
        at = pl.ds(base, size)
        col = lax.broadcasted_iota(jnp.int32, (size, ncol), 1)
        kq[at, :] = jnp.where(col < ncol - 1, kq[at, :] * 0.25, 0.0)
        cm[at, :] = time_step / cm[at, :]

    def prepare_block(b, carry):
        prepare(pl.multiple_of(PAD + b * last_block, 8), last_block)
        return carry

    lax.fori_loop(0, here // last_block, prepare_block, 0)

    hand_sets_on((2,), first_legs[:z_legs])

    pltpu.make_async_copy(req, passed, req_recv.at[0]).wait()

    def hand_on(t, carry):
        w = other_member(t)
        pltpu.make_async_remote_copy(
            passed.at[:, w], asked.at[my_w], req_send.at[1], req_recv.at[1],
            device_id=device_at(my_g, w), device_id_type=MESH,
        ).start()
        return carry

    lax.fori_loop(1, near, hand_on, 0)
    pltpu.make_async_copy(passed.at[:, my_w], asked.at[my_w], req_recv.at[1]).start()
    hand_sets_on((0, 1), first_legs[z_legs:])

    for copy in halos:
        copy.wait()
    prepare(PAD - HALO, HALO)
    prepare(PAD + here, HALO)

    @pl.when(me == 0)
    def _():
        kq[front, :] = jnp.zeros((HALO, ncol), jnp.float32)

    @pl.when(me == n - 1)
    def _():
        tail = pl.ds(PAD + here - HALO, HALO)
        row = lax.broadcasted_iota(jnp.int32, (HALO, ncol), 0)
        kq[tail, :] = jnp.where(row == HALO - 1, 0.0, kq[tail, :])

    blocks = (here + 2 * HALO) // block
    assert blocks * block == here + 2 * HALO

    def weights(b, carry):
        base = pl.multiple_of(PAD - HALO + b * block, 8)
        both = kq[pl.ds(base, block), :] + kq[pl.ds(base - 1, block), :]
        w4[pl.ds(base, block), :] = 4.0 * (both + prev_col(both))
        return carry

    lax.fori_loop(0, blocks, weights, 0)

    def free_step(src, d_to, v_to, first_row, count, size):
        def part(b, carry):
            base = pl.multiple_of(first_row + b * size, 8)
            for i in range(size // 8 + 1):
                at = pl.ds(base + 8 * (i - 1), 8)
                below = pl.ds(base + 8 * (i - 1) + 1, 8)
                for c in range(3):
                    d = src[c, at, :]
                    box = d + src[c, below, :]
                    t = kq[at, :] * (box + next_col(box))
                    term[c, 8 * i : 8 * (i + 1), :] = t
                    if i:
                        t = t + term[c, 8 * i - 1 : 8 * i + 7, :]
                        force = t + prev_col(t) - w4[at, :] * d
                        v = vel[c, at, :] + cm[at, :] * force
                        v_to(base, size)[c, 8 * (i - 1) : 8 * i, :] = v
                        d_to(base, size)[c, 8 * (i - 1) : 8 * i, :] = d + time_step * v
            return carry

        lax.fori_loop(0, count, part, 0)

    def same_rows(ref):
        return lambda base, size: ref.at[:, pl.ds(base, size)]

    def own_rows(ref):
        return lambda base, size: ref.at[:, pl.ds(pl.multiple_of(base - PAD, 8), size)]

    free_step(d0, same_rows(d1), same_rows(vel), PAD - HALO, blocks, block)

    pltpu.make_async_copy(asked, asked, req_recv.at[1]).wait()
    asked_rows[...] = jnp.clip(asked[...].reshape(n, 128).T[:lists_rows], 0, patches - 1)
    to_scalar = pltpu.make_async_copy(asked_rows, asked_s, small_sem.at[1])
    to_scalar.start()
    to_scalar.wait()
    idx_copy.wait()

    for copy in second_legs:
        copy.wait_recv()

    def gather(axis, w, g, dst, at):
        copies = (die_x, die_y, die_z)[axis]
        for i in range(lines[axis] * cap):
            dst[at + i] = copies[i // cap, asked_s[firsts[axis] + i, w * far + g]]

    def line_of(axis, y, x, w):
        return (y * near + w, x * near + w, (y * n_sub + x) * CORES + lax.rem(w, CORES))[axis]

    def planes_at(axis, y, x, w):
        return (axis * n + line_of(axis, y, x, w) * lines[axis]) * cap

    def reply(axis, y, x, w, wanted):
        g = y * n_sub + x

        @pl.when(wanted & ((g != my_g) | (w != my_w)))
        def _():
            size = lines[axis] * cap
            there, here_at = planes_at(axis, y, x, w), planes_at(axis, my_y, my_x, my_w)
            gather(axis, w, g, answer, there)
            pltpu.make_async_remote_copy(
                answer.at[pl.ds(there, size)], got.at[pl.ds(here_at, size)], ans_send, ans_recv,
                device_id=device_at(g, w), device_id_type=MESH,
            ).start()

    rounds = lines[0] * CORES
    assert lines[0] == lines[1]

    def in_round(i):
        return (i >= 0) & (i < rounds)

    def reply_round(r, carry):
        for layer in range(lines[2]):
            i = r - lead * layer
            at_y = lax.rem(my_y * CORES + my_core + 3 * (i + rounds), rounds)
            at_x = lax.rem(my_x * CORES + my_core + 3 * (i + rounds), rounds)
            w_y = layer * CORES + lax.rem(at_y, CORES)
            w_x = layer * CORES + lax.rem(at_x, CORES)
            reply(0, lax.div(at_y, CORES), my_x, w_y, in_round(i))
            reply(1, my_y, lax.div(at_x, CORES), w_x, in_round(i))
        i = r - lead * my_z
        for part in range(lines[0]):
            at = lax.rem(my_g * CORES + my_core + 13 * ((i + rounds) * lines[0] + part), far * CORES)
            g = lax.div(at, CORES)
            reply(2, lax.div(g, n_sub), lax.rem(g, n_sub), my_z * CORES + lax.rem(at, CORES), in_round(i))
        return carry

    assert lead * (lines[2] - 1) <= rounds
    lax.fori_loop(0, rounds + lead * (lines[2] - 1), reply_round, 0)
    for axis in range(3):
        gather(axis, my_w, my_g, got, planes_at(axis, my_y, my_x, my_w))

    free_step(d1, same_rows(d2), same_rows(vel), PAD - HALO, blocks, block)
    free_step(d2, own_rows(od_ref), own_rows(ov_ref), PAD, here // last_block, last_block)

    wire = pl.ds(0, (3 * n - sum(lines)) * cap)
    pltpu.make_async_copy(answer.at[wire], got.at[wire], ans_recv).wait()

    for s in range(steps):
        first_patch[s] = got[idx_s[s, 0]]
    ghost_copy = pltpu.make_async_remote_copy(
        first_patch, ghost, ghost_sem.at[0], ghost_sem.at[1],
        device_id=device(previous), device_id_type=MESH,
    )
    ghost_copy.start()

    def place(j, carry):
        for s in range(steps):
            planes[s, pl.ds(j * 4, 4), :] = got[idx_s[s, j]]
        return carry

    lax.fori_loop(0, seg, place, 0, unroll=8)

    flat = {"cm": cm, "kq": kq, "w4": w4}
    deep = {"d0": d0, "d1": d1, "d2": d2}
    chunk = width * stride

    def correct(q, carry):
        base = PAD + q * chunk

        def rows(name, o):
            at = pl.ds(base + o, width, stride=stride)
            if name in flat:
                return flat[name][at, :]
            return [deep[name][c, at, :] for c in range(3)]

        nearby = [[planes[s, pl.ds(q * width * 4 + c, width, stride=4), :] for c in range(4)] for s in range(steps)]
        u, z = contact_response(nearby, rows)
        at = pl.ds(pl.multiple_of(q * width, 8), width)
        for o in range(-2, 3):
            for c in range(3):
                share_u[o + 2, c, at, :] = u[o][c]
                share_z[o + 2, c, at, :] = z[o][c]
        return carry

    lax.fori_loop(0, seg // width, correct, 0)

    ghost_copy.wait()

    def ghost_rows(name, o):
        at = pl.ds(PAD + here + o, 1)
        if name in flat:
            return flat[name][at, :]
        return [deep[name][c, at, :] for c in range(3)]

    nearby = [[ghost[s, pl.ds(c, 1), :] for c in range(4)] for s in range(steps)]
    u, z = contact_response(nearby, ghost_rows)
    for o in (-2, -1):
        for c in range(3):
            share_u[o + 2, c, pl.ds(seg, 1), :] = u[o][c]
            share_z[o + 2, c, pl.ds(seg, 1), :] = z[o][c]

    pltpu.make_async_copy(answer.at[wire], got.at[wire], ans_send).wait()
    for copy in first_legs + second_legs:
        copy.wait_send()
    pltpu.make_async_copy(req.at[pl.ds(0, far - 1)], passed.at[pl.ds(0, far - 1)], req_send.at[0]).wait()
    pltpu.make_async_copy(asked.at[pl.ds(0, near - 1)], asked.at[pl.ds(0, near - 1)], req_send.at[1]).wait()


def add_share(parts, stride, d_ref, v_ref, share_u, share_z, od_hbm, ov_hbm, d_sum, v_sum, sem):
    here = d_ref.shape[1]
    chunk = here // parts
    width = chunk // stride
    copies = []
    for q in range(parts):
        rows = pl.ds(q * chunk, chunk)
        for a, (src, share, total, dst) in enumerate(
            ((d_ref, share_u, d_sum, od_hbm), (v_ref, share_z, v_sum, ov_hbm))
        ):
            total[:, rows, :] = src[:, rows, :]
            for o in range(-2, 3):
                at = pl.ds(q * chunk + (o + stride if o < 0 else o), width, stride=stride)
                block = pl.ds(q * width + (1 if o < 0 else 0), width)
                for c in range(3):
                    total[c, at, :] += share[o + 2, c, block, :]
            copy = pltpu.make_async_copy(total.at[:, rows], dst.at[:, rows], sem.at[a, q])
            copy.start()
            copies.append(copy)
    for copy in copies:
        copy.wait()


def body(n_dom, n_sub, displace, velocity, nodal_mass, stiffness, die_planes, owners, pairs):
    n = n_dom * n_sub
    here, ncol = displace.shape[1:]
    steps, seg = pairs.shape
    cap = max(2, 2 * seg // n)
    ext = here + 2 * PAD
    tiles = (here + 2 * HALO) // 8
    block = 8 * max(b for b in range(1, 44) if tiles % b == 0)
    last_block = 8 * max(b for b in range(1, 33) if here // 8 % b == 0)
    width = min(32, seg)
    near = min(8, n_dom // 2)
    far = n // near
    lanes = (n_sub + far // n_sub + near // CORES) * cap
    f32, i32 = jnp.float32, jnp.int32
    any_spec = pl.BlockSpec(memory_space=pl.ANY)
    vmem_spec = pl.BlockSpec(memory_space=pltpu.VMEM)
    dma = pltpu.SemaphoreType.DMA
    share = pltpu.VMEM((5, 3, seg + 8, ncol), f32)
    results = pl.pallas_call(
        functools.partial(kernel, n_dom, n_sub, cap, near, LEAD, block, last_block, width),
        out_shape=[pltpu.VMEM(displace.shape, f32)] * 2 + [share] * 2,
        in_specs=[any_spec] * 7,
        out_specs=[vmem_spec] * 4,
        scratch_shapes=[
            pltpu.VMEM((steps, 1, seg), i32),
            pltpu.VMEM((steps, seg), i32),
            pltpu.VMEM((3, ext, ncol), f32),
            pltpu.VMEM((3, ext, ncol), f32),
            pltpu.VMEM((3, ext, ncol), f32),
            pltpu.VMEM((3, ext, ncol), f32),
            pltpu.VMEM((ext, ncol), f32),
            pltpu.VMEM((ext, ncol), f32),
            pltpu.VMEM((ext, ncol), f32),
            pltpu.VMEM((n_sub,) + die_planes.shape[1:], f32),
            pltpu.VMEM((far // n_sub,) + die_planes.shape[1:], f32),
            pltpu.VMEM((near // CORES,) + die_planes.shape[1:], f32),
            pltpu.VMEM((far, near, 128), i32),
            pltpu.VMEM((far, near, 128), i32),
            pltpu.VMEM((near, far, 128), i32),
            pltpu.VMEM((-(-lanes // 8) * 8, n), i32),
            pltpu.SMEM((-(-lanes // 8) * 8, n), i32),
            pltpu.VMEM((8, seg), i32),
            pltpu.SMEM((8, seg), i32),
            pltpu.VMEM((n * steps * cap, 4, ncol), f32),
            pltpu.VMEM((n * steps * cap, 4, ncol), f32),
            pltpu.VMEM((steps, seg * 4 + 32, ncol), f32),
            pltpu.VMEM((steps, 4, ncol), f32),
            pltpu.VMEM((steps, 4, ncol), f32),
            pltpu.VMEM((3, max(block, last_block) + 8, ncol), f32),
            dma((9,)), dma((8,)), dma((8,)), dma((3, 4)), dma((3, 4)), dma((2,)), dma((2,)), dma, dma, dma((2,)), dma((2,)),
        ],
        compiler_params=pltpu.CompilerParams(
            collective_id=0, has_side_effects=True, vmem_limit_bytes=40 * 1024 * 1024
        ),
        name="stamp",
    )(*[
        pltpu.with_memory_space_constraint(x, pltpu.HBM)
        for x in (jnp.swapaxes(owners, 1, 2), pairs, displace, velocity, nodal_mass, stiffness, die_planes)
    ])
    parts = 8 if seg >= 64 else 2
    return pl.pallas_call(
        functools.partial(add_share, parts, here // seg),
        out_shape=[jax.ShapeDtypeStruct(displace.shape, f32)] * 2,
        in_specs=[vmem_spec] * 4,
        out_specs=[any_spec] * 2,
        scratch_shapes=[pltpu.VMEM(displace.shape, f32), pltpu.VMEM(displace.shape, f32), dma((2, parts))],
        compiler_params=pltpu.CompilerParams(vmem_limit_bytes=40 * 1024 * 1024),
        name="add_share",
    )(*[pltpu.with_memory_space_constraint(x, pltpu.VMEM) for x in results])


def solution(mesh):
    in_specs = (
        P(None, ("dom", "sub"), None),
        P(None, ("dom", "sub"), None),
        P(("dom", "sub"), None),
        P(("dom", "sub"), None),
        P(None, ("dom", "sub"), None, None),
        P(None, ("dom", "sub"), None),
        P(None, ("dom", "sub")),
    )
    out_specs = (P(None, ("dom", "sub"), None), P(None, ("dom", "sub"), None))
    run = functools.partial(body, mesh.shape["dom"], mesh.shape["sub"])
    return jax.shard_map(run, mesh=mesh, in_specs=in_specs, out_specs=out_specs, check_vma=False)
```
